32 devices in a mesh: seq: 16 (over z, y, x), fsdp: 2 (over core).
Axes of the slice: x: 2, y: 2, z: 4, core: 2. Of those that a mesh axis runs over, the one named last changes fastest.
Arguments:
- tokens: bfloat16 [2, 2048, 640], P('fsdp', 'seq'), may hold values from -6 to 6
- segments: int32 [2, 2048], P('fsdp', 'seq'), may hold values from 0 to 2, as said below
- positions: int32 [2, 2048], P('fsdp', 'seq'), may hold values from 0 to 2047, as said below
- w_query: bfloat16 [640, 1024], P('fsdp'), may hold values from -0.25 to 0.25
- w_key: bfloat16 [640, 256], P('fsdp'), may hold values from -0.25 to 0.25
- w_value: bfloat16 [640, 256], P('fsdp'), may hold values from -0.25 to 0.25
- w_out: bfloat16 [1024, 640], P('fsdp'), may hold values from -0.1875 to 0.1875
- w_gate: bfloat16 [640, 2048], P('fsdp'), may hold values from -0.25 to 0.25
- w_up: bfloat16 [640, 2048], P('fsdp'), may hold values from -0.25 to 0.25
- w_down: bfloat16 [2048, 640], P('fsdp'), may hold values from -0.125 to 0.125
- norm_gains: bfloat16 [3072], P('fsdp'), may hold values from 0.25 to 1.75
- cotangent: bfloat16 [2, 2048, 640], P('fsdp', 'seq'), may hold values from -6 to 6
Outputs:
- mixed: bfloat16 [2, 2048, 640], P('fsdp', 'seq')
- input_grad: float32 [2, 2048, 640], P('fsdp', 'seq')
- grad_query: float32 [655360], P(('seq', 'fsdp'))
- grad_key: float32 [163840], P(('seq', 'fsdp'))
- grad_value: float32 [163840], P(('seq', 'fsdp'))
- grad_out: float32 [655360], P(('seq', 'fsdp'))
- grad_gate: float32 [1310720], P(('seq', 'fsdp'))
- grad_up: float32 [1310720], P(('seq', 'fsdp'))
- grad_down: float32 [1310720], P(('seq', 'fsdp'))
- grad_gains: float32 [3072], P(('seq', 'fsdp'))
The draws below stay inside these ranges and needn't reach their ends.
Inputs may be any that keep to these rules, and one draw needn't show every extreme that they name: `segments`: segment ids never fall along a row. Segment 0 starts each row and ends within its first 128 tokens; segment 2 fills the last 1 to 127 tokens; segment 1 lies between. Within a segment positions rise by one from token to token; each row starts at position 0 and ends at position 2047.
All inputs are finite; a program needn't handle non-finite values.
Results may differ from the reference program's by a relative error of at most 0.017.
Values may be sent and summed in bfloat16 or wider, within the bound.
No kernel may reach another device: no remote copies, remote signals or barrier semaphores. Data moves between devices by JAX's collectives and lax.ppermute only.
A program may use at most 128 MiB of HBM per device.

```python
import math
import jax
import jax.numpy as jnp
from jax import lax

D = 640
HEADS = 4
HEAD = 256
FF = 2048
WINDOW = 512
TOK_DEV = 128
ROWS = 2
LEN = 2048
GAINS = 3072


def cut_points(key):
    first = jax.random.randint(jax.random.fold_in(key, 11), (ROWS,), 1, TOK_DEV)
    last = LEN - jax.random.randint(jax.random.fold_in(key, 12), (ROWS,), 1, TOK_DEV)
    return (first.astype(jnp.int32), last.astype(jnp.int32))


def draw_segments(key, part):
    first, last = cut_points(key)
    place = jnp.arange(LEN, dtype=jnp.int32)[None, :]
    return (place >= first[:, None]).astype(jnp.int32) + (place >= last[:, None]).astype(jnp.int32)


def draw_positions(key, part):
    first, last = cut_points(key)
    key = jax.random.fold_in(key, 5)
    offset = jax.random.randint(key, (ROWS,), 0, first + 1).astype(jnp.int32)
    place = jnp.arange(LEN, dtype=jnp.int32)[None, :]
    middle = place - first[:, None] + offset[:, None]
    return jnp.where(place < first[:, None], place, jnp.where(place < last[:, None], middle, place)).astype(jnp.int32)


def steps_of(stream_key, extent, cuts, smallest, largest):
    factor_of = 1.0
    for position, parts in cuts:
        steps = jax.random.uniform(jax.random.fold_in(jax.random.fold_in(stream_key, 6), position), (parts,), jnp.float32, smallest / len(cuts), largest / len(cuts))
        factor_of = factor_of * jnp.repeat(jnp.exp(steps), extent[position] // parts).reshape((-1,) + (1,) * (len(extent) - 1 - position))
    return factor_of


def noise(rng, dims, width, most, pieces=(), held_as=jnp.bfloat16):
    factor_of = steps_of(rng, dims, pieces, -0.22, 0.18) if pieces else 1.0
    drawn = jax.random.normal(rng, dims, jnp.float32) * width * factor_of
    return jnp.minimum(jnp.maximum(drawn, -most), most).astype(held_as)


def setup_inputs(seed: int = 0) -> dict:
    splits = jax.random.split(jax.random.key(seed), 13)
    return {
        "tokens": noise(splits[0], (ROWS, LEN, D), 1.0, 6.0, ((0, 2), (1, 16))),
        "segments": draw_segments(jax.random.fold_in(splits[12], 71), 0),
        "positions": draw_positions(jax.random.fold_in(splits[12], 71), 0),
        "w_query": noise(splits[3], (D, HEADS * HEAD), D ** -0.5, 0.25, ((0, 2),)),
        "w_key": noise(splits[4], (D, HEAD), D ** -0.5, 0.25, ((0, 2),)),
        "w_value": noise(splits[5], (D, HEAD), D ** -0.5, 0.25, ((0, 2),)),
        "w_out": noise(splits[6], (HEADS * HEAD, D), (HEADS * HEAD) ** -0.5, 0.1875, ((0, 2),)),
        "w_gate": noise(splits[7], (D, FF), D ** -0.5, 0.25, ((0, 2),)),
        "w_up": noise(splits[8], (D, FF), D ** -0.5, 0.25, ((0, 2),)),
        "w_down": noise(splits[9], (FF, D), FF ** -0.5, 0.125, ((0, 2),)),
        "norm_gains": jnp.clip(1.0 + 0.15 * jax.random.normal(splits[10], (GAINS,), jnp.float32), 0.25, 1.75).astype(jnp.bfloat16),
        "cotangent": noise(splits[11], (ROWS, LEN, D), 1.0, 6.0, ((0, 2), (1, 16))),
    }


EPS = 1e-06

@jax.custom_vjp
def low(v):
    return lax.optimization_barrier(v.astype(jnp.bfloat16)).astype(jnp.float32)

@jax.custom_vjp
def low_back(v):
    return v

def low_keep(v):
    return (low(v), None)

def low_pass(kept, grad):
    return (grad,)

def back_keep(v):
    return (v, None)

def back_low(kept, grad):
    return (low(grad),)
low.defvjp(low_keep, low_pass)
low_back.defvjp(back_keep, back_low)

def norm_rows(value, gain):
    return value * lax.rsqrt(lax.optimization_barrier(jnp.mean(value * value, axis=-1, keepdims=True)) + EPS) * gain

def rotate(value, cosine, sine):
    half = value.shape[-1] // 2
    first = value[..., :half]
    second = value[..., half:]
    return jnp.concatenate([first * cosine - second * sine, second * cosine + first * sine], axis=-1)

def angles(positions, size):
    freq = jnp.exp(jnp.arange(size // 2, dtype=jnp.float32) * (-2.0 * math.log(10000.0) / size))
    turn = positions.astype(jnp.float32)[..., None] * freq
    return (jnp.cos(turn), jnp.sin(turn))

def project(left, right):
    return jnp.einsum('rtd,de->rte', left, right, precision=lax.Precision.HIGHEST)

def reference(tokens, segments, positions, w_query, w_key, w_value, w_out, w_gate, w_up, w_down, norm_gains, cotangent):
    cosine, sine = angles(positions, HEAD)
    scale = HEAD ** (-0.5)
    block = 512 if LEN % 512 == 0 else LEN
    per_row = LEN // block
    count = ROWS * per_row
    seg_pad = jnp.pad(segments, ((0, 0), (WINDOW, 0)), constant_values=-1)

    def attend(query, key_rot, value):
        key_pad = jnp.pad(key_rot, ((0, 0), (WINDOW, 0), (0, 0)))
        value_pad = jnp.pad(value, ((0, 0), (WINDOW, 0), (0, 0)))

        def one_block(index):
            row = (index // per_row).astype(jnp.int32)
            start = (index % per_row * block).astype(jnp.int32)
            zero = jnp.zeros((), jnp.int32)
            query_blk = lax.dynamic_slice(query, (row, start, zero, zero), (1, block, HEADS, HEAD))[0]
            key_blk = lax.dynamic_slice(key_pad, (row, start, zero), (1, block + WINDOW, HEAD))[0]
            value_blk = lax.dynamic_slice(value_pad, (row, start, zero), (1, block + WINDOW, HEAD))[0]
            seg_query = lax.dynamic_slice(segments, (row, start), (1, block))[0]
            seg_key = lax.dynamic_slice(seg_pad, (row, start), (1, block + WINDOW))[0]
            query_index = start + jnp.arange(block, dtype=jnp.int32)
            key_index = start - WINDOW + jnp.arange(block + WINDOW, dtype=jnp.int32)
            gap = query_index[:, None] - key_index[None, :]
            allowed = (seg_query[:, None] == seg_key[None, :]) & (gap >= 0) & (gap < WINDOW)
            scores = low_back(jnp.einsum('qhd,kd->hqk', query_blk, key_blk, precision=lax.Precision.HIGHEST))
            masked = jnp.where(allowed[None], scores, -1e+30)
            top = lax.optimization_barrier(jnp.max(masked, axis=-1, keepdims=True))
            expd = jnp.exp(masked - top)
            probs = low(expd / lax.optimization_barrier(jnp.sum(expd, axis=-1, keepdims=True)))
            mixed_blk = jnp.einsum('hqk,kd->qhd', probs, value_blk, precision=lax.Precision.HIGHEST)
            return mixed_blk.reshape(block, HEADS * HEAD)
        result = lax.map(jax.checkpoint(one_block), jnp.arange(count, dtype=jnp.int32))
        return result.reshape(ROWS, LEN, HEADS * HEAD)

    def forward(hidden, wq_f, wk_f, wv_f, wo_f, wg_f, wu_f, wd_f, gains):
        gain_in = gains[:D]
        gain_q = gains[D:D + HEAD]
        gain_k = gains[D + HEAD:D + 2 * HEAD]
        gain_pa = gains[D + 2 * HEAD:2 * D + 2 * HEAD]
        gain_pf = gains[2 * D + 2 * HEAD:3 * D + 2 * HEAD]
        gain_pff = gains[3 * D + 2 * HEAD:]
        normed = low(norm_rows(hidden, gain_in))
        query = low_back(project(normed, wq_f)).reshape(ROWS, LEN, HEADS, HEAD)
        key_raw = low_back(project(normed, wk_f))
        value = low(low_back(project(normed, wv_f)))
        query = low(rotate(norm_rows(query, gain_q), cosine[:, :, None, :], sine[:, :, None, :]) * scale)
        key_rot = low(rotate(norm_rows(key_raw, gain_k), cosine, sine))
        heads = low(low_back(attend(query, key_rot, value)))
        branch = low_back(project(heads, wo_f))
        after = hidden + norm_rows(branch, gain_pa)
        normed_ff = low(norm_rows(after, gain_pf))
        gate = low_back(project(normed_ff, wg_f))
        up = low_back(project(normed_ff, wu_f))
        inner = low(jax.nn.gelu(gate, approximate=True) * up)
        down = low_back(project(inner, wd_f))
        return after + norm_rows(down, gain_pff)
    floats = [a.astype(jnp.float32) for a in (tokens, w_query, w_key, w_value, w_out, w_gate, w_up, w_down, norm_gains)]
    result, pullback = jax.vjp(forward, *floats)
    grads = pullback(cotangent.astype(jnp.float32))
    return (result.astype(jnp.bfloat16), grads[0], grads[1].reshape(-1), grads[2].reshape(-1), grads[3].reshape(-1), grads[4].reshape(-1), grads[5].reshape(-1), grads[6].reshape(-1), grads[7].reshape(-1), grads[8])
```

```python
import functools
import math

import jax
import jax.numpy as jnp
import numpy as np
from jax import lax
from jax.experimental import pallas as pl
from jax.experimental.pallas import tpu as pltpu
from jax.sharding import PartitionSpec as P

WINDOW = 512
EPS = 1e-06
LANES = 128
F32 = jnp.float32
BF16 = jnp.bfloat16
MIB = 1 << 20


def shifted(x, axis, by):
    peers = lax.axis_size(axis)
    pairs = [(i, i + by) for i in range(peers) if 0 <= i + by < peers]
    return lax.ppermute(x, axis, pairs)


def norm_rows(value, gain):
    return value * lax.rsqrt(jnp.mean(value * value, axis=-1, keepdims=True) + EPS) * gain


def rotate(value, cosine, sine):
    half = value.shape[-1] // 2
    first = value[..., :half]
    second = value[..., half:]
    return jnp.concatenate(
        [first * cosine - second * sine, second * cosine + first * sine], axis=-1
    )


def angles(positions, size):
    freq = jnp.exp(jnp.arange(size // 2, dtype=jnp.float32) * (-2.0 * math.log(10000.0) / size))
    turn = positions.astype(jnp.float32)[..., None] * freq
    return (jnp.cos(turn), jnp.sin(turn))


def product(form, left, right):
    return jnp.einsum(form, left, right, preferred_element_type=jnp.float32)


def general(
    tokens,
    segments,
    positions,
    w_query,
    w_key,
    w_value,
    w_out,
    w_gate,
    w_up,
    w_down,
    norm_gains,
    cotangent,
):
    tok_rows = tokens.shape[1]
    width = tokens.shape[2]
    head_size = w_key.shape[1]
    head_count = w_query.shape[1] // head_size
    reach = (WINDOW - 1 + tok_rows - 1) // tok_rows
    scale = head_size ** (-0.5)
    gathered = tuple(
        lax.all_gather(w, "fsdp", axis=0, tiled=True)
        for w in (w_query, w_key, w_value, w_out, w_gate, w_up, w_down, norm_gains)
    )
    query_full, key_full, value_full, out_full, gate_full, up_full, down_full, gains_full = gathered
    gains = gains_full.astype(jnp.float32)
    gain_in = gains[:width]
    gain_q = gains[width : width + head_size]
    gain_k = gains[width + head_size : width + 2 * head_size]
    gain_pa = gains[width + 2 * head_size : 2 * width + 2 * head_size]
    gain_pf = gains[2 * width + 2 * head_size : 3 * width + 2 * head_size]
    gain_pff = gains[3 * width + 2 * head_size :]
    hidden_in = tokens[0].astype(jnp.float32)
    segment = segments[0]
    cosine, sine = angles(positions[0], head_size)
    normed, first_back = jax.vjp(norm_rows, hidden_in, gain_in)
    normed_low = normed.astype(jnp.bfloat16)
    query_raw = jnp.dot(normed_low, query_full, preferred_element_type=jnp.float32)
    key_raw = jnp.dot(normed_low, key_full, preferred_element_type=jnp.float32)
    value_low = jnp.dot(normed_low, value_full, preferred_element_type=jnp.float32).astype(
        jnp.bfloat16
    )

    def turn(query, key, gain_query, gain_key):
        query = norm_rows(query.reshape(tok_rows, head_count, head_size), gain_query)
        query = rotate(query, cosine[:, None, :], sine[:, None, :]) * scale
        key = rotate(norm_rows(key, gain_key), cosine, sine)
        return (query, key)

    (query_rot, key_rot), turn_back = jax.vjp(turn, query_raw, key_raw, gain_q, gain_k)
    query_low = query_rot.astype(jnp.bfloat16)
    packed = jnp.concatenate([key_rot.astype(jnp.bfloat16), value_low], axis=1)
    pieces = [packed]
    seg_pieces = [segment]
    for distance in range(1, reach + 1):
        far_pack, far_seg = shifted((packed, segment), "seq", distance)
        pieces.insert(0, far_pack)
        seg_pieces.insert(0, far_seg)
    keys_all = jnp.concatenate(pieces, axis=0)
    seg_all = jnp.concatenate(seg_pieces, axis=0)
    key_part = keys_all[:, :head_size]
    value_part = keys_all[:, head_size:]
    place = lax.axis_index("seq")
    query_index = place * tok_rows + jnp.arange(tok_rows, dtype=jnp.int32)
    key_index = (place - reach) * tok_rows + jnp.arange((reach + 1) * tok_rows, dtype=jnp.int32)
    spacing = query_index[:, None] - key_index[None, :]
    allowed = (
        (segment[:, None] == seg_all[None, :])
        & (spacing >= 0)
        & (spacing < WINDOW)
        & (key_index[None, :] >= 0)
    )
    scores = product("qhd,kd->hqk", query_low, key_part)
    masked = jnp.where(allowed[None], scores, -1e30)
    top = jnp.max(masked, axis=-1, keepdims=True)
    expd = jnp.exp(masked - top)
    total = jnp.sum(expd, axis=-1, keepdims=True)
    probs_low = (expd / total).astype(jnp.bfloat16)
    log_total = top + jnp.log(total)
    mixed_heads = (
        product("hqk,kd->qhd", probs_low, value_part)
        .reshape(tok_rows, head_count * head_size)
        .astype(jnp.bfloat16)
    )
    attn_out = jnp.dot(mixed_heads, out_full, preferred_element_type=jnp.float32)

    def middle(resid, branch, gain_a, gain_b):
        after = resid + norm_rows(branch, gain_a)
        return (after, norm_rows(after, gain_b))

    (after, normed_ff), middle_back = jax.vjp(middle, hidden_in, attn_out, gain_pa, gain_pf)
    ff_low = normed_ff.astype(jnp.bfloat16)
    gate = jnp.dot(ff_low, gate_full, preferred_element_type=jnp.float32)
    up_value = jnp.dot(ff_low, up_full, preferred_element_type=jnp.float32)

    def mixer(gate_in, up_in):
        return jax.nn.gelu(gate_in, approximate=True) * up_in

    inner, mixer_back = jax.vjp(mixer, gate, up_value)
    inner_low = inner.astype(jnp.bfloat16)
    down = jnp.dot(inner_low, down_full, preferred_element_type=jnp.float32)

    def finish(resid, branch, gain):
        return resid + norm_rows(branch, gain)

    result, finish_back = jax.vjp(finish, after, down, gain_pff)
    grad_result = cotangent[0].astype(jnp.float32)
    grad_after, grad_down, grad_gpff = finish_back(grad_result)
    down_grad_low = grad_down.astype(jnp.bfloat16)
    grad_w_down = product("tf,td->fd", inner_low, down_grad_low)
    grad_inner = product("td,fd->tf", down_grad_low, down_full)
    grad_gate, grad_upv = mixer_back(grad_inner)
    gate_grad_low = grad_gate.astype(jnp.bfloat16)
    up_grad_low = grad_upv.astype(jnp.bfloat16)
    grad_w_gate = product("td,tf->df", ff_low, gate_grad_low)
    grad_w_up = product("td,tf->df", ff_low, up_grad_low)
    grad_normed_ff = product("tf,df->td", gate_grad_low, gate_full) + product(
        "tf,df->td", up_grad_low, up_full
    )
    grad_resid, grad_branch, grad_gpa, grad_gpf = middle_back((grad_after, grad_normed_ff))
    branch_grad_low = grad_branch.astype(jnp.bfloat16)
    grad_w_out = product("ta,td->ad", mixed_heads, branch_grad_low)
    grad_heads = (
        product("td,ad->ta", branch_grad_low, out_full)
        .astype(jnp.bfloat16)
        .reshape(tok_rows, head_count, head_size)
    )
    scores_again = product("qhd,kd->hqk", query_low, key_part)
    probs = jnp.exp(jnp.where(allowed[None], scores_again, -1e30) - log_total)
    probs_again = probs.astype(jnp.bfloat16)
    grad_probs = product("qhd,kd->hqk", grad_heads, value_part)
    grad_scores = (
        probs * (grad_probs - jnp.sum(probs * grad_probs, axis=-1, keepdims=True))
    ).astype(jnp.bfloat16)
    grad_query_rot = product("hqk,kd->qhd", grad_scores, key_part)
    grad_keys = product("hqk,qhd->kd", grad_scores, query_low)
    grad_values = product("hqk,qhd->kd", probs_again, grad_heads)
    grad_packed = jnp.concatenate([grad_keys, grad_values], axis=1)
    collected = grad_packed[reach * tok_rows :]
    for distance in range(1, reach + 1):
        begin = (reach - distance) * tok_rows
        collected = collected + shifted(
            grad_packed[begin : begin + tok_rows].astype(jnp.bfloat16), "seq", -distance
        ).astype(jnp.float32)
    grad_key_rot = collected[:, :head_size]
    value_grad_low = collected[:, head_size:].astype(jnp.bfloat16)
    grad_q_raw, grad_k_raw, grad_gq, grad_gk = turn_back((grad_query_rot, grad_key_rot))
    query_grad_low = grad_q_raw.astype(jnp.bfloat16)
    key_grad_low = grad_k_raw.astype(jnp.bfloat16)
    grad_w_query = product("td,te->de", normed_low, query_grad_low)
    grad_w_key = product("td,te->de", normed_low, key_grad_low)
    grad_w_value = product("td,te->de", normed_low, value_grad_low)
    grad_normed = (
        product("te,de->td", query_grad_low, query_full)
        + product("te,de->td", key_grad_low, key_full)
        + product("te,de->td", value_grad_low, value_full)
    )
    grad_in, grad_gin = first_back(grad_normed)
    input_grad = (grad_resid + grad_in)[None]
    grad_gains = jnp.concatenate([grad_gin, grad_gq, grad_gk, grad_gpa, grad_gpf, grad_gpff])
    own = tuple(
        lax.psum_scatter(g.reshape(-1), ("seq", "fsdp"), scatter_dimension=0, tiled=True)
        for g in (
            grad_w_query,
            grad_w_key,
            grad_w_value,
            grad_w_out,
            grad_w_gate,
            grad_w_up,
            grad_w_down,
            grad_gains,
        )
    )
    return (result.astype(jnp.bfloat16)[None], input_grad) + own


XY = 4
LINE = 4


def vmem(count):
    return [pl.BlockSpec(memory_space=pltpu.VMEM)] * count


def anywhere(count):
    return [pl.BlockSpec(memory_space=pl.ANY)] * count


def mm(a, b):
    return lax.dot_general(a, b, (((1,), (0,)), ((), ())), preferred_element_type=F32)


def mm_nt(a, b):
    return lax.dot_general(a, b, (((1,), (1,)), ((), ())), preferred_element_type=F32)


def mm_tn(a, b):
    return lax.dot_general(a, b, (((0,), (0,)), ((), ())), preferred_element_type=F32)


def inverse_rms(x):
    return lax.rsqrt(jnp.mean(x * x, axis=-1, keepdims=True) + EPS)


def norm_back(hat, inv, gain, grad):
    scaled = grad * gain
    return inv * (scaled - hat * jnp.mean(hat * scaled, axis=-1, keepdims=True))


def turn_fwd(x, cosine, sine):
    half = x.shape[1] // 2
    a, b = x[:, :half], x[:, half:]
    return jnp.concatenate([a * cosine - b * sine, b * cosine + a * sine], axis=1)


def turn_bwd(x, cosine, sine):
    half = x.shape[1] // 2
    a, b = x[:, :half], x[:, half:]
    return jnp.concatenate([a * cosine + b * sine, b * cosine - a * sine], axis=1)


def assemble(core, pairs, sems):
    copies = []
    for n, (mine, theirs, full) in enumerate(pairs):
        rows = mine.shape[0]
        for side, (part, at) in enumerate(((mine, core), (theirs, 1 - core))):
            begin = pl.multiple_of(at * rows, 16)
            copy = pltpu.make_async_copy(part, full.at[pl.ds(begin, rows)], sems.at[n, side])
            copy.start()
            copies.append(copy)
    return copies


def attention_kernel(
    reach,
    meta,
    *refs,
):
    halo = refs[: reach + 1]
    (
        gains,
        cos_ref,
        sin_ref,
        wq_a,
        wq_b,
        wk_a,
        wk_b,
        wv_a,
        wv_b,
        n1_out,
        qraw_out,
        q_out,
        kraw_out,
        k_out,
        v_out,
        p_out,
        ao_out,
        wq,
        wk,
        wv,
        sems,
    ) = refs[reach + 1 :]
    rows = halo[0].shape[0]
    width = n1_out.shape[1]
    size = k_out.shape[1]
    heads = q_out.shape[1] // size
    scale = size ** (-0.5)
    place, core = meta[0], meta[1]
    copies = assemble(core, ((wk_a, wk_b, wk), (wv_a, wv_b, wv), (wq_a, wq_b, wq)), sems)
    g_in = gains[:, :width]
    g_q = gains[:, width : width + size]
    g_k = gains[:, width + size : width + 2 * size]
    for block in range(reach + 1):
        x = halo[block][:, :width].astype(F32)
        n1_out[block * rows : (block + 1) * rows, :] = (x * inverse_rms(x) * g_in).astype(BF16)
    for copy in copies[:4]:
        copy.wait()
    n1 = n1_out[...]
    kraw = mm(n1, wk[...])
    kraw_out[...] = kraw
    k = turn_fwd(kraw * inverse_rms(kraw) * g_k, cos_ref[...], sin_ref[...]).astype(BF16)
    k_out[...] = k
    v = mm(n1, wv[...]).astype(BF16)
    v_out[...] = v
    for copy in copies[4:]:
        copy.wait()
    keys = (reach + 1) * rows
    lane = lax.broadcasted_iota(jnp.int32, (rows, LANES), 1)
    pick = jnp.where(lane == 0, 1.0, 0.0).astype(BF16)
    seg_keys = jnp.concatenate([mm_nt(pick, halo[b][:, width:]) for b in range(reach + 1)], axis=1)
    seg_own = halo[reach][:, width : width + 1].astype(F32)
    at_query = reach * rows + lax.broadcasted_iota(jnp.int32, (rows, keys), 0)
    at_key = lax.broadcasted_iota(jnp.int32, (rows, keys), 1)
    gap = at_query - at_key
    allowed = (
        (seg_keys == seg_own)
        & (gap >= 0)
        & (gap < WINDOW)
        & (at_key >= (reach - place) * rows)
    )
    cos_own, sin_own = cos_ref[reach * rows :, :], sin_ref[reach * rows :, :]
    for h in range(heads):
        cols = slice(h * size, (h + 1) * size)
        qraw = mm(n1_out[reach * rows :, :], wq[:, cols])
        qraw_out[:, cols] = qraw
        q = turn_fwd(qraw * inverse_rms(qraw) * g_q, cos_own, sin_own) * scale
        q = q.astype(BF16)
        q_out[:, cols] = q
        s = jnp.where(allowed, mm_nt(q, k), -1e30)
        e = jnp.exp(s - jnp.max(s, axis=-1, keepdims=True))
        p = e / jnp.sum(e, axis=-1, keepdims=True)
        p_out[h] = p
        ao_out[:, cols] = mm(p.astype(BF16), v).astype(BF16)


def pick_half(core, unit, width):
    row = lax.broadcasted_iota(jnp.int32, (LANES, width), 0)
    col = lax.broadcasted_iota(jnp.int32, (LANES, width), 1)
    want = (lax.div(row, unit) * 2 + core) * unit + lax.rem(row, unit)
    return jnp.where(col == want, 1.0, 0.0).astype(BF16)


def store_lanes(ref, base, value):
    rows = value.shape[0]
    for b in range(value.shape[1] // LANES):
        ref[base + b * rows : base + (b + 1) * rows, :] = value[:, b * LANES : (b + 1) * LANES]
    return base + rows * (value.shape[1] // LANES)


def feed_kernel(
    meta,
    tok,
    ct,
    gains,
    order,
    ao_ref,
    wo_a,
    wo_b,
    wg_a,
    wg_b,
    wu_a,
    wu_b,
    wd_a,
    wd_b,
    mixed_out,
    dx_out,
    dao_out,
    dg_out,
    keep,
    send,
    wo,
    wg,
    wu,
    wd,
    gate_s,
    up_s,
    hid_s,
    dg_s,
    du_s,
    sems,
):
    core = meta[1]
    rows, width = ct.shape
    size2 = gains.shape[1] - 4 * width
    ff = wg.shape[1]
    copies = assemble(
        core, ((wo_a, wo_b, wo), (wg_a, wg_b, wg), (wu_a, wu_b, wu), (wd_a, wd_b, wd)), sems
    )
    base = width + size2
    g_pa = gains[:, base : base + width]
    g_pf = gains[:, base + width : base + 2 * width]
    g_pff = gains[:, base + 2 * width :]
    x = tok[:, :width].astype(F32)
    c = ct[...].astype(F32)
    for copy in copies[:2]:
        copy.wait()
    ya = mm(ao_ref[...], wo[...])
    inv_a = inverse_rms(ya)
    hat_a = ya * inv_a
    x2 = x + hat_a * g_pa
    inv_f = inverse_rms(x2)
    hat_f = x2 * inv_f
    n2 = (hat_f * g_pf).astype(BF16)
    for copy in copies[2:]:
        copy.wait()
    part = 512
    root = math.sqrt(2.0 / math.pi)
    f = jnp.zeros((rows, width), F32)
    for at in range(0, ff, part):
        cols = slice(at, at + part)
        gate = mm(n2, wg[:, cols])
        up = mm(n2, wu[:, cols])
        gate_s[:, cols] = gate
        up_s[:, cols] = up
        t = jnp.tanh(root * (gate + 0.044715 * (gate * gate * gate)))
        hid = (0.5 * gate * (1.0 + t) * up).astype(BF16)
        hid_s[:, cols] = hid
        f = f + mm(hid, wd[cols, :])
    inv_d = inverse_rms(f)
    hat_d = f * inv_d
    mixed_out[...] = (x2 + hat_d * g_pff).astype(BF16)
    df = norm_back(hat_d, inv_d, g_pff, c).astype(BF16)
    dn2 = jnp.zeros((rows, width), F32)
    for at in range(0, ff, part):
        cols = slice(at, at + part)
        dhid = mm_nt(df, wd[cols, :])
        gate = gate_s[:, cols]
        up = up_s[:, cols]
        t = jnp.tanh(root * (gate + 0.044715 * (gate * gate * gate)))
        act = 0.5 * gate * (1.0 + t)
        slope = 0.5 * (1.0 + t) + 0.5 * gate * (1.0 - t * t) * (
            root * (1.0 + 3.0 * 0.044715 * (gate * gate))
        )
        dgate = (dhid * up * slope).astype(BF16)
        dup = (dhid * act).astype(BF16)
        dg_s[:, cols] = dgate
        du_s[:, cols] = dup
        dn2 = dn2 + mm_nt(dgate, wg[:, cols]) + mm_nt(dup, wu[:, cols])
    dx2 = c + norm_back(hat_f, inv_f, g_pf, dn2)
    dx_out[...] = dx2
    dya = norm_back(hat_a, inv_a, g_pa, dx2).astype(BF16)
    dao_out[...] = mm_nt(dya, wo[...]).astype(BF16)
    dg_out[:, :width] = jnp.sum(dx2 * hat_a, axis=0, keepdims=True)
    dg_out[:, width : 2 * width] = jnp.sum(dn2 * hat_f, axis=0, keepdims=True)
    dg_out[:, 2 * width :] = jnp.sum(c * hat_d, axis=0, keepdims=True)
    ranks = lax.broadcasted_iota(jnp.int32, (width, width), 1)
    perm = jnp.where(ranks == order[...], 1.0, 0.0).astype(BF16)
    n2_t = mm_nt(perm, n2).astype(BF16)
    half = width // 2
    keep[:half, :] = n2_t[:half]
    send[:half, :] = n2_t[half:]
    at = half
    for source, unit in ((hid_s, ff // 32), (ao_ref, ao_ref.shape[1] // 32)):
        for ref, side in ((keep, core), (send, 1 - core)):
            pick = pick_half(side, unit, 2 * LANES)
            for b in range(source.shape[1] // (2 * LANES)):
                block = source[:, 2 * b * LANES : 2 * (b + 1) * LANES]
                ref[at + b * LANES : at + (b + 1) * LANES, :] = mm_nt(pick, block).astype(BF16)
        at += source.shape[1] // 2
    for ref in (keep, send):
        base = store_lanes(ref, at, dg_s[...])
        base = store_lanes(ref, base, du_s[...])
        base = store_lanes(ref, base, df)
        store_lanes(ref, base, dya)


def load_lanes(ref, base, rows, cols):
    blocks = [ref[base + b * rows : base + (b + 1) * rows, :] for b in range(cols // LANES)]
    return jnp.concatenate(blocks, axis=1), base + rows * (cols // LANES)


def put(xk, xs, first, plane, at, value):
    x_bit, y_bit = plane & 1, plane >> 1
    lead, other = (x_bit, y_bit) if first == "x" else (y_bit, x_bit)
    ref = xs if lead else xk
    ref[other, at : at + value.shape[0], :] = value


def grads_kernel(
    meta, width, ff, attn, mine, recv, gk, gs, uk, us, dk, ds, ok, os, left_s, right_s, prod_s
):
    place = meta[0]
    half = width // 2
    rows = LANES

    def both(base, count):
        left_s[:count, :rows] = mine[base : base + count, :]
        left_s[:count, rows:] = recv[base : base + count, :]
        return left_s[:count, :]

    def right(base, cols):
        for side, ref in enumerate((mine, recv)):
            for b in range(cols // LANES):
                right_s[side * rows : (side + 1) * rows, b * LANES : (b + 1) * LANES] = ref[
                    base + b * rows : base + (b + 1) * rows, :
                ]

    at_hid = half
    at_ao = at_hid + ff // 2
    at_gate = at_ao + attn // 2
    at_up = at_gate + ff
    at_df = at_up + ff
    at_dya = at_df + width
    per = half // XY
    n2 = both(0, half)
    for base, (keep, send), first in ((at_gate, (gk, gs), "x"), (at_up, (uk, us), "y")):
        right(base, ff)
        for col in range(0, ff, 512):
            out = mm(n2, right_s[:, col : col + 512]).astype(BF16)
            for plane in range(XY):
                for b in range(4):
                    put(
                        keep,
                        send,
                        first,
                        plane,
                        (col // LANES + b) * per,
                        out[plane * per : (plane + 1) * per, b * LANES : (b + 1) * LANES],
                    )
    for base, at_left, count, (keep, send), first in (
        (at_df, at_hid, ff // 2, (dk, ds), "x"),
        (at_dya, at_ao, attn // 2, (ok, os), "y"),
    ):
        left = both(at_left, count)
        right(base, width)
        prod_s[:count, :] = mm(left, right_s[:, :width])
        unit = count // (XY * LINE)
        for plane in range(XY):
            for line in range(LINE):
                whose = (place ^ (line * XY + plane)) * unit
                block = prod_s[pl.ds(pl.multiple_of(whose, unit), unit), :].astype(BF16)
                for b in range(width // LANES):
                    put(
                        keep,
                        send,
                        first,
                        plane,
                        b * unit * LINE + line * unit,
                        block[:, b * LANES : (b + 1) * LANES],
                    )


def back_kernel(
    reach,
    meta,
    *refs,
):
    halo = refs[: reach + 1]
    (
        gains,
        order,
        cos_ref,
        sin_ref,
        n1_ref,
        qraw_ref,
        q_ref,
        kraw_ref,
        k_ref,
        v_ref,
        p_ref,
        dao_ref,
        wq_a,
        wq_b,
        wk_a,
        wk_b,
        wv_a,
        wv_b,
        keep,
        send,
        dn1_own,
        dn1_far,
        dg_out,
        wq,
        wk,
        wv,
        dqr_s,
        dkv_s,
        sems,
    ) = refs[reach + 1 :]
    core = meta[1]
    rows = halo[0].shape[0]
    width = n1_ref.shape[1]
    size = k_ref.shape[1]
    heads = q_ref.shape[1] // size
    scale = size ** (-0.5)
    copies = assemble(core, ((wk_a, wk_b, wk), (wv_a, wv_b, wv), (wq_a, wq_b, wq)), sems)
    g_in = gains[:, :width]
    g_q = gains[:, width : width + size]
    g_k = gains[:, width + size : width + 2 * size]
    k = k_ref[...]
    v = v_ref[...]
    keys = (reach + 1) * rows
    cos_own, sin_own = cos_ref[reach * rows :, :], sin_ref[reach * rows :, :]
    dk = jnp.zeros((keys, size), F32)
    dv = jnp.zeros((keys, size), F32)
    dgq = jnp.zeros((1, size), F32)
    for h in range(heads):
        cols = slice(h * size, (h + 1) * size)
        p = p_ref[h]
        dao = dao_ref[:, cols]
        dp = mm_nt(dao, v)
        ds = (p * (dp - jnp.sum(p * dp, axis=-1, keepdims=True))).astype(BF16)
        dv = dv + mm_tn(p.astype(BF16), dao)
        dk = dk + mm_tn(ds, q_ref[:, cols])
        dq = turn_bwd(mm(ds, k) * scale, cos_own, sin_own)
        qraw = qraw_ref[:, cols]
        inv = inverse_rms(qraw)
        hat = qraw * inv
        dgq = dgq + jnp.sum(dq * hat, axis=0, keepdims=True)
        dqr_s[:, cols] = norm_back(hat, inv, g_q, dq).astype(BF16)
    dk = turn_bwd(dk, cos_ref[...], sin_ref[...])
    kraw = kraw_ref[...]
    inv = inverse_rms(kraw)
    hat = kraw * inv
    dg_out[:, width : width + size] = dgq
    dg_out[:, width + size :] = jnp.sum(dk * hat, axis=0, keepdims=True)
    dkv_s[:, :size] = norm_back(hat, inv, g_k, dk).astype(BF16)
    dkv_s[:, size:] = dv.astype(BF16)
    ranks = lax.broadcasted_iota(jnp.int32, (width, width), 1)
    perm = jnp.where(ranks == order[...], 1.0, 0.0).astype(BF16)
    n1_t = mm_nt(perm, n1_ref[...]).astype(BF16)
    half = width // 2
    per = half // XY
    attn = heads * size
    for ref, begin in ((send, half), (keep, 0)):
        left = n1_t[begin : begin + half]
        own = left[:, reach * rows :]
        at = 0
        for value, left_part, total in (
            (dqr_s, own, attn),
            (dkv_s, left, 2 * size),
        ):
            for col in range(0, total, 512):
                out = mm(left_part, value[:, col : col + 512]).astype(BF16)
                for plane in range(XY):
                    for b in range(4):
                        ref[
                            plane,
                            at + (col // LANES + b) * per : at + (col // LANES + b + 1) * per,
                            :,
                        ] = out[plane * per : (plane + 1) * per, b * LANES : (b + 1) * LANES]
            at += total // LANES * per
    for copy in copies:
        copy.wait()
    dgi = jnp.zeros((1, width), F32)
    for block in range(reach + 1):
        span = slice(block * rows, (block + 1) * rows)
        dn1 = mm_nt(dkv_s[span, :size], wk[...]) + mm_nt(dkv_s[span, size:], wv[...])
        if block == reach:
            dn1 = dn1 + mm_nt(dqr_s[...], wq[...])
        x = halo[block][:, :width].astype(F32)
        dgi = dgi + jnp.sum(dn1 * (x * inverse_rms(x)), axis=0, keepdims=True)
        if block == reach:
            dn1_own[...] = dn1
        else:
            dn1_far[block] = dn1.astype(BF16)
    dg_out[:, :width] = dgi


def call(kernel, meta, args, specs, outs, scratch, limit, flops):
    return pl.pallas_call(
        kernel,
        out_shape=outs,
        in_specs=[pl.BlockSpec(memory_space=pltpu.SMEM)] + specs,
        out_specs=vmem(len(outs)),
        scratch_shapes=scratch,
        compiler_params=pltpu.CompilerParams(vmem_limit_bytes=limit * MIB),
        cost_estimate=pl.CostEstimate(flops=flops, bytes_accessed=8 * MIB, transcendentals=0),
    )(meta, *args)


def shape(dims, dtype):
    return jax.ShapeDtypeStruct(dims, dtype)


def fast(
    tokens,
    segments,
    positions,
    w_query,
    w_key,
    w_value,
    w_out,
    w_gate,
    w_up,
    w_down,
    norm_gains,
    cotangent,
):
    rows, width = tokens.shape[1:]
    size = w_key.shape[1]
    attn = w_query.shape[1]
    heads = attn // size
    ff = w_gate.shape[1]
    count = norm_gains.shape[0] * 2
    reach = (WINDOW - 1 + rows - 1) // rows
    keys = (reach + 1) * rows
    place = lax.axis_index("seq")
    core = lax.axis_index("fsdp")
    meta = jnp.stack([place, core]).astype(jnp.int32)

    def partner(value):
        return lax.ppermute(value, "fsdp", [(0, 1), (1, 0)])

    def across(value, bits):
        return lax.ppermute(value, "seq", [(i, i ^ bits) for i in range(XY * LINE)])

    weights = (w_query, w_key, w_value, w_out, w_gate, w_up, w_down)
    other = [partner(w) for w in weights]
    gains_far = partner(norm_gains)
    seg_cols = jnp.broadcast_to(segments[0].astype(BF16)[:, None], (rows, LANES))
    tok = jnp.concatenate([tokens[0], seg_cols], axis=1)
    halo = [shifted(tok, "seq", distance) for distance in range(reach, 0, -1)] + [tok]

    gains = jnp.where(
        core == 0,
        jnp.concatenate([norm_gains, gains_far]),
        jnp.concatenate([gains_far, norm_gains]),
    ).astype(F32)[None]
    unit = width // (2 * XY * LINE)
    new = np.arange(width) // unit
    core_bit, plane, line = new // (XY * LINE), new // LINE % XY, new % LINE
    owner = (jnp.asarray(line * XY + plane, jnp.int32) ^ place) * 2 + (
        jnp.asarray(core_bit, jnp.int32) ^ core
    )
    order = (owner * unit + jnp.asarray(np.arange(width) % unit, jnp.int32))[:, None]
    freq = np.exp(np.arange(size // 2, dtype=np.float64) * (-2.0 * math.log(10000.0) / size))
    turn = np.arange(keys, dtype=np.float64)[:, None] * freq
    cosine = jnp.asarray(np.cos(turn).astype(np.float32))
    sine = jnp.asarray(np.sin(turn).astype(np.float32))

    n1, qraw, q, kraw, k, v, p, ao = call(
        functools.partial(attention_kernel, reach),
        meta,
        (*halo, gains, cosine, sine, w_query, other[0], w_key, other[1], w_value, other[2]),
        vmem(reach + 4) + anywhere(6),
        [
            shape((keys, width), BF16),
            shape((rows, attn), F32),
            shape((rows, attn), BF16),
            shape((keys, size), F32),
            shape((keys, size), BF16),
            shape((keys, size), BF16),
            shape((heads, rows, keys), F32),
            shape((rows, attn), BF16),
        ],
        [
            pltpu.VMEM((width, attn), BF16),
            pltpu.VMEM((width, size), BF16),
            pltpu.VMEM((width, size), BF16),
            pltpu.SemaphoreType.DMA((3, 2)),
        ],
        24,
        3 * 10**9,
    )

    pack = width // 2 + ff // 2 + attn // 2 + 2 * ff + 2 * width
    mixed, dx, dao, dg_post, mlp_keep, mlp_send = call(
        feed_kernel,
        meta,
        (
            tok,
            cotangent[0],
            gains,
            order,
            ao,
            w_out,
            other[3],
            w_gate,
            other[4],
            w_up,
            other[5],
            w_down,
            other[6],
        ),
        vmem(5) + anywhere(8),
        [
            shape((rows, width), BF16),
            shape((rows, width), F32),
            shape((rows, attn), BF16),
            shape((1, 3 * width), F32),
            shape((pack, LANES), BF16),
            shape((pack, LANES), BF16),
        ],
        [
            pltpu.VMEM((attn, width), BF16),
            pltpu.VMEM((width, ff), BF16),
            pltpu.VMEM((width, ff), BF16),
            pltpu.VMEM((ff, width), BF16),
            pltpu.VMEM((rows, ff), F32),
            pltpu.VMEM((rows, ff), F32),
            pltpu.VMEM((rows, ff), BF16),
            pltpu.VMEM((rows, ff), BF16),
            pltpu.VMEM((rows, ff), BF16),
            pltpu.SemaphoreType.DMA((4, 2)),
        ],
        36,
        4 * 10**9,
    )
    mlp_recv = partner(mlp_send)

    per_ff = width // 2 // XY * ff // LANES
    per_down = ff // 2 // XY * width // LANES
    per_out = attn // 2 // XY * width // LANES
    halves = []
    for per in (per_ff, per_ff, per_down, per_out):
        halves += [shape((2, per, LANES), BF16)] * 2
    gk, gs, uk, us, dk, ds, ok, os = call(
        lambda meta_ref, *refs: grads_kernel(meta_ref, width, ff, attn, *refs),
        meta,
        (mlp_keep, mlp_recv),
        vmem(2),
        halves,
        [
            pltpu.VMEM((ff // 2, 2 * LANES), BF16),
            pltpu.VMEM((2 * LANES, ff), BF16),
            pltpu.VMEM((ff // 2, width), F32),
        ],
        32,
        10**9,
    )

    per_q = width // 2 // XY * attn // LANES
    per_k = width // 2 // XY * size // LANES
    per_back = per_q + 2 * per_k
    back_keep, back_send, dn1_own, dn1_far, dg_pre = call(
        functools.partial(back_kernel, reach),
        meta,
        (
            *halo,
            gains,
            order,
            cosine,
            sine,
            n1,
            qraw,
            q,
            kraw,
            k,
            v,
            p,
            dao,
            w_query,
            other[0],
            w_key,
            other[1],
            w_value,
            other[2],
        ),
        vmem(reach + 13) + anywhere(6),
        [
            shape((XY, per_back + 16, LANES), BF16),
            shape((XY, per_back + 16, LANES), BF16),
            shape((rows, width), F32),
            shape((reach, rows, width), BF16),
            shape((1, width + 2 * size), F32),
        ],
        [
            pltpu.VMEM((width, attn), BF16),
            pltpu.VMEM((width, size), BF16),
            pltpu.VMEM((width, size), BF16),
            pltpu.VMEM((rows, attn), BF16),
            pltpu.VMEM((keys, 2 * size), BF16),
            pltpu.SemaphoreType.DMA((3, 2)),
        ],
        32,
        4 * 10**9,
    )
    share = count // (2 * XY * LINE)
    dg = jnp.concatenate([dg_pre, dg_post], axis=1).reshape(2 * XY * LINE, share)
    new = np.arange(2 * XY * LINE)
    core_bit, plane, line = new // (XY * LINE), new // LINE % XY, new % LINE
    owner = (jnp.asarray(line * XY + plane, jnp.int32) ^ place) * 2 + (
        jnp.asarray(core_bit, jnp.int32) ^ core
    )
    dg = jnp.take(dg, owner, axis=0).reshape(2, XY, LINE, share).astype(BF16)
    dg = jnp.pad(dg, ((0, 0), (0, 0), (0, 16 - LINE), (0, LANES - share)))
    back_keep = lax.dynamic_update_slice(back_keep, dg[0], (0, per_back, 0))
    back_send = lax.dynamic_update_slice(back_send, dg[1], (0, per_back, 0))
    back_recv = partner(back_send)

    def add(a, b):
        return (a.astype(F32) + b.astype(F32)).astype(BF16)

    def plane_sum(keep, send, bits):
        keep = add(keep, across(send, bits))
        return add(keep[0], across(keep[1], 3 - bits))

    def line_sum(parts):
        total = parts[0].astype(F32)
        for step in range(1, LINE):
            total = total + across(parts[step], step * XY).astype(F32)
        return total

    def by_line(value, blocks):
        unit = value.shape[0] // (blocks * LINE)
        return value.reshape(blocks, LINE, unit, LANES).transpose(1, 0, 2, 3)

    def flat(total, blocks):
        unit = total.shape[0] // blocks
        return total.reshape(blocks, unit, LANES).transpose(1, 0, 2).reshape(-1)

    gate_sum = plane_sum(gk, gs, 1)
    up_sum = plane_sum(uk, us, 2)
    down_sum = plane_sum(dk, ds, 1)
    out_sum = plane_sum(ok, os, 2)
    mid = per_q // 2 + per_k
    both = add(back_keep, back_recv)
    back_x = plane_sum(both[0::2, :mid], both[1::2, :mid], 1)
    back_y = plane_sum(both[:2, mid:], both[2:, mid:], 2)
    back_sum = jnp.concatenate([back_x, back_y], axis=0)

    def joined(*pieces):
        return jnp.concatenate([by_line(v, b).reshape(LINE, -1, LANES) for v, b in pieces], axis=1)

    wide = ff // LANES
    narrow = width // LANES
    first = line_sum(joined((gate_sum, wide), (up_sum, wide)))
    second = line_sum(joined((down_sum, narrow), (out_sum, narrow)))
    scales = back_sum[per_back : per_back + LINE].reshape(LINE, 1, LANES)
    third = line_sum(
        jnp.concatenate(
            [joined((back_sum[:per_back], (attn + 2 * size) // LANES)), scales], axis=1
        )
    )
    own_gate = flat(first[: per_ff // LINE], wide)
    own_up = flat(first[per_ff // LINE :], wide)
    own_down = flat(second[: per_down // LINE], narrow)
    own_out = flat(second[per_down // LINE :], narrow)
    a, b = per_q // LINE, (per_q + per_k) // LINE
    own_query = flat(third[:a], attn // LANES)
    own_key = flat(third[a:b], size // LANES)
    own_value = flat(third[b : per_back // LINE], size // LANES)
    own_gains = third[per_back // LINE, :share]

    dn1 = dn1_own
    for index in range(reach):
        dn1 = dn1 + shifted(dn1_far[index], "seq", index - reach).astype(F32)
    x = tokens[0].astype(F32)
    inv = inverse_rms(x)
    input_grad = dx + norm_back(x * inv, inv, gains[:, :width], dn1)
    return (
        mixed[None],
        input_grad[None],
        own_query,
        own_key,
        own_value,
        own_out,
        own_gate,
        own_up,
        own_down,
        own_gains,
    )


def solution(mesh):
    placed = (
        P("fsdp", "seq", None),
        P("fsdp", "seq"),
        P("fsdp", "seq"),
        P("fsdp", None),
        P("fsdp", None),
        P("fsdp", None),
        P("fsdp", None),
        P("fsdp", None),
        P("fsdp", None),
        P("fsdp", None),
        P("fsdp"),
        P("fsdp", "seq", None),
    )
    small = mesh.shape["seq"] == XY * LINE and mesh.shape["fsdp"] == 2
    return jax.shard_map(
        fast if small else general,
        mesh=mesh,
        in_specs=placed,
        out_specs=(
            P("fsdp", "seq", None),
            P("fsdp", "seq", None),
            P(("seq", "fsdp")),
            P(("seq", "fsdp")),
            P(("seq", "fsdp")),
            P(("seq", "fsdp")),
            P(("seq", "fsdp")),
            P(("seq", "fsdp")),
            P(("seq", "fsdp")),
            P(("seq", "fsdp")),
        ),
        check_vma=False,
    )
```

```python
import functools
import math

import jax
import jax.numpy as jnp
import numpy as np
from jax import lax
from jax.experimental import pallas as pl
from jax.experimental.pallas import tpu as pltpu
from jax.sharding import PartitionSpec as P

WINDOW = 512
EPS = 1e-06
LANES = 128
SEG_ROWS = 16
F32 = jnp.float32
BF16 = jnp.bfloat16
MIB = 1 << 20


def shifted(x, axis, by):
    peers = lax.axis_size(axis)
    pairs = [(i, i + by) for i in range(peers) if 0 <= i + by < peers]
    return lax.ppermute(x, axis, pairs)


def norm_rows(value, gain):
    return value * lax.rsqrt(jnp.mean(value * value, axis=-1, keepdims=True) + EPS) * gain


def rotate(value, cosine, sine):
    half = value.shape[-1] // 2
    first = value[..., :half]
    second = value[..., half:]
    return jnp.concatenate(
        [first * cosine - second * sine, second * cosine + first * sine], axis=-1
    )


def angles(positions, size):
    freq = jnp.exp(jnp.arange(size // 2, dtype=jnp.float32) * (-2.0 * math.log(10000.0) / size))
    turn = positions.astype(jnp.float32)[..., None] * freq
    return (jnp.cos(turn), jnp.sin(turn))


def product(form, left, right):
    return jnp.einsum(form, left, right, preferred_element_type=jnp.float32)


def general(
    tokens,
    segments,
    positions,
    w_query,
    w_key,
    w_value,
    w_out,
    w_gate,
    w_up,
    w_down,
    norm_gains,
    cotangent,
):
    tok_rows = tokens.shape[1]
    width = tokens.shape[2]
    head_size = w_key.shape[1]
    head_count = w_query.shape[1] // head_size
    reach = (WINDOW - 1 + tok_rows - 1) // tok_rows
    scale = head_size ** (-0.5)
    gathered = tuple(
        lax.all_gather(w, "fsdp", axis=0, tiled=True)
        for w in (w_query, w_key, w_value, w_out, w_gate, w_up, w_down, norm_gains)
    )
    query_full, key_full, value_full, out_full, gate_full, up_full, down_full, gains_full = gathered
    gains = gains_full.astype(jnp.float32)
    gain_in = gains[:width]
    gain_q = gains[width : width + head_size]
    gain_k = gains[width + head_size : width + 2 * head_size]
    gain_pa = gains[width + 2 * head_size : 2 * width + 2 * head_size]
    gain_pf = gains[2 * width + 2 * head_size : 3 * width + 2 * head_size]
    gain_pff = gains[3 * width + 2 * head_size :]
    hidden_in = tokens[0].astype(jnp.float32)
    segment = segments[0]
    cosine, sine = angles(positions[0], head_size)
    normed, first_back = jax.vjp(norm_rows, hidden_in, gain_in)
    normed_low = normed.astype(jnp.bfloat16)
    query_raw = jnp.dot(normed_low, query_full, preferred_element_type=jnp.float32)
    key_raw = jnp.dot(normed_low, key_full, preferred_element_type=jnp.float32)
    value_low = jnp.dot(normed_low, value_full, preferred_element_type=jnp.float32).astype(
        jnp.bfloat16
    )

    def turn(query, key, gain_query, gain_key):
        query = norm_rows(query.reshape(tok_rows, head_count, head_size), gain_query)
        query = rotate(query, cosine[:, None, :], sine[:, None, :]) * scale
        key = rotate(norm_rows(key, gain_key), cosine, sine)
        return (query, key)

    (query_rot, key_rot), turn_back = jax.vjp(turn, query_raw, key_raw, gain_q, gain_k)
    query_low = query_rot.astype(jnp.bfloat16)
    packed = jnp.concatenate([key_rot.astype(jnp.bfloat16), value_low], axis=1)
    pieces = [packed]
    seg_pieces = [segment]
    for distance in range(1, reach + 1):
        far_pack, far_seg = shifted((packed, segment), "seq", distance)
        pieces.insert(0, far_pack)
        seg_pieces.insert(0, far_seg)
    keys_all = jnp.concatenate(pieces, axis=0)
    seg_all = jnp.concatenate(seg_pieces, axis=0)
    key_part = keys_all[:, :head_size]
    value_part = keys_all[:, head_size:]
    place = lax.axis_index("seq")
    query_index = place * tok_rows + jnp.arange(tok_rows, dtype=jnp.int32)
    key_index = (place - reach) * tok_rows + jnp.arange((reach + 1) * tok_rows, dtype=jnp.int32)
    spacing = query_index[:, None] - key_index[None, :]
    allowed = (
        (segment[:, None] == seg_all[None, :])
        & (spacing >= 0)
        & (spacing < WINDOW)
        & (key_index[None, :] >= 0)
    )
    scores = product("qhd,kd->hqk", query_low, key_part)
    masked = jnp.where(allowed[None], scores, -1e30)
    top = jnp.max(masked, axis=-1, keepdims=True)
    expd = jnp.exp(masked - top)
    total = jnp.sum(expd, axis=-1, keepdims=True)
    probs_low = (expd / total).astype(jnp.bfloat16)
    log_total = top + jnp.log(total)
    mixed_heads = (
        product("hqk,kd->qhd", probs_low, value_part)
        .reshape(tok_rows, head_count * head_size)
        .astype(jnp.bfloat16)
    )
    attn_out = jnp.dot(mixed_heads, out_full, preferred_element_type=jnp.float32)

    def middle(resid, branch, gain_a, gain_b):
        after = resid + norm_rows(branch, gain_a)
        return (after, norm_rows(after, gain_b))

    (after, normed_ff), middle_back = jax.vjp(middle, hidden_in, attn_out, gain_pa, gain_pf)
    ff_low = normed_ff.astype(jnp.bfloat16)
    gate = jnp.dot(ff_low, gate_full, preferred_element_type=jnp.float32)
    up_value = jnp.dot(ff_low, up_full, preferred_element_type=jnp.float32)

    def mixer(gate_in, up_in):
        return jax.nn.gelu(gate_in, approximate=True) * up_in

    inner, mixer_back = jax.vjp(mixer, gate, up_value)
    inner_low = inner.astype(jnp.bfloat16)
    down = jnp.dot(inner_low, down_full, preferred_element_type=jnp.float32)

    def finish(resid, branch, gain):
        return resid + norm_rows(branch, gain)

    result, finish_back = jax.vjp(finish, after, down, gain_pff)
    grad_result = cotangent[0].astype(jnp.float32)
    grad_after, grad_down, grad_gpff = finish_back(grad_result)
    down_grad_low = grad_down.astype(jnp.bfloat16)
    grad_w_down = product("tf,td->fd", inner_low, down_grad_low)
    grad_inner = product("td,fd->tf", down_grad_low, down_full)
    grad_gate, grad_upv = mixer_back(grad_inner)
    gate_grad_low = grad_gate.astype(jnp.bfloat16)
    up_grad_low = grad_upv.astype(jnp.bfloat16)
    grad_w_gate = product("td,tf->df", ff_low, gate_grad_low)
    grad_w_up = product("td,tf->df", ff_low, up_grad_low)
    grad_normed_ff = product("tf,df->td", gate_grad_low, gate_full) + product(
        "tf,df->td", up_grad_low, up_full
    )
    grad_resid, grad_branch, grad_gpa, grad_gpf = middle_back((grad_after, grad_normed_ff))
    branch_grad_low = grad_branch.astype(jnp.bfloat16)
    grad_w_out = product("ta,td->ad", mixed_heads, branch_grad_low)
    grad_heads = (
        product("td,ad->ta", branch_grad_low, out_full)
        .astype(jnp.bfloat16)
        .reshape(tok_rows, head_count, head_size)
    )
    scores_again = product("qhd,kd->hqk", query_low, key_part)
    probs = jnp.exp(jnp.where(allowed[None], scores_again, -1e30) - log_total)
    probs_again = probs.astype(jnp.bfloat16)
    grad_probs = product("qhd,kd->hqk", grad_heads, value_part)
    grad_scores = (
        probs * (grad_probs - jnp.sum(probs * grad_probs, axis=-1, keepdims=True))
    ).astype(jnp.bfloat16)
    grad_query_rot = product("hqk,kd->qhd", grad_scores, key_part)
    grad_keys = product("hqk,qhd->kd", grad_scores, query_low)
    grad_values = product("hqk,qhd->kd", probs_again, grad_heads)
    grad_packed = jnp.concatenate([grad_keys, grad_values], axis=1)
    collected = grad_packed[reach * tok_rows :]
    for distance in range(1, reach + 1):
        begin = (reach - distance) * tok_rows
        collected = collected + shifted(
            grad_packed[begin : begin + tok_rows].astype(jnp.bfloat16), "seq", -distance
        ).astype(jnp.float32)
    grad_key_rot = collected[:, :head_size]
    value_grad_low = collected[:, head_size:].astype(jnp.bfloat16)
    grad_q_raw, grad_k_raw, grad_gq, grad_gk = turn_back((grad_query_rot, grad_key_rot))
    query_grad_low = grad_q_raw.astype(jnp.bfloat16)
    key_grad_low = grad_k_raw.astype(jnp.bfloat16)
    grad_w_query = product("td,te->de", normed_low, query_grad_low)
    grad_w_key = product("td,te->de", normed_low, key_grad_low)
    grad_w_value = product("td,te->de", normed_low, value_grad_low)
    grad_normed = (
        product("te,de->td", query_grad_low, query_full)
        + product("te,de->td", key_grad_low, key_full)
        + product("te,de->td", value_grad_low, value_full)
    )
    grad_in, grad_gin = first_back(grad_normed)
    input_grad = (grad_resid + grad_in)[None]
    grad_gains = jnp.concatenate([grad_gin, grad_gq, grad_gk, grad_gpa, grad_gpf, grad_gpff])
    own = tuple(
        lax.psum_scatter(g.reshape(-1), ("seq", "fsdp"), scatter_dimension=0, tiled=True)
        for g in (
            grad_w_query,
            grad_w_key,
            grad_w_value,
            grad_w_out,
            grad_w_gate,
            grad_w_up,
            grad_w_down,
            grad_gains,
        )
    )
    return (result.astype(jnp.bfloat16)[None], input_grad) + own


XY = 4
LINE = 4


def mm(a, b):
    return lax.dot_general(a, b, (((1,), (0,)), ((), ())), preferred_element_type=F32)


def mm_nt(a, b):
    return lax.dot_general(a, b, (((1,), (1,)), ((), ())), preferred_element_type=F32)


def mm_tn(a, b):
    return lax.dot_general(a, b, (((0,), (0,)), ((), ())), preferred_element_type=F32)


def inverse_rms(x):
    return lax.rsqrt(jnp.mean(x * x, axis=-1, keepdims=True) + EPS)


def norm_back(hat, inv, gain, grad):
    scaled = grad * gain
    return inv * (scaled - hat * jnp.mean(hat * scaled, axis=-1, keepdims=True))


def turn_fwd(x, cosine, sine):
    half = x.shape[1] // 2
    a, b = x[:, :half], x[:, half:]
    return jnp.concatenate([a * cosine - b * sine, b * cosine + a * sine], axis=1)


def turn_bwd(x, cosine, sine):
    half = x.shape[1] // 2
    a, b = x[:, :half], x[:, half:]
    return jnp.concatenate([a * cosine + b * sine, b * cosine - a * sine], axis=1)


def all_gains(core, mine, theirs):
    a = mine[...].astype(F32)
    b = theirs[...].astype(F32)[: a.shape[0]]
    low, high = jnp.where(core == 0, a, b), jnp.where(core == 0, b, a)
    rows = [half[r : r + 1, :] for half in (low, high) for r in range(a.shape[0])]
    return jnp.concatenate(rows, axis=1)


def row_order(table, place, core):
    width = table.shape[0]
    owner = table[:, :1] ^ (place * 2 + core)
    source = owner * (width // (2 * XY * LINE)) + table[:, 1:2]
    ranks = lax.broadcasted_iota(jnp.int32, (width, width), 1)
    return jnp.where(ranks == source, 1.0, 0.0).astype(BF16)


class Traffic:
    def __init__(self, sems):
        self.sems = sems
        self.used = 0
        self.pending = []

    def start(self, source, target):
        copy = pltpu.make_async_copy(source, target, self.sems.at[self.used])
        self.used += 1
        copy.start()
        return copy

    def fetch(self, pairs):
        return [self.start(source, target) for source, target in pairs]

    def halves(self, core, mine, pack, pieces, full):
        rows = mine.shape[0]
        begin = pl.multiple_of(core * rows, 16)
        copies = [self.start(mine, full.at[pl.ds(begin, rows)])]
        for row, number, pack_row, column, cols in pieces:
            begin = pl.multiple_of((1 - core) * rows + row, 16)
            source = pack.at[pack_row : pack_row + number, column : column + cols]
            copies.append(self.start(source, full.at[pl.ds(begin, number)]))
        return copies

    def emit(self, source, target):
        self.pending.append(self.start(source, target))

    def finish(self):
        for copy in self.pending:
            copy.wait()


def pack_layout(rows, widths, talls):
    layout, column = [], 0
    for width in widths:
        layout.append([(0, rows, 0, column, width)])
        column += width
    at = 0
    for height, width in talls:
        pieces, done = [], 0
        while done < height:
            take = min(height - done, rows - at % rows)
            pieces.append((done, take, at % rows, column + at // rows * talls[0][1], width))
            done, at = done + take, at + take
        layout.append(pieces)
    return layout, column + -(-at // rows) * talls[0][1]


def prepare_kernel(layout, *refs):
    count = len(layout)
    tok_h, seg_h, *weights_h = refs[: count + 2]
    ext_h, pack_h = refs[count + 2 : count + 4]
    tok, seg, *weights = refs[count + 4 : 2 * count + 6]
    ext, gain_s, sems = refs[2 * count + 6 :]
    traffic = Traffic(sems)
    first = traffic.fetch([(tok_h, tok), (seg_h, seg)])
    rest = traffic.fetch(list(zip(weights_h, weights)))
    wait(first)
    rows, width = tok.shape
    ext[:rows, :] = tok[...]
    ext[rows:, :] = jnp.zeros((SEG_ROWS, width), BF16)
    ids = seg[...].astype(F32)
    ext[rows:, :rows] = jnp.broadcast_to(ids, (SEG_ROWS, rows)).astype(BF16)
    traffic.emit(ext, ext_h)
    for copy, source, pieces in zip(rest, weights, layout):
        copy.wait()
        if source is weights[-1]:
            missing = gain_s.shape[0] - source.shape[0]
            filled = [source[...].astype(F32), jnp.zeros((missing, LANES), F32)]
            gain_s[...] = jnp.concatenate(filled, axis=0).astype(BF16)
            source = gain_s
        for row, number, pack_row, column, cols in pieces:
            traffic.emit(
                source.at[row : row + number, :],
                pack_h.at[pack_row : pack_row + number, column : column + cols],
            )
    traffic.finish()


def wait(copies):
    for copy in copies:
        copy.wait()


def attention(reach, place, halo, gains, cos_ref, sin_ref, wq, wk, wv, outs, ready):
    n1_out, qraw_out, q_out, kraw_out, k_out, v_out, p_out, ao_out = outs
    width = n1_out.shape[1]
    rows = halo[0].shape[0] - SEG_ROWS
    size = k_out.shape[1]
    heads = q_out.shape[1] // size
    scale = size ** (-0.5)
    ready("halo")
    gains = gains()
    g_in = gains[:, :width]
    g_q = gains[:, width : width + size]
    g_k = gains[:, width + size : width + 2 * size]
    for block in range(reach + 1):
        x = halo[block][:rows, :].astype(F32)
        n1_out[block * rows : (block + 1) * rows, :] = (x * inverse_rms(x) * g_in).astype(BF16)
    ready("kv")
    n1 = n1_out[...]
    kraw = mm(n1, wk[...])
    kraw_out[...] = kraw
    k = turn_fwd(kraw * inverse_rms(kraw) * g_k, cos_ref[...], sin_ref[...]).astype(BF16)
    k_out[...] = k
    v = mm(n1, wv[...]).astype(BF16)
    v_out[...] = v
    keys = (reach + 1) * rows
    seg_rows = [halo[b][rows:, :rows].astype(F32)[:1] for b in range(reach + 1)]
    seg_keys = jnp.concatenate(seg_rows, axis=1)
    square = lax.broadcasted_iota(jnp.int32, (rows, rows), 0) == lax.broadcasted_iota(
        jnp.int32, (rows, rows), 1
    )
    seg_own = jnp.sum(jnp.where(square, seg_rows[reach], 0.0), axis=1, keepdims=True)
    at_query = reach * rows + lax.broadcasted_iota(jnp.int32, (rows, keys), 0)
    at_key = lax.broadcasted_iota(jnp.int32, (rows, keys), 1)
    gap = at_query - at_key
    allowed = (
        (seg_keys == seg_own)
        & (gap >= 0)
        & (gap < WINDOW)
        & (at_key >= (reach - place) * rows)
    )
    cos_own, sin_own = cos_ref[reach * rows :, :], sin_ref[reach * rows :, :]
    ready("query")
    for h in range(heads):
        cols = slice(h * size, (h + 1) * size)
        qraw = mm(n1_out[reach * rows :, :], wq[:, cols])
        qraw_out[:, cols] = qraw
        q = turn_fwd(qraw * inverse_rms(qraw) * g_q, cos_own, sin_own) * scale
        q = q.astype(BF16)
        q_out[:, cols] = q
        s = jnp.where(allowed, mm_nt(q, k), -1e30)
        e = jnp.exp(s - jnp.max(s, axis=-1, keepdims=True))
        p = e / jnp.sum(e, axis=-1, keepdims=True)
        p_out[h] = p
        ao_out[:, cols] = mm(p.astype(BF16), v).astype(BF16)


def pick_half(core, unit, width):
    row = lax.broadcasted_iota(jnp.int32, (LANES, width), 0)
    col = lax.broadcasted_iota(jnp.int32, (LANES, width), 1)
    want = (lax.div(row, unit) * 2 + core) * unit + lax.rem(row, unit)
    return jnp.where(col == want, 1.0, 0.0).astype(BF16)


def store_lanes(ref, base, value):
    rows = value.shape[0]
    for b in range(value.shape[1] // LANES):
        ref[base + b * rows : base + (b + 1) * rows, :] = value[:, b * LANES : (b + 1) * LANES]
    return base + rows * (value.shape[1] // LANES)


def forward_kernel(reach, layout, *refs):
    halo_h, refs = refs[: reach + 1], refs[reach + 1 :]
    ct_h, gains_h, order_h, cos_h, sin_h = refs[:5]
    wq_a, wk_a, wv_a, wg_a, wu_a, wo_a, wd_a, pack_h = refs[5:13]
    outs_h, refs = refs[13:27], refs[27:]
    halo, refs = refs[: reach + 1], refs[reach + 1 :]
    ct, gain_a, order, cos_ref, sin_ref = refs[:5]
    outs, refs = refs[5:19], refs[19:]
    wq, wk, wv, wo, wg, wu, wd, gate_s, up_s, hid_s, dg_s, du_s, ao_ref, gain_b, sems = refs
    place, core = lax.axis_index("seq"), lax.axis_index("fsdp")
    traffic = Traffic(sems)
    waits = {}
    _, _, pack_row, column, cols = layout[7][0]
    gain_far = pack_h.at[pack_row : pack_row + 16, column : column + cols]
    waits["halo"] = traffic.fetch(list(zip(halo_h, halo)))
    waits["halo"] += traffic.fetch([(gains_h, gain_a), (gain_far, gain_b)])
    waits["kv"] = traffic.halves(core, wk_a, pack_h, layout[1], wk)
    waits["kv"] += traffic.halves(core, wv_a, pack_h, layout[2], wv)
    waits["kv"] += traffic.fetch([(cos_h, cos_ref), (sin_h, sin_ref)])
    waits["query"] = traffic.halves(core, wq_a, pack_h, layout[0], wq)
    waits["out"] = traffic.halves(core, wo_a, pack_h, layout[5], wo)
    waits["gate"] = traffic.halves(core, wg_a, pack_h, layout[3], wg)
    waits["gate"] += traffic.halves(core, wu_a, pack_h, layout[4], wu)
    waits["down"] = traffic.halves(core, wd_a, pack_h, layout[6], wd)
    waits["rest"] = traffic.fetch([(ct_h, ct), (order_h, order)])

    def ready(name):
        wait(waits[name])

    attention(
        reach,
        place,
        halo,
        lambda: all_gains(core, gain_a, gain_b),
        cos_ref,
        sin_ref,
        wq,
        wk,
        wv,
        (*outs[:7], ao_ref),
        ready,
    )
    for source, target in zip(outs[:7], outs_h[:7]):
        traffic.emit(source, target)
    mixed_out, dx_out, dao_out, dg_out, keep, send, gains_out = outs[7:]
    rows, width = ct.shape
    gains = all_gains(core, gain_a, gain_b)
    gains_out[...] = gains
    size2 = gains.shape[1] - 4 * width
    ff = wg.shape[1]
    base = width + size2
    g_pa = gains[:, base : base + width]
    g_pf = gains[:, base + width : base + 2 * width]
    g_pff = gains[:, base + 2 * width :]
    x = halo[reach][:rows, :].astype(F32)
    ready("out")
    ya = mm(ao_ref[...], wo[...])
    inv_a = inverse_rms(ya)
    hat_a = ya * inv_a
    x2 = x + hat_a * g_pa
    inv_f = inverse_rms(x2)
    hat_f = x2 * inv_f
    n2 = (hat_f * g_pf).astype(BF16)
    ready("gate")
    ready("down")
    ready("rest")
    c = ct[...].astype(F32)
    part = 512
    root = math.sqrt(2.0 / math.pi)
    f = jnp.zeros((rows, width), F32)
    for at in range(0, ff, part):
        cols = slice(at, at + part)
        gate = mm(n2, wg[:, cols])
        up = mm(n2, wu[:, cols])
        gate_s[:, cols] = gate
        up_s[:, cols] = up
        t = jnp.tanh(root * (gate + 0.044715 * (gate * gate * gate)))
        hid = (0.5 * gate * (1.0 + t) * up).astype(BF16)
        hid_s[:, cols] = hid
        f = f + mm(hid, wd[cols, :])
    inv_d = inverse_rms(f)
    hat_d = f * inv_d
    mixed_out[...] = (x2 + hat_d * g_pff).astype(BF16)
    df = norm_back(hat_d, inv_d, g_pff, c).astype(BF16)
    dn2 = jnp.zeros((rows, width), F32)
    for at in range(0, ff, part):
        cols = slice(at, at + part)
        dhid = mm_nt(df, wd[cols, :])
        gate = gate_s[:, cols]
        up = up_s[:, cols]
        t = jnp.tanh(root * (gate + 0.044715 * (gate * gate * gate)))
        act = 0.5 * gate * (1.0 + t)
        slope = 0.5 * (1.0 + t) + 0.5 * gate * (1.0 - t * t) * (
            root * (1.0 + 3.0 * 0.044715 * (gate * gate))
        )
        dgate = (dhid * up * slope).astype(BF16)
        dup = (dhid * act).astype(BF16)
        dg_s[:, cols] = dgate
        du_s[:, cols] = dup
        dn2 = dn2 + mm_nt(dgate, wg[:, cols]) + mm_nt(dup, wu[:, cols])
    dx2 = c + norm_back(hat_f, inv_f, g_pf, dn2)
    dx_out[...] = dx2
    dya = norm_back(hat_a, inv_a, g_pa, dx2).astype(BF16)
    dao_out[...] = mm_nt(dya, wo[...]).astype(BF16)
    dg_out[:, :width] = jnp.sum(dx2 * hat_a, axis=0, keepdims=True)
    dg_out[:, width : 2 * width] = jnp.sum(dn2 * hat_f, axis=0, keepdims=True)
    dg_out[:, 2 * width :] = jnp.sum(c * hat_d, axis=0, keepdims=True)
    perm = row_order(order, place, core)
    n2_t = mm_nt(perm, n2).astype(BF16)
    half = width // 2
    keep[:half, :] = n2_t[:half]
    send[:half, :] = n2_t[half:]
    at = half
    for source, unit in ((hid_s, ff // 32), (ao_ref, ao_ref.shape[1] // 32)):
        for ref, side in ((keep, core), (send, 1 - core)):
            pick = pick_half(side, unit, 2 * LANES)
            for b in range(source.shape[1] // (2 * LANES)):
                block = source[:, 2 * b * LANES : 2 * (b + 1) * LANES]
                ref[at + b * LANES : at + (b + 1) * LANES, :] = mm_nt(pick, block).astype(BF16)
        at += source.shape[1] // 2
    for ref in (keep, send):
        base = store_lanes(ref, at, dg_s[...])
        base = store_lanes(ref, base, du_s[...])
        base = store_lanes(ref, base, df)
        store_lanes(ref, base, dya)
    for source, target in zip(outs[7:], outs_h[7:]):
        traffic.emit(source, target)
    traffic.finish()


def load_lanes(ref, base, rows, cols):
    blocks = [ref[base + b * rows : base + (b + 1) * rows, :] for b in range(cols // LANES)]
    return jnp.concatenate(blocks, axis=1), base + rows * (cols // LANES)


def put(xk, xs, first, plane, at, value):
    x_bit, y_bit = plane & 1, plane >> 1
    lead, other = (x_bit, y_bit) if first == "x" else (y_bit, x_bit)
    ref = xs if lead else xk
    ref[other, at : at + value.shape[0], :] = value


def grads_kernel(width, ff, attn, *refs):
    sources = refs[:2]
    outs_h = refs[2:8]
    outs = refs[8:14]
    gk, gs, uk, us, dk, ds = outs
    n2_s, hid_s, ao_s, gate_s, up_s, df_s, dya_s, prod_s, sems = refs[14:]
    traffic = Traffic(sems)
    place = lax.axis_index("seq")
    half = width // 2
    rows = LANES

    def sent(ref):
        traffic.emit(ref, outs_h[[r is ref for r in outs].index(True)])

    def lefts(base, target):
        return [
            traffic.start(
                source.at[base : base + target.shape[0], :],
                target.at[:, side * rows : (side + 1) * rows],
            )
            for side, source in enumerate(sources)
        ]

    def rights(base, target):
        return [
            traffic.start(
                source.at[base + b * rows : base + (b + 1) * rows, :],
                target.at[side * rows : (side + 1) * rows, b * LANES : (b + 1) * LANES],
            )
            for side, source in enumerate(sources)
            for b in range(target.shape[1] // LANES)
        ]

    at_hid = half
    at_ao = at_hid + ff // 2
    at_gate = at_ao + attn // 2
    at_up = at_gate + ff
    at_df = at_up + ff
    at_dya = at_df + width
    per = half // XY
    gate_w = lefts(0, n2_s) + rights(at_gate, gate_s)
    up_w = rights(at_up, up_s)
    down_w = lefts(at_hid, hid_s) + rights(at_df, df_s)
    out_w = lefts(at_ao, ao_s) + rights(at_dya, dya_s)
    for copies, right, (keep, send), first in (
        (gate_w, gate_s, (gk, gs), "x"),
        (up_w, up_s, (uk, us), "y"),
    ):
        wait(copies)
        for col in range(0, ff, 512):
            out = mm(n2_s[...], right[:, col : col + 512]).astype(BF16)
            for plane in range(XY):
                for b in range(4):
                    put(
                        keep,
                        send,
                        first,
                        plane,
                        (col // LANES + b) * per,
                        out[plane * per : (plane + 1) * per, b * LANES : (b + 1) * LANES],
                    )
        sent(send)
        sent(keep)
    row = 0
    for copies, left, right in ((down_w, hid_s, df_s), (out_w, ao_s, dya_s)):
        wait(copies)
        count = left.shape[0]
        prod_s[:count, :] = mm(left[...], right[...])
        unit = count // (XY * LINE)
        for plane in range(XY):
            for line in range(LINE):
                whose = (place ^ (line * XY + plane)) * unit
                block = prod_s[pl.ds(pl.multiple_of(whose, unit), unit), :].astype(BF16)
                ref = ds if line & 1 else dk
                chunk = (plane & 1) * 4 + (plane >> 1) * 2 + (line >> 1)
                for b in range(width // LANES):
                    ref[chunk, row + b * unit : row + (b + 1) * unit, :] = block[
                        :, b * LANES : (b + 1) * LANES
                    ]
        row += width // LANES * unit
    sent(ds)
    sent(dk)
    traffic.finish()


def back_kernel(reach, layout, *refs):
    count = reach + 15
    ins_h, refs = refs[:count], refs[count:]
    _, wq_a, wk_a, wv_a, pack_h = refs[:5]
    outs_h, refs = refs[5:9], refs[9:]
    ins, refs = refs[:count], refs[count:]
    halo = ins[: reach + 1]
    (
        gains,
        order,
        scale_order,
        dg_post,
        cos_ref,
        sin_ref,
        n1_ref,
        qraw_ref,
        q_ref,
        kraw_ref,
        k_ref,
        v_ref,
        p_ref,
        dao_ref,
    ) = ins[reach + 1 :]
    outs = keep, send, dn1_own, dn1_far = refs[:4]
    wq, wk, wv, dqr_s, dkv_s, sems = refs[4:]
    place, core = lax.axis_index("seq"), lax.axis_index("fsdp")
    traffic = Traffic(sems)
    heads = p_ref.shape[0]
    first = traffic.fetch([(ins_h[n], ins[n]) for n in (count - 1, count - 3, count - 4)])
    p_w = traffic.fetch([(ins_h[count - 2].at[h], p_ref.at[h]) for h in range(heads)])
    second = traffic.fetch([(ins_h[n], ins[n]) for n in range(reach + 1, count - 4)])
    copies = traffic.fetch(list(zip(ins_h[: reach + 1], halo)))
    for n, (mine, full) in enumerate(((wq_a, wq), (wk_a, wk), (wv_a, wv))):
        copies += traffic.halves(core, mine, pack_h, layout[n], full)
    wait(first)
    rows = halo[0].shape[0] - SEG_ROWS
    width = n1_ref.shape[1]
    size = k_ref.shape[1]
    scale = size ** (-0.5)
    k = k_ref[...]
    v = v_ref[...]
    keys = (reach + 1) * rows
    dk = jnp.zeros((keys, size), F32)
    dv = jnp.zeros((keys, size), F32)
    dgq = jnp.zeros((1, size), F32)
    for h in range(heads):
        cols = slice(h * size, (h + 1) * size)
        p_w[h].wait()
        p = p_ref[h]
        dao = dao_ref[:, cols]
        dp = mm_nt(dao, v)
        ds = (p * (dp - jnp.sum(p * dp, axis=-1, keepdims=True))).astype(BF16)
        dv = dv + mm_tn(p.astype(BF16), dao)
        if h == 0:
            wait(second)
            g_q = gains[:, width : width + size]
            g_k = gains[:, width + size : width + 2 * size]
            cos_own, sin_own = cos_ref[reach * rows :, :], sin_ref[reach * rows :, :]
        dk = dk + mm_tn(ds, q_ref[:, cols])
        dq = turn_bwd(mm(ds, k) * scale, cos_own, sin_own)
        qraw = qraw_ref[:, cols]
        inv = inverse_rms(qraw)
        hat = qraw * inv
        dgq = dgq + jnp.sum(dq * hat, axis=0, keepdims=True)
        dqr_s[:, cols] = norm_back(hat, inv, g_q, dq).astype(BF16)
    dk = turn_bwd(dk, cos_ref[...], sin_ref[...])
    kraw = kraw_ref[...]
    inv = inverse_rms(kraw)
    hat = kraw * inv
    dgk = jnp.sum(dk * hat, axis=0, keepdims=True)
    dkv_s[:, :size] = norm_back(hat, inv, g_k, dk).astype(BF16)
    dkv_s[:, size:] = dv.astype(BF16)
    perm = row_order(order, place, core)
    n1_t = mm_nt(perm, n1_ref[...]).astype(BF16)
    half = width // 2
    per = half // XY
    attn = heads * size
    wait(copies)
    dgi = jnp.zeros((1, width), F32)
    for block in range(reach + 1):
        span = slice(block * rows, (block + 1) * rows)
        dn1 = mm_nt(dkv_s[span, :size], wk[...]) + mm_nt(dkv_s[span, size:], wv[...])
        if block == reach:
            dn1 = dn1 + mm_nt(dqr_s[...], wq[...])
        x = halo[block][:rows, :].astype(F32)
        dgi = dgi + jnp.sum(dn1 * (x * inverse_rms(x)), axis=0, keepdims=True)
        if block == reach:
            dn1_own[...] = dn1
        else:
            bits = (place ^ (place - (reach - block))) & (XY - 1)
            low = dn1.astype(BF16)
            for b in range(width // LANES):
                dn1_far[bits, b * rows : (b + 1) * rows, :] = low[:, b * LANES : (b + 1) * LANES]
    scales = owners_rows(jnp.concatenate([dgi, dgq, dgk, dg_post[...]], axis=1))
    owner = scale_order[:, :1] ^ (place * 2 + core)
    mine = scale_order[:, 1:2] * 1024 + (owner & 3) * 8 + (owner >> 2)
    columns = lax.broadcasted_iota(jnp.int32, (mine.shape[0], 2 * XY * LINE), 1)
    scales = mm(jnp.where(columns == mine, 1.0, 0.0).astype(BF16), scales).astype(BF16)
    rows_each = scales.shape[0] // (2 * XY)
    for ref, begin, group in ((send, half, XY), (keep, 0, 0)):
        left = n1_t[begin : begin + half]
        own = left[:, reach * rows :]
        at = 0
        for value, left_part, total in (
            (dqr_s, own, attn),
            (dkv_s, left, 2 * size),
        ):
            for col in range(0, total, 512):
                out = mm(left_part, value[:, col : col + 512]).astype(BF16)
                for plane in range(XY):
                    for b in range(4):
                        ref[
                            plane,
                            at + (col // LANES + b) * per : at + (col // LANES + b + 1) * per,
                            :,
                        ] = out[plane * per : (plane + 1) * per, b * LANES : (b + 1) * LANES]
            at += total // LANES * per
        for plane in range(XY):
            row = (group + plane) * rows_each
            ref[plane, at : at + rows_each, :] = scales[row : row + rows_each]
        traffic.emit(ref, outs_h[0 if ref is keep else 1])
    for n in (3, 2):
        traffic.emit(outs[n], outs_h[n])
    traffic.finish()


def owners_rows(line):
    pieces = [line[:, r * LANES : (r + 1) * LANES] for r in range(line.shape[1] // LANES)]
    first, second, third = (jnp.concatenate(pieces[n::3], axis=0) for n in range(3))
    lane = lax.broadcasted_iota(jnp.int32, first.shape, 1)
    quarter = LANES // 4
    groups = [
        first,
        jnp.where(
            lane < quarter, pltpu.roll(first, quarter, 1), pltpu.roll(second, quarter, 1)
        ),
        jnp.where(
            lane < 2 * quarter,
            pltpu.roll(second, 2 * quarter, 1),
            pltpu.roll(third, 2 * quarter, 1),
        ),
        pltpu.roll(third, 3 * quarter, 1),
    ]
    return jnp.concatenate(groups, axis=0).astype(BF16)


def collect_kernel(skip, *refs):
    ins_h, outs_h = refs[: XY + 1], refs[XY + 1 : XY + 3]
    ins, outs, sems = refs[XY + 3 : 2 * XY + 4], refs[2 * XY + 4 : 2 * XY + 6], refs[-1]
    traffic = Traffic(sems)
    own, far, *near = ins
    near_h = [ref.at[skip:, :] for ref in ins_h[2:]]
    wait(traffic.fetch(list(zip((ins_h[0], ins_h[1].at[0], *near_h), ins))))
    place = lax.axis_index("seq") & (XY - 1)
    rows = own.shape[0]
    total = own[...]
    below = far[...].astype(F32)
    for bits, ref in enumerate(near, 1):
        part = ref[...].astype(F32)
        mine = (place ^ bits) > place
        below = below + jnp.where(mine, 0.0, part)
        lanes = [part[b * rows : (b + 1) * rows] for b in range(part.shape[0] // rows)]
        total = total + jnp.where(mine, jnp.concatenate(lanes, axis=1), 0.0)
    outs[0][...] = total
    outs[1][...] = below.astype(BF16)
    traffic.emit(outs[1], outs_h[1])
    traffic.emit(outs[0], outs_h[0])
    traffic.finish()


def finish_kernel(*refs):
    ins_h, out_h, ins, out, sems = refs[:5], refs[5], refs[6:11], refs[11], refs[12]
    traffic = Traffic(sems)
    wait(traffic.fetch(list(zip(ins_h, ins))))
    tok, gains, dx, dn1, above = ins
    rows, width = dx.shape
    lanes = [above[b * rows : (b + 1) * rows, :] for b in range(width // LANES)]
    total = dn1[...] + jnp.concatenate(lanes, axis=1).astype(F32)
    x = tok[:rows, :].astype(F32)
    inv = inverse_rms(x)
    out[...] = dx[...] + norm_back(x * inv, inv, gains[:, :width], total)
    traffic.emit(out, out_h)
    traffic.finish()


def line_split_kernel(groups, entries, extra, direct, *refs):
    count = sum(groups)
    ins_h, keep_h, send_h = refs[:count], refs[count], refs[count + 1]
    ins = refs[count + 2 : 2 * count + 2]
    keep, send, split, *sums, sems = refs[2 * count + 2 :]
    traffic = Traffic(sems)
    copies = traffic.fetch(list(zip(ins_h, ins)))
    at = 0
    for number, total in zip(groups, sums):
        wait(copies[at : at + number])
        value = ins[at][...].astype(F32)
        for other in ins[at + 1 : at + number]:
            value = value + other[: value.shape[0], :].astype(F32)
        total[...] = value
        at += number
    at = 0
    for group, row, blocks, unit in entries:
        for b in range(blocks):
            for position in range(LINE):
                begin = row + (b * LINE + position) * unit
                split[position, at : at + unit, :] = sums[group][begin : begin + unit, :]
            at += unit
    if extra:
        group, row = extra
        for position in range(LINE):
            one = sums[group][row + position : row + position + 1, :]
            split[position, at : at + 16, :] = jnp.broadcast_to(one, (16, LANES))
    order = ((keep, (0,)), (send, (1, 2, 3))) if direct else ((keep, (0, 2)), (send, (1, 3)))
    for ref, positions in order:
        for n, position in enumerate(positions):
            ref[n] = split[position].astype(ref.dtype)
    traffic.emit(send, send_h)
    traffic.emit(keep, keep_h)
    traffic.finish()


def join_kernel(parts, entries, extra, *refs):
    count = len(entries) + extra
    ins_h, outs_h = refs[:parts], refs[parts : parts + count]
    ins = refs[parts + count : 2 * parts + count]
    outs = refs[2 * parts + count : 2 * parts + 2 * count]
    sum_s, sems = refs[2 * parts + 2 * count :]
    traffic = Traffic(sems)
    wait(traffic.fetch(list(zip(ins_h, ins))))
    total = ins[0][...].astype(F32)
    for part in ins[1:]:
        total = total + part[...].astype(F32)
    sum_s[...] = total
    at = 0
    for (blocks, unit), out in zip(entries, outs):
        for b in range(blocks):
            out[pl.ds(b, unit, stride=blocks), :] = sum_s[at : at + unit, :]
            at += unit
    if extra:
        outs[-1][...] = sum_s[at : at + 8, :]
    for out, out_h in zip(outs, outs_h):
        traffic.emit(out, out_h)
    traffic.finish()


def call(kernel, fetched, others, outs, scratch, copies, flops, limit=56):
    hbm = pl.BlockSpec(memory_space=pl.ANY)
    return pl.pallas_call(
        kernel,
        out_shape=outs,
        in_specs=[hbm] * (len(fetched) + len(others)),
        out_specs=[hbm] * len(outs),
        scratch_shapes=[pltpu.VMEM(a.shape, a.dtype) for a in (*fetched, *outs)]
        + scratch
        + [pltpu.SemaphoreType.DMA((copies,))],
        compiler_params=pltpu.CompilerParams(vmem_limit_bytes=limit * MIB),
        cost_estimate=pl.CostEstimate(flops=flops, bytes_accessed=8 * MIB, transcendentals=0),
    )(*fetched, *others)


def shape(dims, dtype):
    return jax.ShapeDtypeStruct(dims, dtype)


def fast(
    tokens,
    segments,
    positions,
    w_query,
    w_key,
    w_value,
    w_out,
    w_gate,
    w_up,
    w_down,
    norm_gains,
    cotangent,
):
    rows, width = tokens.shape[1:]
    size = w_key.shape[1]
    attn = w_query.shape[1]
    heads = attn // size
    ff = w_gate.shape[1]
    count = norm_gains.shape[0] * 2
    reach = (WINDOW - 1 + rows - 1) // rows
    keys = (reach + 1) * rows
    place = lax.axis_index("seq")
    core = lax.axis_index("fsdp")

    def partner(value):
        return lax.ppermute(value, "fsdp", [(0, 1), (1, 0)])

    def across(value, bits):
        return lax.ppermute(value, "seq", [(i, i ^ bits) for i in range(XY * LINE)])

    gains_own = norm_gains.reshape(-1, LANES)
    weights = (w_query, w_key, w_value, w_gate, w_up, w_out, w_down)
    layout, columns = pack_layout(
        width // 2,
        [w.shape[1] for w in weights[:5]],
        [w.shape for w in weights[5:]] + [(16, LANES)],
    )
    tok, pack = pl.pallas_call(
        functools.partial(prepare_kernel, layout),
        out_shape=[
            shape((rows + SEG_ROWS, width), BF16),
            shape((width // 2, columns), BF16),
        ],
        in_specs=[pl.BlockSpec(memory_space=pl.ANY)] * 10,
        out_specs=[pl.BlockSpec(memory_space=pl.ANY)] * 2,
        scratch_shapes=[pltpu.VMEM((rows, width), BF16), pltpu.VMEM((1, rows), jnp.int32)]
        + [pltpu.VMEM(w.shape, BF16) for w in (*weights, gains_own)]
        + [
            pltpu.VMEM((rows + SEG_ROWS, width), BF16),
            pltpu.VMEM((16, LANES), BF16),
            pltpu.SemaphoreType.DMA((40,)),
        ],
        compiler_params=pltpu.CompilerParams(vmem_limit_bytes=56 * MIB),
    )(tokens[0], segments, *weights, gains_own)
    pack_far = partner(pack)
    halo = [shifted(tok, "seq", distance) for distance in range(reach, 0, -1)] + [tok]

    unit = width // (2 * XY * LINE)
    new = np.arange(width) // unit
    core_bit, plane, line = new // (XY * LINE), new // LINE % XY, new % LINE
    owner = (line * XY + plane) * 2 + core_bit
    order = jnp.asarray(np.stack([owner, np.arange(width) % unit], axis=1).astype(np.int32))
    freq = np.exp(np.arange(size // 2, dtype=np.float64) * (-2.0 * math.log(10000.0) / size))
    turn = np.arange(keys, dtype=np.float64)[:, None] * freq
    cosine = jnp.asarray(np.cos(turn).astype(np.float32))
    sine = jnp.asarray(np.sin(turn).astype(np.float32))

    packed = width // 2 + ff // 2 + attn // 2 + 2 * ff + 2 * width
    n1, qraw, q, kraw, k, v, p, mixed, dx, dao, dg_post, mlp_keep, mlp_send, gains = call(
        functools.partial(forward_kernel, reach, layout),
        (*halo, cotangent[0], gains_own, order, cosine, sine),
        (*weights, pack_far),
        [
            shape((keys, width), BF16),
            shape((rows, attn), F32),
            shape((rows, attn), BF16),
            shape((keys, size), F32),
            shape((keys, size), BF16),
            shape((keys, size), BF16),
            shape((heads, rows, keys), F32),
            shape((rows, width), BF16),
            shape((rows, width), F32),
            shape((rows, attn), BF16),
            shape((1, 3 * width), F32),
            shape((packed, LANES), BF16),
            shape((packed, LANES), BF16),
            shape((1, count), F32),
        ],
        [
            pltpu.VMEM((width, attn), BF16),
            pltpu.VMEM((width, size), BF16),
            pltpu.VMEM((width, size), BF16),
            pltpu.VMEM((attn, width), BF16),
            pltpu.VMEM((width, ff), BF16),
            pltpu.VMEM((width, ff), BF16),
            pltpu.VMEM((ff, width), BF16),
            pltpu.VMEM((rows, ff), F32),
            pltpu.VMEM((rows, ff), F32),
            pltpu.VMEM((rows, ff), BF16),
            pltpu.VMEM((rows, ff), BF16),
            pltpu.VMEM((rows, ff), BF16),
            pltpu.VMEM((rows, attn), BF16),
            pltpu.VMEM((16, LANES), BF16),
        ],
        72,
        7 * 10**9,
    )
    mlp_recv = partner(mlp_send)

    per_ff = width // 2 // XY * ff // LANES
    per_down = ff // 2 // XY * width // LANES
    per_out = attn // 2 // XY * width // LANES
    halves = [shape((2, per_ff, LANES), BF16)] * 2
    halves += [shape((2, per_ff, LANES), BF16)] * 2
    halves += [shape((8, (per_down + per_out) // LINE, LANES), BF16)] * 2
    gk, gs, uk, us, dk, ds = call(
        functools.partial(grads_kernel, width, ff, attn),
        (),
        (mlp_keep, mlp_recv),
        halves,
        [
            pltpu.VMEM((width // 2, 2 * LANES), BF16),
            pltpu.VMEM((ff // 2, 2 * LANES), BF16),
            pltpu.VMEM((attn // 2, 2 * LANES), BF16),
            pltpu.VMEM((2 * LANES, ff), BF16),
            pltpu.VMEM((2 * LANES, ff), BF16),
            pltpu.VMEM((2 * LANES, width), BF16),
            pltpu.VMEM((2 * LANES, width), BF16),
            pltpu.VMEM((ff // 2, width), F32),
        ],
        128,
        10**9,
        32,
    )

    per_q = width // 2 // XY * attn // LANES
    per_k = width // 2 // XY * size // LANES
    per_back = per_q + 2 * per_k
    share = count // (2 * XY * LINE)
    new = np.arange(2 * XY * 16)
    core_bit, plane, line = new // (XY * 16), new // 16 % XY, new % 16
    owner = (line % LINE * XY + plane) * 2 + core_bit
    scale_order = jnp.asarray(np.stack([owner, line // LINE], axis=1).astype(np.int32))
    back_keep, back_send, dn1_own, dn1_far = call(
        functools.partial(back_kernel, reach, layout),
        (*halo, gains, order, scale_order, dg_post, cosine, sine, n1, qraw, q, kraw, k, v, p, dao),
        (gk, *weights[:3], pack_far),
        [
            shape((XY, per_back + 16, LANES), BF16),
            shape((XY, per_back + 16, LANES), BF16),
            shape((rows, width), F32),
            shape((XY, rows * width // LANES, LANES), BF16),
        ],
        [
            pltpu.VMEM((width, attn), BF16),
            pltpu.VMEM((width, size), BF16),
            pltpu.VMEM((width, size), BF16),
            pltpu.VMEM((rows, attn), BF16),
            pltpu.VMEM((keys, 2 * size), BF16),
        ],
        64,
        4 * 10**9,
    )
    back_recv = partner(back_send)

    def add(a, b):
        return (a.astype(F32) + b.astype(F32)).astype(BF16)

    def step(keep, send, bits):
        near = across(send, bits)
        half = keep.shape[0] // 2
        return add(keep[:half], near[:half]), add(keep[half:], near[half:])

    def line_split(groups, entries, extra, direct):
        part = sum(blocks * unit for _, _, blocks, unit in entries) + (16 if extra else 0)
        stay = 1 if direct else 2
        return call(
            functools.partial(
                line_split_kernel, [len(g) for g in groups], entries, extra, direct
            ),
            [array for g in groups for array in g],
            (),
            [shape((stay, part, LANES), BF16), shape((LINE - stay, part, LANES), BF16)],
            [pltpu.VMEM((LINE, part, LANES), F32)]
            + [pltpu.VMEM(g[0].shape, F32) for g in groups],
            sum(len(g) for g in groups) + 2,
            10**8,
            24,
        )

    def join(parts, entries, extra=False):
        outs = [shape((blocks * unit, LANES), F32) for blocks, unit in entries]
        if extra:
            outs.append(shape((8, LANES), F32))
        return call(
            functools.partial(join_kernel, len(parts), entries, int(extra)),
            parts,
            (),
            outs,
            [pltpu.VMEM(parts[0].shape, F32)],
            len(parts) + len(outs),
            10**8,
            24,
        )

    wide, narrow = ff // LANES, width // LANES
    unit_out, unit_down = attn // 32, ff // 32

    gate_0, gate_1 = step(gk, gs, 1)
    up_0, up_1 = step(uk, us, 2)
    gate_2, up_2 = across(gate_1, 2), across(up_1, 1)
    flat = lambda value: value.reshape(value.shape[1:])
    keep, send = line_split(
        ((flat(gate_0), flat(gate_2)), (flat(up_0), flat(up_2))),
        ((0, 0, wide, unit), (1, 0, wide, unit)),
        None,
        False,
    )
    mlp_0, mlp_1 = step(keep, send, XY)
    own_gate, own_up = join(
        (flat(mlp_0), flat(across(mlp_1, 2 * XY))), ((wide, unit), (wide, unit))
    )
    down_0, down_1 = step(dk, ds, XY)
    down_0, down_1 = step(down_0, down_1, 1)
    down_0, down_1 = step(down_0, down_1, 2)
    own_down, own_out = join(
        (flat(down_0), flat(across(down_1, 2 * XY))), ((narrow, unit_down), (narrow, unit_out))
    )

    planes = [add(back_keep[n], back_recv[n]) for n in range(XY)]
    planes = [planes[0]] + [
        across(jnp.concatenate([planes[n], dn1_far[n]]), n) for n in range(1, XY)
    ]
    keep, send = line_split(
        (planes,),
        (
            (0, 0, attn // LANES, unit),
            (0, per_q, size // LANES, unit),
            (0, per_q + per_k, size // LANES, unit),
        ),
        (0, per_back),
        True,
    )
    own_query, own_key, own_value, own_gains = join(
        (flat(keep), *[across(send[n], (n + 1) * XY) for n in range(LINE - 1)]),
        ((attn // LANES, unit), (size // LANES, unit), (size // LANES, unit)),
        True,
    )

    far_shape = (rows * width // LANES, LANES)
    dn1, below = pl.pallas_call(
        functools.partial(collect_kernel, per_back + 16),
        out_shape=[shape((rows, width), F32), shape(far_shape, BF16)],
        in_specs=[pl.BlockSpec(memory_space=pl.ANY)] * (XY + 1),
        out_specs=[pl.BlockSpec(memory_space=pl.ANY)] * 2,
        scratch_shapes=[pltpu.VMEM((rows, width), F32)]
        + [pltpu.VMEM(far_shape, BF16)] * XY
        + [pltpu.VMEM((rows, width), F32), pltpu.VMEM(far_shape, BF16)]
        + [pltpu.SemaphoreType.DMA((XY + 3,))],
        compiler_params=pltpu.CompilerParams(vmem_limit_bytes=24 * MIB),
    )(dn1_own, dn1_far, *planes[1:])
    (input_grad,) = call(
        finish_kernel,
        (tok, gains, dx, dn1, shifted(below, "seq", -XY)),
        (),
        [shape((rows, width), F32)],
        [],
        6,
        10**8,
        24,
    )
    return (
        mixed[None],
        input_grad[None],
        own_query.reshape(-1),
        own_key.reshape(-1),
        own_value.reshape(-1),
        own_out.reshape(-1),
        own_gate.reshape(-1),
        own_up.reshape(-1),
        own_down.reshape(-1),
        own_gains[0, :share],
    )


def solution(mesh):
    placed = (
        P("fsdp", "seq", None),
        P("fsdp", "seq"),
        P("fsdp", "seq"),
        P("fsdp", None),
        P("fsdp", None),
        P("fsdp", None),
        P("fsdp", None),
        P("fsdp", None),
        P("fsdp", None),
        P("fsdp", None),
        P("fsdp"),
        P("fsdp", "seq", None),
    )
    small = mesh.shape["seq"] == XY * LINE and mesh.shape["fsdp"] == 2
    return jax.shard_map(
        fast if small else general,
        mesh=mesh,
        in_specs=placed,
        out_specs=(
            P("fsdp", "seq", None),
            P("fsdp", "seq", None),
            P(("seq", "fsdp")),
            P(("seq", "fsdp")),
            P(("seq", "fsdp")),
            P(("seq", "fsdp")),
            P(("seq", "fsdp")),
            P(("seq", "fsdp")),
            P(("seq", "fsdp")),
            P(("seq", "fsdp")),
        ),
        check_vma=False,
    )
```

```python
import functools
import math

import jax
import jax.numpy as jnp
import numpy as np
from jax import lax
from jax.experimental import pallas as pl
from jax.experimental.pallas import tpu as pltpu
from jax.sharding import PartitionSpec as P

WINDOW = 512
EPS = 1e-06
LANES = 128
SEG_ROWS = 16
F32 = jnp.float32
BF16 = jnp.bfloat16
MIB = 1 << 20


def shifted(x, axis, by):
    peers = lax.axis_size(axis)
    pairs = [(i, i + by) for i in range(peers) if 0 <= i + by < peers]
    return lax.ppermute(x, axis, pairs)


def norm_rows(value, gain):
    return value * lax.rsqrt(jnp.mean(value * value, axis=-1, keepdims=True) + EPS) * gain


def rotate(value, cosine, sine):
    half = value.shape[-1] // 2
    first = value[..., :half]
    second = value[..., half:]
    return jnp.concatenate(
        [first * cosine - second * sine, second * cosine + first * sine], axis=-1
    )


def angles(positions, size):
    freq = jnp.exp(jnp.arange(size // 2, dtype=jnp.float32) * (-2.0 * math.log(10000.0) / size))
    turn = positions.astype(jnp.float32)[..., None] * freq
    return (jnp.cos(turn), jnp.sin(turn))


def product(form, left, right):
    return jnp.einsum(form, left, right, preferred_element_type=jnp.float32)


def general(
    tokens,
    segments,
    positions,
    w_query,
    w_key,
    w_value,
    w_out,
    w_gate,
    w_up,
    w_down,
    norm_gains,
    cotangent,
):
    tok_rows = tokens.shape[1]
    width = tokens.shape[2]
    head_size = w_key.shape[1]
    head_count = w_query.shape[1] // head_size
    reach = (WINDOW - 1 + tok_rows - 1) // tok_rows
    scale = head_size ** (-0.5)
    gathered = tuple(
        lax.all_gather(w, "fsdp", axis=0, tiled=True)
        for w in (w_query, w_key, w_value, w_out, w_gate, w_up, w_down, norm_gains)
    )
    query_full, key_full, value_full, out_full, gate_full, up_full, down_full, gains_full = gathered
    gains = gains_full.astype(jnp.float32)
    gain_in = gains[:width]
    gain_q = gains[width : width + head_size]
    gain_k = gains[width + head_size : width + 2 * head_size]
    gain_pa = gains[width + 2 * head_size : 2 * width + 2 * head_size]
    gain_pf = gains[2 * width + 2 * head_size : 3 * width + 2 * head_size]
    gain_pff = gains[3 * width + 2 * head_size :]
    hidden_in = tokens[0].astype(jnp.float32)
    segment = segments[0]
    cosine, sine = angles(positions[0], head_size)
    normed, first_back = jax.vjp(norm_rows, hidden_in, gain_in)
    normed_low = normed.astype(jnp.bfloat16)
    query_raw = jnp.dot(normed_low, query_full, preferred_element_type=jnp.float32)
    key_raw = jnp.dot(normed_low, key_full, preferred_element_type=jnp.float32)
    value_low = jnp.dot(normed_low, value_full, preferred_element_type=jnp.float32).astype(
        jnp.bfloat16
    )

    def turn(query, key, gain_query, gain_key):
        query = norm_rows(query.reshape(tok_rows, head_count, head_size), gain_query)
        query = rotate(query, cosine[:, None, :], sine[:, None, :]) * scale
        key = rotate(norm_rows(key, gain_key), cosine, sine)
        return (query, key)

    (query_rot, key_rot), turn_back = jax.vjp(turn, query_raw, key_raw, gain_q, gain_k)
    query_low = query_rot.astype(jnp.bfloat16)
    packed = jnp.concatenate([key_rot.astype(jnp.bfloat16), value_low], axis=1)
    pieces = [packed]
    seg_pieces = [segment]
    for distance in range(1, reach + 1):
        far_pack, far_seg = shifted((packed, segment), "seq", distance)
        pieces.insert(0, far_pack)
        seg_pieces.insert(0, far_seg)
    keys_all = jnp.concatenate(pieces, axis=0)
    seg_all = jnp.concatenate(seg_pieces, axis=0)
    key_part = keys_all[:, :head_size]
    value_part = keys_all[:, head_size:]
    place = lax.axis_index("seq")
    query_index = place * tok_rows + jnp.arange(tok_rows, dtype=jnp.int32)
    key_index = (place - reach) * tok_rows + jnp.arange((reach + 1) * tok_rows, dtype=jnp.int32)
    spacing = query_index[:, None] - key_index[None, :]
    allowed = (
        (segment[:, None] == seg_all[None, :])
        & (spacing >= 0)
        & (spacing < WINDOW)
        & (key_index[None, :] >= 0)
    )
    scores = product("qhd,kd->hqk", query_low, key_part)
    masked = jnp.where(allowed[None], scores, -1e30)
    top = jnp.max(masked, axis=-1, keepdims=True)
    expd = jnp.exp(masked - top)
    total = jnp.sum(expd, axis=-1, keepdims=True)
    probs_low = (expd / total).astype(jnp.bfloat16)
    log_total = top + jnp.log(total)
    mixed_heads = (
        product("hqk,kd->qhd", probs_low, value_part)
        .reshape(tok_rows, head_count * head_size)
        .astype(jnp.bfloat16)
    )
    attn_out = jnp.dot(mixed_heads, out_full, preferred_element_type=jnp.float32)

    def middle(resid, branch, gain_a, gain_b):
        after = resid + norm_rows(branch, gain_a)
        return (after, norm_rows(after, gain_b))

    (after, normed_ff), middle_back = jax.vjp(middle, hidden_in, attn_out, gain_pa, gain_pf)
    ff_low = normed_ff.astype(jnp.bfloat16)
    gate = jnp.dot(ff_low, gate_full, preferred_element_type=jnp.float32)
    up_value = jnp.dot(ff_low, up_full, preferred_element_type=jnp.float32)

    def mixer(gate_in, up_in):
        return jax.nn.gelu(gate_in, approximate=True) * up_in

    inner, mixer_back = jax.vjp(mixer, gate, up_value)
    inner_low = inner.astype(jnp.bfloat16)
    down = jnp.dot(inner_low, down_full, preferred_element_type=jnp.float32)

    def finish(resid, branch, gain):
        return resid + norm_rows(branch, gain)

    result, finish_back = jax.vjp(finish, after, down, gain_pff)
    grad_result = cotangent[0].astype(jnp.float32)
    grad_after, grad_down, grad_gpff = finish_back(grad_result)
    down_grad_low = grad_down.astype(jnp.bfloat16)
    grad_w_down = product("tf,td->fd", inner_low, down_grad_low)
    grad_inner = product("td,fd->tf", down_grad_low, down_full)
    grad_gate, grad_upv = mixer_back(grad_inner)
    gate_grad_low = grad_gate.astype(jnp.bfloat16)
    up_grad_low = grad_upv.astype(jnp.bfloat16)
    grad_w_gate = product("td,tf->df", ff_low, gate_grad_low)
    grad_w_up = product("td,tf->df", ff_low, up_grad_low)
    grad_normed_ff = product("tf,df->td", gate_grad_low, gate_full) + product(
        "tf,df->td", up_grad_low, up_full
    )
    grad_resid, grad_branch, grad_gpa, grad_gpf = middle_back((grad_after, grad_normed_ff))
    branch_grad_low = grad_branch.astype(jnp.bfloat16)
    grad_w_out = product("ta,td->ad", mixed_heads, branch_grad_low)
    grad_heads = (
        product("td,ad->ta", branch_grad_low, out_full)
        .astype(jnp.bfloat16)
        .reshape(tok_rows, head_count, head_size)
    )
    scores_again = product("qhd,kd->hqk", query_low, key_part)
    probs = jnp.exp(jnp.where(allowed[None], scores_again, -1e30) - log_total)
    probs_again = probs.astype(jnp.bfloat16)
    grad_probs = product("qhd,kd->hqk", grad_heads, value_part)
    grad_scores = (
        probs * (grad_probs - jnp.sum(probs * grad_probs, axis=-1, keepdims=True))
    ).astype(jnp.bfloat16)
    grad_query_rot = product("hqk,kd->qhd", grad_scores, key_part)
    grad_keys = product("hqk,qhd->kd", grad_scores, query_low)
    grad_values = product("hqk,qhd->kd", probs_again, grad_heads)
    grad_packed = jnp.concatenate([grad_keys, grad_values], axis=1)
    collected = grad_packed[reach * tok_rows :]
    for distance in range(1, reach + 1):
        begin = (reach - distance) * tok_rows
        collected = collected + shifted(
            grad_packed[begin : begin + tok_rows].astype(jnp.bfloat16), "seq", -distance
        ).astype(jnp.float32)
    grad_key_rot = collected[:, :head_size]
    value_grad_low = collected[:, head_size:].astype(jnp.bfloat16)
    grad_q_raw, grad_k_raw, grad_gq, grad_gk = turn_back((grad_query_rot, grad_key_rot))
    query_grad_low = grad_q_raw.astype(jnp.bfloat16)
    key_grad_low = grad_k_raw.astype(jnp.bfloat16)
    grad_w_query = product("td,te->de", normed_low, query_grad_low)
    grad_w_key = product("td,te->de", normed_low, key_grad_low)
    grad_w_value = product("td,te->de", normed_low, value_grad_low)
    grad_normed = (
        product("te,de->td", query_grad_low, query_full)
        + product("te,de->td", key_grad_low, key_full)
        + product("te,de->td", value_grad_low, value_full)
    )
    grad_in, grad_gin = first_back(grad_normed)
    input_grad = (grad_resid + grad_in)[None]
    grad_gains = jnp.concatenate([grad_gin, grad_gq, grad_gk, grad_gpa, grad_gpf, grad_gpff])
    own = tuple(
        lax.psum_scatter(g.reshape(-1), ("seq", "fsdp"), scatter_dimension=0, tiled=True)
        for g in (
            grad_w_query,
            grad_w_key,
            grad_w_value,
            grad_w_out,
            grad_w_gate,
            grad_w_up,
            grad_w_down,
            grad_gains,
        )
    )
    return (result.astype(jnp.bfloat16)[None], input_grad) + own


XY = 4
LINE = 4


def mm(a, b):
    return lax.dot_general(a, b, (((1,), (0,)), ((), ())), preferred_element_type=F32)


def mm_nt(a, b):
    return lax.dot_general(a, b, (((1,), (1,)), ((), ())), preferred_element_type=F32)


def mm_tn(a, b):
    return lax.dot_general(a, b, (((0,), (0,)), ((), ())), preferred_element_type=F32)


def inverse_rms(x):
    return lax.rsqrt(jnp.mean(x * x, axis=-1, keepdims=True) + EPS)


def norm_back(hat, inv, gain, grad):
    scaled = grad * gain
    return inv * (scaled - hat * jnp.mean(hat * scaled, axis=-1, keepdims=True))


def turn_fwd(x, cosine, sine):
    half = x.shape[1] // 2
    a, b = x[:, :half], x[:, half:]
    return jnp.concatenate([a * cosine - b * sine, b * cosine + a * sine], axis=1)


def turn_bwd(x, cosine, sine):
    half = x.shape[1] // 2
    a, b = x[:, :half], x[:, half:]
    return jnp.concatenate([a * cosine + b * sine, b * cosine - a * sine], axis=1)


def all_gains(core, mine, theirs):
    a = mine[...].astype(F32)
    b = theirs[...].astype(F32)[: a.shape[0]]
    low, high = jnp.where(core == 0, a, b), jnp.where(core == 0, b, a)
    rows = [half[r : r + 1, :] for half in (low, high) for r in range(a.shape[0])]
    return jnp.concatenate(rows, axis=1)


def row_order(table, width, place, core):
    owner = table[:, :1] ^ (place * 2 + core)
    source = owner * (width // (2 * XY * LINE)) + table[:, 1:2]
    ranks = lax.broadcasted_iota(jnp.int32, (table.shape[0], width), 1)
    return jnp.where(ranks == source, 1.0, 0.0).astype(BF16)


class Traffic:
    def __init__(self, sems):
        self.sems = sems
        self.used = 0
        self.pending = []

    def start(self, source, target):
        copy = pltpu.make_async_copy(source, target, self.sems.at[self.used])
        self.used += 1
        copy.start()
        return copy

    def fetch(self, pairs):
        return [self.start(source, target) for source, target in pairs]

    def halves(self, core, mine, pack, pieces, full):
        rows = mine.shape[0]
        begin = pl.multiple_of(core * rows, 16)
        copies = [self.start(mine, full.at[pl.ds(begin, rows)])]
        for row, number, pack_row, column, cols in pieces:
            begin = pl.multiple_of((1 - core) * rows + row, 16)
            source = pack.at[pack_row : pack_row + number, column : column + cols]
            copies.append(self.start(source, full.at[pl.ds(begin, number)]))
        return copies

    def emit(self, source, target):
        self.pending.append(self.start(source, target))

    def finish(self):
        for copy in self.pending:
            copy.wait()


def pack_layout(rows, widths, talls):
    layout, column = [], 0
    for width in widths:
        layout.append([(0, rows, 0, column, width)])
        column += width
    at = 0
    for height, width in talls:
        pieces, done = [], 0
        while done < height:
            take = min(height - done, rows - at % rows)
            pieces.append((done, take, at % rows, column + at // rows * talls[0][1], width))
            done, at = done + take, at + take
        layout.append(pieces)
    return layout, column + -(-at // rows) * talls[0][1]


def prepare_kernel(layout, *refs):
    count = len(layout)
    tok_h, seg_h, *weights_h = refs[: count + 2]
    ext_h, pack_h = refs[count + 2 : count + 4]
    tok, seg, *weights = refs[count + 4 : 2 * count + 6]
    ext, gain_s, sems = refs[2 * count + 6 :]
    traffic = Traffic(sems)
    first = traffic.fetch([(tok_h, tok), (seg_h, seg)])
    rest = traffic.fetch(list(zip(weights_h, weights)))
    wait(first)
    rows, width = tok.shape
    ext[:rows, :] = tok[...]
    ext[rows:, :] = jnp.zeros((SEG_ROWS, width), BF16)
    ids = seg[...].astype(F32)
    ext[rows:, :rows] = jnp.broadcast_to(ids, (SEG_ROWS, rows)).astype(BF16)
    traffic.emit(ext, ext_h)
    for copy, source, pieces in zip(rest, weights, layout):
        copy.wait()
        if source is weights[-1]:
            missing = gain_s.shape[0] - source.shape[0]
            filled = [source[...].astype(F32), jnp.zeros((missing, LANES), F32)]
            gain_s[...] = jnp.concatenate(filled, axis=0).astype(BF16)
            source = gain_s
        for row, number, pack_row, column, cols in pieces:
            traffic.emit(
                source.at[row : row + number, :],
                pack_h.at[pack_row : pack_row + number, column : column + cols],
            )
    traffic.finish()


def wait(copies):
    for copy in copies:
        copy.wait()


def attention(reach, place, halo, gains, cos_ref, sin_ref, wq, wk, wv, outs, ready):
    n1_out, qraw_out, q_out, kraw_out, k_out, v_out, p_out, ao_out = outs
    width = n1_out.shape[1]
    rows = halo[0].shape[0] - SEG_ROWS
    size = k_out.shape[1]
    heads = q_out.shape[1] // size
    scale = size ** (-0.5)
    ready("halo")
    gains = gains()
    g_in = gains[:, :width]
    g_q = gains[:, width : width + size]
    g_k = gains[:, width + size : width + 2 * size]
    for block in range(reach + 1):
        x = halo[block][:rows, :].astype(F32)
        n1_out[block * rows : (block + 1) * rows, :] = (x * inverse_rms(x) * g_in).astype(BF16)
    ready("kv")
    n1 = n1_out[...]
    kraw = mm(n1, wk[...])
    kraw_out[...] = kraw
    k = turn_fwd(kraw * inverse_rms(kraw) * g_k, cos_ref[...], sin_ref[...]).astype(BF16)
    k_out[...] = k
    v = mm(n1, wv[...]).astype(BF16)
    v_out[...] = v
    keys = (reach + 1) * rows
    seg_rows = [halo[b][rows:, :rows].astype(F32)[:1] for b in range(reach + 1)]
    seg_keys = jnp.concatenate(seg_rows, axis=1)
    square = lax.broadcasted_iota(jnp.int32, (rows, rows), 0) == lax.broadcasted_iota(
        jnp.int32, (rows, rows), 1
    )
    seg_own = jnp.sum(jnp.where(square, seg_rows[reach], 0.0), axis=1, keepdims=True)
    at_query = reach * rows + lax.broadcasted_iota(jnp.int32, (rows, keys), 0)
    at_key = lax.broadcasted_iota(jnp.int32, (rows, keys), 1)
    gap = at_query - at_key
    allowed = (
        (seg_keys == seg_own)
        & (gap >= 0)
        & (gap < WINDOW)
        & (at_key >= (reach - place) * rows)
    )
    cos_own, sin_own = cos_ref[reach * rows :, :], sin_ref[reach * rows :, :]
    ready("query")
    for h in range(heads):
        cols = slice(h * size, (h + 1) * size)
        qraw = mm(n1_out[reach * rows :, :], wq[:, cols])
        qraw_out[:, cols] = qraw
        q = turn_fwd(qraw * inverse_rms(qraw) * g_q, cos_own, sin_own) * scale
        q = q.astype(BF16)
        q_out[:, cols] = q
        s = jnp.where(allowed, mm_nt(q, k), -1e30)
        e = jnp.exp(s - jnp.max(s, axis=-1, keepdims=True))
        p = e * (1.0 / jnp.sum(e, axis=-1, keepdims=True))
        p_out[h] = p
        ao_out[:, cols] = mm(p.astype(BF16), v).astype(BF16)


def pick_halves(core, unit):
    row = lax.broadcasted_iota(jnp.int32, (2 * LANES, 2 * LANES), 0)
    col = lax.broadcasted_iota(jnp.int32, (2 * LANES, 2 * LANES), 1)
    side = jnp.where(col < LANES, core, 1 - core)
    at = col & (LANES - 1)
    want = (lax.div(at, unit) * 2 + side) * unit + lax.rem(at, unit)
    return jnp.where(row == want, 1.0, 0.0).astype(BF16)


def store_halves(keep, send, base, source, unit, core):
    pick = pick_halves(core, unit)
    for b in range(source.shape[1] // (2 * LANES)):
        block = mm(source[:, 2 * b * LANES : 2 * (b + 1) * LANES], pick).astype(BF16)
        keep[:, base + b * LANES : base + (b + 1) * LANES] = block[:, :LANES]
        send[:, base + b * LANES : base + (b + 1) * LANES] = block[:, LANES:]


def pair_columns(width, ff, attn):
    sizes = (ff, ff, width, width, ff // 2, attn // 2, padded(width // 2))
    starts = [sum(sizes[:n]) for n in range(len(sizes) + 1)]
    return starts[:-1], starts[-1]


def padded(columns):
    return -(-columns // LANES) * LANES


def forward_kernel(reach, layout, *refs):
    halo_h, refs = refs[: reach + 1], refs[reach + 1 :]
    ct_h, gains_h, order_h, cos_h, sin_h = refs[:5]
    wq_a, wk_a, wv_a, wg_a, wu_a, wo_a, wd_a, pack_h = refs[5:13]
    outs_h, refs = refs[13:27], refs[27:]
    halo, refs = refs[: reach + 1], refs[reach + 1 :]
    ct, gain_a, order, cos_ref, sin_ref = refs[:5]
    outs, refs = refs[5:19], refs[19:]
    wq, wk, wv, wo, wg, wu, wd, act_s, slope_s, hid_s, ao_ref, gain_b, sems = refs
    place, core = lax.axis_index("seq"), lax.axis_index("fsdp")
    traffic = Traffic(sems)
    waits = {}
    _, _, pack_row, column, cols = layout[7][0]
    gain_far = pack_h.at[pack_row : pack_row + 16, column : column + cols]
    waits["halo"] = traffic.fetch(list(zip(halo_h, halo)))
    waits["halo"] += traffic.fetch([(gains_h, gain_a), (gain_far, gain_b)])
    waits["kv"] = traffic.halves(core, wk_a, pack_h, layout[1], wk)
    waits["kv"] += traffic.halves(core, wv_a, pack_h, layout[2], wv)
    waits["kv"] += traffic.fetch([(cos_h, cos_ref), (sin_h, sin_ref)])
    waits["query"] = traffic.halves(core, wq_a, pack_h, layout[0], wq)
    waits["out"] = traffic.halves(core, wo_a, pack_h, layout[5], wo)
    waits["gate"] = traffic.halves(core, wg_a, pack_h, layout[3], wg)
    waits["gate"] += traffic.halves(core, wu_a, pack_h, layout[4], wu)
    waits["down"] = traffic.halves(core, wd_a, pack_h, layout[6], wd)
    waits["rest"] = traffic.fetch([(ct_h, ct), (order_h, order)])

    def ready(name):
        wait(waits[name])

    attention(
        reach,
        place,
        halo,
        lambda: all_gains(core, gain_a, gain_b),
        cos_ref,
        sin_ref,
        wq,
        wk,
        wv,
        (*outs[:7], ao_ref),
        ready,
    )
    for source, target in zip(outs[:7], outs_h[:7]):
        traffic.emit(source, target)
    mixed_out, dx_out, dao_out, dg_out, keep, send, gains_out = outs[7:]
    rows, width = ct.shape
    gains = all_gains(core, gain_a, gain_b)
    gains_out[...] = gains
    size2 = gains.shape[1] - 4 * width
    ff = wg.shape[1]
    base = width + size2
    g_pa = gains[:, base : base + width]
    g_pf = gains[:, base + width : base + 2 * width]
    g_pff = gains[:, base + 2 * width :]
    x = halo[reach][:rows, :].astype(F32)
    ready("out")
    ya = mm(ao_ref[...], wo[...])
    inv_a = inverse_rms(ya)
    hat_a = ya * inv_a
    x2 = x + hat_a * g_pa
    inv_f = inverse_rms(x2)
    hat_f = x2 * inv_f
    n2 = (hat_f * g_pf).astype(BF16)
    ready("gate")
    ready("down")
    ready("rest")
    c = ct[...].astype(F32)
    part = 512
    (at_gate, at_up, at_df, at_dya, at_hid, at_ao, at_n2), end = pair_columns(
        width, ff, ao_ref.shape[1]
    )
    keep_h, send_h = outs_h[11:13]

    def sent(begin, stop):
        for ref, target in ((send, send_h), (keep, keep_h)):
            traffic.emit(ref.at[:, begin:stop], target.at[:, begin:stop])

    n2_owned = mm_nt(n2, row_order(order, width, place, core)).astype(BF16)
    half = n2_owned.shape[1] // 2
    keep[:, at_n2:end] = n2_owned[:, :half]
    send[:, at_n2:end] = n2_owned[:, half:]
    store_halves(keep, send, at_ao, ao_ref, ao_ref.shape[1] // 32, core)
    sent(at_ao, end)
    root = math.sqrt(2.0 / math.pi)
    f = jnp.zeros((rows, width), F32)
    for at in range(0, ff, part):
        cols = slice(at, at + part)
        gate = mm(n2, wg[:, cols])
        up = mm(n2, wu[:, cols])
        t = jnp.tanh(root * (gate + 0.044715 * (gate * gate * gate)))
        act = 0.5 * gate * (1.0 + t)
        slope = 0.5 * (1.0 + t) + 0.5 * gate * (1.0 - t * t) * (
            root * (1.0 + 3.0 * 0.044715 * (gate * gate))
        )
        act_s[:, cols] = act
        slope_s[:, cols] = up * slope
        hid = (act * up).astype(BF16)
        hid_s[:, cols] = hid
        f = f + mm(hid, wd[cols, :])
    store_halves(keep, send, at_hid, hid_s, ff // 32, core)
    sent(at_hid, at_ao)
    inv_d = inverse_rms(f)
    hat_d = f * inv_d
    mixed_out[...] = (x2 + hat_d * g_pff).astype(BF16)
    traffic.emit(mixed_out, outs_h[7])
    df = norm_back(hat_d, inv_d, g_pff, c).astype(BF16)
    for ref in (send, keep):
        ref[:, at_df : at_df + width] = df
    sent(at_df, at_df + width)
    dn2 = jnp.zeros((rows, width), F32)
    for at in range(0, ff, part):
        cols = slice(at, at + part)
        dhid = mm_nt(df, wd[cols, :])
        dgate = (dhid * slope_s[:, cols]).astype(BF16)
        dup = (dhid * act_s[:, cols]).astype(BF16)
        for ref in (send, keep):
            ref[:, at_gate + at : at_gate + at + part] = dgate
            ref[:, at_up + at : at_up + at + part] = dup
        sent(at_gate + at, at_gate + at + part)
        sent(at_up + at, at_up + at + part)
        dn2 = dn2 + mm_nt(dgate, wg[:, cols]) + mm_nt(dup, wu[:, cols])
    dx2 = c + norm_back(hat_f, inv_f, g_pf, dn2)
    dya = norm_back(hat_a, inv_a, g_pa, dx2).astype(BF16)
    for ref in (send, keep):
        ref[:, at_dya : at_dya + width] = dya
    sent(at_dya, at_dya + width)
    dao_out[...] = mm_nt(dya, wo[...]).astype(BF16)
    traffic.emit(dao_out, outs_h[9])
    dx_out[...] = dx2
    traffic.emit(dx_out, outs_h[8])
    dg_out[:, :width] = jnp.sum(dx2 * hat_a, axis=0, keepdims=True)
    dg_out[:, width : 2 * width] = jnp.sum(dn2 * hat_f, axis=0, keepdims=True)
    dg_out[:, 2 * width :] = jnp.sum(c * hat_d, axis=0, keepdims=True)
    traffic.emit(dg_out, outs_h[10])
    traffic.emit(gains_out, outs_h[13])
    traffic.finish()


def put(xk, xs, first, plane, at, value):
    x_bit, y_bit = plane & 1, plane >> 1
    lead, other = (x_bit, y_bit) if first == "x" else (y_bit, x_bit)
    ref = xs if lead else xk
    ref[other, at : at + value.shape[0], :] = value


def grads_kernel(width, ff, attn, *refs):
    sources, outs_h, outs = refs[:2], refs[3:9], refs[9:15]
    gk, gs, uk, us, dk, ds = outs
    both, prod_s, sems = refs[15:]
    traffic = Traffic(sems)
    place = lax.axis_index("seq")
    (at_gate, at_up, at_df, at_dya, at_hid, at_ao, at_n2), end = pair_columns(width, ff, attn)

    def sent(ref):
        traffic.emit(ref, outs_h[[r is ref for r in outs].index(True)])

    def fetch(begin, stop):
        return traffic.fetch(
            (source.at[:, begin:stop], both.at[side * LANES : (side + 1) * LANES, begin:stop])
            for side, source in enumerate(sources)
        )

    gate_w = fetch(at_n2, end) + fetch(at_gate, at_up)
    up_w = fetch(at_up, at_df)
    rest_w = fetch(at_df, at_n2)
    per = width // 2 // XY
    for copies, base, (keep, send), first in (
        (gate_w, at_gate, (gk, gs), "x"),
        (up_w, at_up, (uk, us), "y"),
    ):
        wait(copies)
        for col in range(0, ff, 512):
            right = both[:, base + col : base + col + 512]
            out = mm_tn(both[:, at_n2:end], right).astype(BF16)
            for plane in range(XY):
                for b in range(4):
                    put(
                        keep,
                        send,
                        first,
                        plane,
                        (col // LANES + b) * per,
                        out[plane * per : (plane + 1) * per, b * LANES : (b + 1) * LANES],
                    )
        sent(send)
        sent(keep)
    wait(rest_w)
    row = 0
    for at_left, at_right, count in ((at_hid, at_df, ff // 2), (at_ao, at_dya, attn // 2)):
        left, right = both[:, at_left : at_left + count], both[:, at_right : at_right + width]
        prod_s[:count, :] = mm_tn(left, right)
        unit = count // (XY * LINE)
        for plane in range(XY):
            for line in range(LINE):
                whose = (place ^ (line * XY + plane)) * unit
                block = prod_s[pl.ds(pl.multiple_of(whose, unit), unit), :].astype(BF16)
                ref = ds if line & 1 else dk
                chunk = (plane >> 1) * 4 + (plane & 1) * 2 + (line >> 1)
                for b in range(width // LANES):
                    ref[chunk, row + b * unit : row + (b + 1) * unit, :] = block[
                        :, b * LANES : (b + 1) * LANES
                    ]
        row += width // LANES * unit
    sent(ds)
    sent(dk)
    traffic.finish()


def heads_kernel(*refs):
    count = 9
    ins_h, outs_h, refs = refs[:count], refs[count : count + 4], refs[count + 4 :]
    ins, outs, sems = refs[:count], refs[count : count + 4], refs[-1]
    gains, cos_ref, sin_ref, qraw_ref, q_ref, k_ref, v_ref, dao_ref, p_ref = ins
    dqr, dkr, dv_out, dgq_out = outs
    traffic = Traffic(sems)
    heads = p_ref.shape[0]
    first = traffic.fetch([(ins_h[n], ins[n]) for n in (7, 6, 5)])
    p_w = [traffic.start(ins_h[8].at[0], p_ref.at[0])]
    second = traffic.fetch([(ins_h[n], ins[n]) for n in range(5)])
    p_w += [traffic.start(ins_h[8].at[h], p_ref.at[h]) for h in range(1, heads)]
    wait(first)
    rows, size = q_ref.shape[0], k_ref.shape[1]
    keys = k_ref.shape[0]
    width = gains.shape[1] // 4 - size // 2
    scale = size ** (-0.5)
    k, v = k_ref[...], v_ref[...]
    dk = jnp.zeros((keys, size), F32)
    dv = jnp.zeros((keys, size), F32)
    dgq = jnp.zeros((1, size), F32)
    for h in range(heads):
        cols = slice(h * size, (h + 1) * size)
        p_w[h].wait()
        p = p_ref[h]
        dao = dao_ref[:, cols]
        dp = mm_nt(dao, v)
        ds = (p * (dp - jnp.sum(p * dp, axis=-1, keepdims=True))).astype(BF16)
        dv = dv + mm_tn(p.astype(BF16), dao)
        if h == 0:
            wait(second)
            g_q = gains[:, width : width + size]
            cos_own, sin_own = cos_ref[keys - rows :, :], sin_ref[keys - rows :, :]
        dk = dk + mm_tn(ds, q_ref[:, cols])
        dq = turn_bwd(mm(ds, k) * scale, cos_own, sin_own)
        qraw = qraw_ref[:, cols]
        inv = inverse_rms(qraw)
        hat = qraw * inv
        dgq = dgq + jnp.sum(dq * hat, axis=0, keepdims=True)
        dqr[:, cols] = norm_back(hat, inv, g_q, dq).astype(BF16)
    dkr[...] = turn_bwd(dk, cos_ref[...], sin_ref[...])
    dv_out[...] = dv.astype(BF16)
    dgq_out[...] = dgq
    for source, target in zip(outs, outs_h):
        traffic.emit(source, target)
    traffic.finish()


def back_kernel(reach, layout, *refs):
    count = reach + 11
    ins_h, refs = refs[:count], refs[count:]
    _, wq_a, wk_a, wv_a, pack_h = refs[:5]
    outs_h, refs = refs[5:9], refs[9:]
    ins, refs = refs[:count], refs[count:]
    halo = ins[: reach + 1]
    gains, order, scale_order, dg_post, dgq, n1_ref, kraw_ref, dkr, dqr, dv_ref = ins[reach + 1 :]
    outs = keep, send, dn1_own, dn1_far = refs[:4]
    wq, wk, wv, dkv_s, sems = refs[4:]
    place, core = lax.axis_index("seq"), lax.axis_index("fsdp")
    traffic = Traffic(sems)
    first = traffic.fetch([(ins_h[n], ins[n]) for n in (reach + 2, reach + 6)])
    second = traffic.fetch([(ins_h[n], ins[n]) for n in range(reach + 7, count)])
    second += traffic.fetch([(ins_h[reach + 1], ins[reach + 1])])
    copies = traffic.fetch([(ins_h[n], ins[n]) for n in range(reach + 3, reach + 6)])
    copies += traffic.fetch(list(zip(ins_h[: reach + 1], halo)))
    for n, (mine, full) in enumerate(((wq_a, wq), (wk_a, wk), (wv_a, wv))):
        copies += traffic.halves(core, mine, pack_h, layout[n], full)
    rows = halo[0].shape[0] - SEG_ROWS
    width = n1_ref.shape[1]
    size = kraw_ref.shape[1]
    wait(first)
    perm = row_order(order, width, place, core)
    n1_t = mm_nt(perm, n1_ref[...]).astype(BF16)
    wait(second)
    g_k = gains[:, width + size : width + 2 * size]
    kraw = kraw_ref[...]
    inv = inverse_rms(kraw)
    hat = kraw * inv
    dk = dkr[...]
    dgk = jnp.sum(dk * hat, axis=0, keepdims=True)
    dkv_s[:, :size] = norm_back(hat, inv, g_k, dk).astype(BF16)
    dkv_s[:, size:] = dv_ref[...]
    half = width // 2
    per = half // XY
    attn = dqr.shape[1]
    wait(copies)
    dgi = jnp.zeros((1, width), F32)
    for block in range(reach + 1):
        span = slice(block * rows, (block + 1) * rows)
        dn1 = mm_nt(dkv_s[span, :size], wk[...]) + mm_nt(dkv_s[span, size:], wv[...])
        if block == reach:
            dn1 = dn1 + mm_nt(dqr[...], wq[...])
        x = halo[block][:rows, :].astype(F32)
        dgi = dgi + jnp.sum(dn1 * (x * inverse_rms(x)), axis=0, keepdims=True)
        if block == reach:
            dn1_own[...] = dn1
        else:
            bits = (place ^ (place - (reach - block))) & (XY - 1)
            low = dn1.astype(BF16)
            for b in range(width // LANES):
                dn1_far[bits, b * rows : (b + 1) * rows, :] = low[:, b * LANES : (b + 1) * LANES]
    scales = owners_rows(jnp.concatenate([dgi, dgq[...], dgk, dg_post[...]], axis=1))
    owner = scale_order[:, :1] ^ (place * 2 + core)
    mine = scale_order[:, 1:2] * 1024 + (owner & 3) * 8 + (owner >> 2)
    columns = lax.broadcasted_iota(jnp.int32, (mine.shape[0], 2 * XY * LINE), 1)
    scales = mm(jnp.where(columns == mine, 1.0, 0.0).astype(BF16), scales).astype(BF16)
    rows_each = scales.shape[0] // (2 * XY)
    for ref, begin, group in ((send, half, XY), (keep, 0, 0)):
        left = n1_t[begin : begin + half]
        own = left[:, reach * rows :]
        at = 0
        for value, left_part, total in (
            (dqr, own, attn),
            (dkv_s, left, 2 * size),
        ):
            for col in range(0, total, 512):
                out = mm(left_part, value[:, col : col + 512]).astype(BF16)
                for plane in range(XY):
                    for b in range(4):
                        ref[
                            plane,
                            at + (col // LANES + b) * per : at + (col // LANES + b + 1) * per,
                            :,
                        ] = out[plane * per : (plane + 1) * per, b * LANES : (b + 1) * LANES]
            at += total // LANES * per
        for plane in range(XY):
            row = (group + plane) * rows_each
            ref[plane, at : at + rows_each, :] = scales[row : row + rows_each]
        traffic.emit(ref, outs_h[0 if ref is keep else 1])
    for n in (3, 2):
        traffic.emit(outs[n], outs_h[n])
    traffic.finish()


def owners_rows(line):
    pieces = [line[:, r * LANES : (r + 1) * LANES] for r in range(line.shape[1] // LANES)]
    first, second, third = (jnp.concatenate(pieces[n::3], axis=0) for n in range(3))
    lane = lax.broadcasted_iota(jnp.int32, first.shape, 1)
    quarter = LANES // 4
    groups = [
        first,
        jnp.where(
            lane < quarter, pltpu.roll(first, quarter, 1), pltpu.roll(second, quarter, 1)
        ),
        jnp.where(
            lane < 2 * quarter,
            pltpu.roll(second, 2 * quarter, 1),
            pltpu.roll(third, 2 * quarter, 1),
        ),
        pltpu.roll(third, 3 * quarter, 1),
    ]
    return jnp.concatenate(groups, axis=0).astype(BF16)


def collect_kernel(skip, *refs):
    own_h, far_h, *near = refs[: XY + 1]
    total_out, below_out, own, far, sems = refs[XY + 3 :]
    traffic = Traffic(sems)
    wait(traffic.fetch([(own_h, own), (far_h.at[0], far)]))
    place = lax.axis_index("seq") & (XY - 1)
    rows = own.shape[0]
    total = own[...]
    below = far[...].astype(F32)
    for bits, ref in enumerate(near, 1):
        part = ref[skip:, :].astype(F32)
        mine = (place ^ bits) > place
        below = below + jnp.where(mine, 0.0, part)
        lanes = [part[b * rows : (b + 1) * rows] for b in range(part.shape[0] // rows)]
        total = total + jnp.where(mine, jnp.concatenate(lanes, axis=1), 0.0)
    total_out[...] = total
    below_out[...] = below.astype(BF16)


def finish_kernel(*refs):
    ins_h, (dn1, above), out_h, ins = refs[:3], refs[3:5], refs[5], refs[6:9]
    out, sems = refs[9:]
    traffic = Traffic(sems)
    wait(traffic.fetch(list(zip(ins_h, ins))))
    tok, gains, dx = ins
    rows, width = dx.shape
    lanes = [above[b * rows : (b + 1) * rows, :] for b in range(width // LANES)]
    total = dn1[...] + jnp.concatenate(lanes, axis=1).astype(F32)
    x = tok[:rows, :].astype(F32)
    inv = inverse_rms(x)
    out[...] = dx[...] + norm_back(x * inv, inv, gains[:, :width], total)
    traffic.emit(out, out_h)
    traffic.finish()


def line_split_kernel(groups, entries, extra, direct, after, *refs):
    count = sum(groups)
    ins, (keep, send, split, *sums) = refs[:count], refs[count + after :]
    at = 0
    for number, total in zip(groups, sums):
        value = ins[at][...].astype(F32)
        for other in ins[at + 1 : at + number]:
            value = value + other[: value.shape[0], :].astype(F32)
        total[...] = value
        at += number
    at = 0
    for group, row, blocks, unit in entries:
        for b in range(blocks):
            for position in range(LINE):
                begin = row + (b * LINE + position) * unit
                split[position, at : at + unit, :] = sums[group][begin : begin + unit, :]
            at += unit
    if extra:
        group, row = extra
        for position in range(LINE):
            one = sums[group][row + position : row + position + 1, :]
            split[position, at : at + 16, :] = jnp.broadcast_to(one, (16, LANES))
    order = ((keep, (0,)), (send, (1, 2, 3))) if direct else ((keep, (0, 2)), (send, (1, 3)))
    for ref, positions in order:
        for n, position in enumerate(positions):
            ref[n] = split[position].astype(ref.dtype)


def join_kernel(parts, entries, extra, *refs):
    count = len(entries) + extra
    ins, outs_h, outs = refs[:parts], refs[parts : parts + count], refs[parts + count :][:count]
    sum_s, sems = refs[parts + 2 * count :]
    traffic = Traffic(sems)
    total = ins[0][...].astype(F32)
    for part in ins[1:]:
        total = total + part[...].astype(F32)
    sum_s[...] = total
    at = 0
    for (blocks, unit), out in zip(entries, outs):
        for b in range(blocks):
            out[pl.ds(b, unit, stride=blocks), :] = sum_s[at : at + unit, :]
            at += unit
    if extra:
        outs[-1][...] = sum_s[at : at + 8, :]
    for out, out_h in zip(outs, outs_h):
        traffic.emit(out, out_h)
    traffic.finish()


def call(kernel, fetched, others, outs, scratch, copies, limit=61):
    hbm = pl.BlockSpec(memory_space=pl.ANY)
    return pl.pallas_call(
        kernel,
        out_shape=outs,
        in_specs=[hbm] * (len(fetched) + len(others)),
        out_specs=[hbm] * len(outs),
        scratch_shapes=[pltpu.VMEM(a.shape, a.dtype) for a in (*fetched, *outs)]
        + scratch
        + [pltpu.SemaphoreType.DMA((copies,))],
        compiler_params=pltpu.CompilerParams(vmem_limit_bytes=limit * MIB),
        cost_estimate=pl.CostEstimate(flops=0, bytes_accessed=0, transcendentals=0),
    )(*fetched, *others)


def shape(dims, dtype):
    return jax.ShapeDtypeStruct(dims, dtype)


vmem = pl.BlockSpec(memory_space=pltpu.VMEM)
hbm = pl.BlockSpec(memory_space=pl.ANY)


def fast(
    tokens,
    segments,
    positions,
    w_query,
    w_key,
    w_value,
    w_out,
    w_gate,
    w_up,
    w_down,
    norm_gains,
    cotangent,
):
    rows, width = tokens.shape[1:]
    size = w_key.shape[1]
    attn = w_query.shape[1]
    heads = attn // size
    ff = w_gate.shape[1]
    count = norm_gains.shape[0] * 2
    reach = (WINDOW - 1 + rows - 1) // rows
    keys = (reach + 1) * rows
    place = lax.axis_index("seq")
    core = lax.axis_index("fsdp")

    def partner(value):
        return lax.ppermute(value, "fsdp", [(0, 1), (1, 0)])

    def across(value, bits):
        return lax.ppermute(value, "seq", [(i, i ^ bits) for i in range(XY * LINE)])

    gains_own = norm_gains.reshape(-1, LANES)
    weights = (w_query, w_key, w_value, w_gate, w_up, w_out, w_down)
    layout, columns = pack_layout(
        width // 2,
        [w.shape[1] for w in weights[:5]],
        [w.shape for w in weights[5:]] + [(16, LANES)],
    )
    tok, pack = pl.pallas_call(
        functools.partial(prepare_kernel, layout),
        out_shape=[
            shape((rows + SEG_ROWS, width), BF16),
            shape((width // 2, columns), BF16),
        ],
        in_specs=[pl.BlockSpec(memory_space=pl.ANY)] * 10,
        out_specs=[pl.BlockSpec(memory_space=pl.ANY)] * 2,
        scratch_shapes=[pltpu.VMEM((rows, width), BF16), pltpu.VMEM((1, rows), jnp.int32)]
        + [pltpu.VMEM(w.shape, BF16) for w in (*weights, gains_own)]
        + [
            pltpu.VMEM((rows + SEG_ROWS, width), BF16),
            pltpu.VMEM((16, LANES), BF16),
            pltpu.SemaphoreType.DMA((40,)),
        ],
        compiler_params=pltpu.CompilerParams(vmem_limit_bytes=61 * MIB),
    )(tokens[0], segments, *weights, gains_own)
    pack_far = partner(pack)
    halo = [shifted(tok, "seq", distance) for distance in range(reach, 0, -1)] + [tok]

    unit = width // (2 * XY * LINE)
    new = np.arange(width) // unit
    core_bit, plane, line = new // (XY * LINE), new // LINE % XY, new % LINE
    owner = (line * XY + plane) * 2 + core_bit
    order = jnp.asarray(np.stack([owner, np.arange(width) % unit], axis=1).astype(np.int32))
    apart = np.full((2, padded(width // 2), 2), [0, 1 << 20])
    apart[:, : width // 2] = np.stack([owner, np.arange(width) % unit], axis=1).reshape(2, -1, 2)
    order_pair = jnp.asarray(apart.reshape(-1, 2).astype(np.int32))
    freq = np.exp(np.arange(size // 2, dtype=np.float64) * (-2.0 * math.log(10000.0) / size))
    turn = np.arange(keys, dtype=np.float64)[:, None] * freq
    cosine = jnp.asarray(np.cos(turn).astype(np.float32))
    sine = jnp.asarray(np.sin(turn).astype(np.float32))

    pair_end = pair_columns(width, ff, attn)[1]
    n1, qraw, q, kraw, k, v, p, mixed, dx, dao, dg_post, mlp_keep, mlp_send, gains = call(
        functools.partial(forward_kernel, reach, layout),
        (*halo, cotangent[0], gains_own, order_pair, cosine, sine),
        (*weights, pack_far),
        [
            shape((keys, width), BF16),
            shape((rows, attn), F32),
            shape((rows, attn), BF16),
            shape((keys, size), F32),
            shape((keys, size), BF16),
            shape((keys, size), BF16),
            shape((heads, rows, keys), F32),
            shape((rows, width), BF16),
            shape((rows, width), F32),
            shape((rows, attn), BF16),
            shape((1, 3 * width), F32),
            shape((rows, pair_end), BF16),
            shape((rows, pair_end), BF16),
            shape((1, count), F32),
        ],
        [
            pltpu.VMEM((width, attn), BF16),
            pltpu.VMEM((width, size), BF16),
            pltpu.VMEM((width, size), BF16),
            pltpu.VMEM((attn, width), BF16),
            pltpu.VMEM((width, ff), BF16),
            pltpu.VMEM((width, ff), BF16),
            pltpu.VMEM((ff, width), BF16),
            pltpu.VMEM((rows, ff), F32),
            pltpu.VMEM((rows, ff), F32),
            pltpu.VMEM((rows, ff), BF16),
            pltpu.VMEM((rows, attn), BF16),
            pltpu.VMEM((16, LANES), BF16),
        ],
        128,
    )
    mlp_recv = partner(mlp_send)

    dqr, dkr, dv, dgq = call(
        heads_kernel,
        (gains, cosine, sine, qraw, q, k, v, dao, p),
        (),
        [
            shape((rows, attn), BF16),
            shape((keys, size), F32),
            shape((keys, size), BF16),
            shape((1, size), F32),
        ],
        [],
        24,
    )

    per_ff = width // 2 // XY * ff // LANES
    per_down = ff // 2 // XY * width // LANES
    per_out = attn // 2 // XY * width // LANES
    gk, gs, uk, us, dk, ds = call(
        functools.partial(grads_kernel, width, ff, attn),
        (),
        (mlp_keep, mlp_recv, dgq),
        [shape((2, per_ff, LANES), BF16)] * 4
        + [shape((8, (per_down + per_out) // LINE, LANES), BF16)] * 2,
        [
            pltpu.VMEM((2 * rows, pair_end), BF16),
            pltpu.VMEM((ff // 2, width), F32),
        ],
        16,
    )

    per_q = width // 2 // XY * attn // LANES
    per_k = width // 2 // XY * size // LANES
    per_back = per_q + 2 * per_k
    share = count // (2 * XY * LINE)
    new = np.arange(2 * XY * 16)
    core_bit, plane, line = new // (XY * 16), new // 16 % XY, new % 16
    owner = (line % LINE * XY + plane) * 2 + core_bit
    scale_order = jnp.asarray(np.stack([owner, line // LINE], axis=1).astype(np.int32))
    back_keep, back_send, dn1_own, dn1_far = call(
        functools.partial(back_kernel, reach, layout),
        (*halo, gains, order, scale_order, dg_post, dgq, n1, kraw, dkr, dqr, dv),
        (gk, *weights[:3], pack_far),
        [
            shape((XY, per_back + 16, LANES), BF16),
            shape((XY, per_back + 16, LANES), BF16),
            shape((rows, width), F32),
            shape((XY, rows * width // LANES, LANES), BF16),
        ],
        [
            pltpu.VMEM((width, attn), BF16),
            pltpu.VMEM((width, size), BF16),
            pltpu.VMEM((width, size), BF16),
            pltpu.VMEM((keys, 2 * size), BF16),
        ],
        64,
    )
    back_recv = partner(back_send)

    def add(a, b):
        return (a.astype(F32) + b.astype(F32)).astype(BF16)

    def halves(keep, near):
        half = keep.shape[0] // 2
        return add(keep[:half], near[:half]), add(keep[half:], near[half:])

    def step(keep, send, bits):
        return halves(keep, across(send, bits))

    def line_split(groups, entries, extra, direct, after=()):
        part = sum(blocks * unit for _, _, blocks, unit in entries) + (16 if extra else 0)
        stay = 1 if direct else 2
        arrays = [array for g in groups for array in g]
        return pl.pallas_call(
            functools.partial(
                line_split_kernel, [len(g) for g in groups], entries, extra, direct, len(after)
            ),
            out_shape=[shape((n, part, LANES), BF16) for n in (stay, LINE - stay)],
            in_specs=[vmem] * len(arrays) + [hbm] * len(after),
            out_specs=[vmem] * 2,
            scratch_shapes=[pltpu.VMEM((LINE, part, LANES), F32)]
            + [pltpu.VMEM(g[0].shape, F32) for g in groups],
            compiler_params=pltpu.CompilerParams(vmem_limit_bytes=12 * MIB),
            cost_estimate=pl.CostEstimate(flops=0, bytes_accessed=0, transcendentals=0),
        )(*arrays, *after)

    def join(parts, entries, extra=False):
        outs = [shape((blocks * unit, LANES), F32) for blocks, unit in entries]
        if extra:
            outs.append(shape((8, LANES), F32))
        return pl.pallas_call(
            functools.partial(join_kernel, len(parts), entries, int(extra)),
            out_shape=outs,
            in_specs=[vmem] * len(parts),
            out_specs=[hbm] * len(outs),
            scratch_shapes=[pltpu.VMEM(a.shape, a.dtype) for a in outs]
            + [pltpu.VMEM(parts[0].shape, F32), pltpu.SemaphoreType.DMA((len(outs),))],
            compiler_params=pltpu.CompilerParams(vmem_limit_bytes=12 * MIB),
            cost_estimate=pl.CostEstimate(flops=0, bytes_accessed=0, transcendentals=0),
        )(*parts)

    wide, narrow = ff // LANES, width // LANES
    unit_out, unit_down = attn // 32, ff // 32

    planes = [add(back_keep[n], back_recv[n]) for n in range(XY)]
    planes = [planes[0]] + [
        across(jnp.concatenate([planes[n], dn1_far[n]]), n) for n in range(1, XY)
    ]

    gate_0, gate_1 = step(gk, gs, 1)
    up_0, up_1 = step(uk, us, 2)
    gate_2, up_2 = across(gate_1, 2), across(up_1, 1)
    flat = lambda value: value.reshape(value.shape[1:])
    keep, send = line_split(
        ((flat(gate_0), flat(gate_2)), (flat(up_0), flat(up_2))),
        ((0, 0, wide, unit), (1, 0, wide, unit)),
        None,
        False,
    )
    mlp_0, mlp_1 = step(keep, send, XY)
    own_gate, own_up = join(
        (flat(mlp_0), flat(across(mlp_1, 2 * XY))), ((wide, unit), (wide, unit))
    )
    down_0, down_1 = step(dk, ds, XY)
    down_0, down_1 = step(down_0, down_1, 2)
    down_2, down_3 = step(down_0, down_1, 1)
    own_down, own_out = join(
        (flat(down_2), flat(across(down_3, 2 * XY))), ((narrow, unit_down), (narrow, unit_out))
    )

    far_shape = (rows * width // LANES, LANES)
    dn1, below = pl.pallas_call(
        functools.partial(collect_kernel, per_back + 16),
        out_shape=[shape((rows, width), F32), shape(far_shape, BF16)],
        in_specs=[hbm] * 2 + [vmem] * (XY - 1) + [hbm] * 2,
        out_specs=[vmem] * 2,
        scratch_shapes=[
            pltpu.VMEM((rows, width), F32),
            pltpu.VMEM(far_shape, BF16),
            pltpu.SemaphoreType.DMA((2,)),
        ],
        compiler_params=pltpu.CompilerParams(vmem_limit_bytes=12 * MIB),
        cost_estimate=pl.CostEstimate(flops=0, bytes_accessed=0, transcendentals=0),
    )(dn1_own, dn1_far, *planes[1:], own_gate, own_down)
    keep, send = line_split(
        (planes,),
        (
            (0, 0, attn // LANES, unit),
            (0, per_q, size // LANES, unit),
            (0, per_q + per_k, size // LANES, unit),
        ),
        (0, per_back),
        True,
        (below,),
    )
    own_query, own_key, own_value, own_gains = join(
        (flat(keep), *[across(send[n], (n + 1) * XY) for n in range(LINE - 1)]),
        ((attn // LANES, unit), (size // LANES, unit), (size // LANES, unit)),
        True,
    )

    input_grad = pl.pallas_call(
        finish_kernel,
        out_shape=shape((rows, width), F32),
        in_specs=[hbm] * 3 + [vmem] * 2,
        out_specs=hbm,
        scratch_shapes=[pltpu.VMEM(a.shape, a.dtype) for a in (tok, gains, dx, dx)]
        + [pltpu.SemaphoreType.DMA((4,))],
        compiler_params=pltpu.CompilerParams(vmem_limit_bytes=12 * MIB),
        cost_estimate=pl.CostEstimate(flops=0, bytes_accessed=0, transcendentals=0),
    )(tok, gains, dx, dn1, shifted(below, "seq", -XY))
    return (
        mixed[None],
        input_grad[None],
        own_query.reshape(-1),
        own_key.reshape(-1),
        own_value.reshape(-1),
        own_out.reshape(-1),
        own_gate.reshape(-1),
        own_up.reshape(-1),
        own_down.reshape(-1),
        own_gains[0, :share],
    )


def solution(mesh):
    placed = (
        P("fsdp", "seq", None),
        P("fsdp", "seq"),
        P("fsdp", "seq"),
        P("fsdp", None),
        P("fsdp", None),
        P("fsdp", None),
        P("fsdp", None),
        P("fsdp", None),
        P("fsdp", None),
        P("fsdp", None),
        P("fsdp"),
        P("fsdp", "seq", None),
    )
    small = mesh.shape["seq"] == XY * LINE and mesh.shape["fsdp"] == 2
    return jax.shard_map(
        fast if small else general,
        mesh=mesh,
        in_specs=placed,
        out_specs=(
            P("fsdp", "seq", None),
            P("fsdp", "seq", None),
            P(("seq", "fsdp")),
            P(("seq", "fsdp")),
            P(("seq", "fsdp")),
            P(("seq", "fsdp")),
            P(("seq", "fsdp")),
            P(("seq", "fsdp")),
            P(("seq", "fsdp")),
            P(("seq", "fsdp")),
        ),
        check_vma=False,
    )
```

```python
import functools
import math

import jax
import jax.numpy as jnp
import numpy as np
from jax import lax
from jax.experimental import pallas as pl
from jax.experimental.pallas import tpu as pltpu
from jax.sharding import PartitionSpec as P

WINDOW = 512
EPS = 1e-06
LANES = 128
SEG_ROWS = 16
F32 = jnp.float32
BF16 = jnp.bfloat16
MIB = 1 << 20


def shifted(x, axis, by):
    peers = lax.axis_size(axis)
    pairs = [(i, i + by) for i in range(peers) if 0 <= i + by < peers]
    return lax.ppermute(x, axis, pairs)


def norm_rows(value, gain):
    return value * lax.rsqrt(jnp.mean(value * value, axis=-1, keepdims=True) + EPS) * gain


def rotate(value, cosine, sine):
    half = value.shape[-1] // 2
    first = value[..., :half]
    second = value[..., half:]
    return jnp.concatenate(
        [first * cosine - second * sine, second * cosine + first * sine], axis=-1
    )


def angles(positions, size):
    freq = jnp.exp(jnp.arange(size // 2, dtype=jnp.float32) * (-2.0 * math.log(10000.0) / size))
    turn = positions.astype(jnp.float32)[..., None] * freq
    return (jnp.cos(turn), jnp.sin(turn))


def product(form, left, right):
    return jnp.einsum(form, left, right, preferred_element_type=jnp.float32)


def general(
    tokens,
    segments,
    positions,
    w_query,
    w_key,
    w_value,
    w_out,
    w_gate,
    w_up,
    w_down,
    norm_gains,
    cotangent,
):
    tok_rows = tokens.shape[1]
    width = tokens.shape[2]
    head_size = w_key.shape[1]
    head_count = w_query.shape[1] // head_size
    reach = (WINDOW - 1 + tok_rows - 1) // tok_rows
    scale = head_size ** (-0.5)
    gathered = tuple(
        lax.all_gather(w, "fsdp", axis=0, tiled=True)
        for w in (w_query, w_key, w_value, w_out, w_gate, w_up, w_down, norm_gains)
    )
    query_full, key_full, value_full, out_full, gate_full, up_full, down_full, gains_full = gathered
    gains = gains_full.astype(jnp.float32)
    gain_in = gains[:width]
    gain_q = gains[width : width + head_size]
    gain_k = gains[width + head_size : width + 2 * head_size]
    gain_pa = gains[width + 2 * head_size : 2 * width + 2 * head_size]
    gain_pf = gains[2 * width + 2 * head_size : 3 * width + 2 * head_size]
    gain_pff = gains[3 * width + 2 * head_size :]
    hidden_in = tokens[0].astype(jnp.float32)
    segment = segments[0]
    cosine, sine = angles(positions[0], head_size)
    normed, first_back = jax.vjp(norm_rows, hidden_in, gain_in)
    normed_low = normed.astype(jnp.bfloat16)
    query_raw = jnp.dot(normed_low, query_full, preferred_element_type=jnp.float32)
    key_raw = jnp.dot(normed_low, key_full, preferred_element_type=jnp.float32)
    value_low = jnp.dot(normed_low, value_full, preferred_element_type=jnp.float32).astype(
        jnp.bfloat16
    )

    def turn(query, key, gain_query, gain_key):
        query = norm_rows(query.reshape(tok_rows, head_count, head_size), gain_query)
        query = rotate(query, cosine[:, None, :], sine[:, None, :]) * scale
        key = rotate(norm_rows(key, gain_key), cosine, sine)
        return (query, key)

    (query_rot, key_rot), turn_back = jax.vjp(turn, query_raw, key_raw, gain_q, gain_k)
    query_low = query_rot.astype(jnp.bfloat16)
    packed = jnp.concatenate([key_rot.astype(jnp.bfloat16), value_low], axis=1)
    pieces = [packed]
    seg_pieces = [segment]
    for distance in range(1, reach + 1):
        far_pack, far_seg = shifted((packed, segment), "seq", distance)
        pieces.insert(0, far_pack)
        seg_pieces.insert(0, far_seg)
    keys_all = jnp.concatenate(pieces, axis=0)
    seg_all = jnp.concatenate(seg_pieces, axis=0)
    key_part = keys_all[:, :head_size]
    value_part = keys_all[:, head_size:]
    place = lax.axis_index("seq")
    query_index = place * tok_rows + jnp.arange(tok_rows, dtype=jnp.int32)
    key_index = (place - reach) * tok_rows + jnp.arange((reach + 1) * tok_rows, dtype=jnp.int32)
    spacing = query_index[:, None] - key_index[None, :]
    allowed = (
        (segment[:, None] == seg_all[None, :])
        & (spacing >= 0)
        & (spacing < WINDOW)
        & (key_index[None, :] >= 0)
    )
    scores = product("qhd,kd->hqk", query_low, key_part)
    masked = jnp.where(allowed[None], scores, -1e30)
    top = jnp.max(masked, axis=-1, keepdims=True)
    expd = jnp.exp(masked - top)
    total = jnp.sum(expd, axis=-1, keepdims=True)
    probs_low = (expd / total).astype(jnp.bfloat16)
    log_total = top + jnp.log(total)
    mixed_heads = (
        product("hqk,kd->qhd", probs_low, value_part)
        .reshape(tok_rows, head_count * head_size)
        .astype(jnp.bfloat16)
    )
    attn_out = jnp.dot(mixed_heads, out_full, preferred_element_type=jnp.float32)

    def middle(resid, branch, gain_a, gain_b):
        after = resid + norm_rows(branch, gain_a)
        return (after, norm_rows(after, gain_b))

    (after, normed_ff), middle_back = jax.vjp(middle, hidden_in, attn_out, gain_pa, gain_pf)
    ff_low = normed_ff.astype(jnp.bfloat16)
    gate = jnp.dot(ff_low, gate_full, preferred_element_type=jnp.float32)
    up_value = jnp.dot(ff_low, up_full, preferred_element_type=jnp.float32)

    def mixer(gate_in, up_in):
        return jax.nn.gelu(gate_in, approximate=True) * up_in

    inner, mixer_back = jax.vjp(mixer, gate, up_value)
    inner_low = inner.astype(jnp.bfloat16)
    down = jnp.dot(inner_low, down_full, preferred_element_type=jnp.float32)

    def finish(resid, branch, gain):
        return resid + norm_rows(branch, gain)

    result, finish_back = jax.vjp(finish, after, down, gain_pff)
    grad_result = cotangent[0].astype(jnp.float32)
    grad_after, grad_down, grad_gpff = finish_back(grad_result)
    down_grad_low = grad_down.astype(jnp.bfloat16)
    grad_w_down = product("tf,td->fd", inner_low, down_grad_low)
    grad_inner = product("td,fd->tf", down_grad_low, down_full)
    grad_gate, grad_upv = mixer_back(grad_inner)
    gate_grad_low = grad_gate.astype(jnp.bfloat16)
    up_grad_low = grad_upv.astype(jnp.bfloat16)
    grad_w_gate = product("td,tf->df", ff_low, gate_grad_low)
    grad_w_up = product("td,tf->df", ff_low, up_grad_low)
    grad_normed_ff = product("tf,df->td", gate_grad_low, gate_full) + product(
        "tf,df->td", up_grad_low, up_full
    )
    grad_resid, grad_branch, grad_gpa, grad_gpf = middle_back((grad_after, grad_normed_ff))
    branch_grad_low = grad_branch.astype(jnp.bfloat16)
    grad_w_out = product("ta,td->ad", mixed_heads, branch_grad_low)
    grad_heads = (
        product("td,ad->ta", branch_grad_low, out_full)
        .astype(jnp.bfloat16)
        .reshape(tok_rows, head_count, head_size)
    )
    scores_again = product("qhd,kd->hqk", query_low, key_part)
    probs = jnp.exp(jnp.where(allowed[None], scores_again, -1e30) - log_total)
    probs_again = probs.astype(jnp.bfloat16)
    grad_probs = product("qhd,kd->hqk", grad_heads, value_part)
    grad_scores = (
        probs * (grad_probs - jnp.sum(probs * grad_probs, axis=-1, keepdims=True))
    ).astype(jnp.bfloat16)
    grad_query_rot = product("hqk,kd->qhd", grad_scores, key_part)
    grad_keys = product("hqk,qhd->kd", grad_scores, query_low)
    grad_values = product("hqk,qhd->kd", probs_again, grad_heads)
    grad_packed = jnp.concatenate([grad_keys, grad_values], axis=1)
    collected = grad_packed[reach * tok_rows :]
    for distance in range(1, reach + 1):
        begin = (reach - distance) * tok_rows
        collected = collected + shifted(
            grad_packed[begin : begin + tok_rows].astype(jnp.bfloat16), "seq", -distance
        ).astype(jnp.float32)
    grad_key_rot = collected[:, :head_size]
    value_grad_low = collected[:, head_size:].astype(jnp.bfloat16)
    grad_q_raw, grad_k_raw, grad_gq, grad_gk = turn_back((grad_query_rot, grad_key_rot))
    query_grad_low = grad_q_raw.astype(jnp.bfloat16)
    key_grad_low = grad_k_raw.astype(jnp.bfloat16)
    grad_w_query = product("td,te->de", normed_low, query_grad_low)
    grad_w_key = product("td,te->de", normed_low, key_grad_low)
    grad_w_value = product("td,te->de", normed_low, value_grad_low)
    grad_normed = (
        product("te,de->td", query_grad_low, query_full)
        + product("te,de->td", key_grad_low, key_full)
        + product("te,de->td", value_grad_low, value_full)
    )
    grad_in, grad_gin = first_back(grad_normed)
    input_grad = (grad_resid + grad_in)[None]
    grad_gains = jnp.concatenate([grad_gin, grad_gq, grad_gk, grad_gpa, grad_gpf, grad_gpff])
    own = tuple(
        lax.psum_scatter(g.reshape(-1), ("seq", "fsdp"), scatter_dimension=0, tiled=True)
        for g in (
            grad_w_query,
            grad_w_key,
            grad_w_value,
            grad_w_out,
            grad_w_gate,
            grad_w_up,
            grad_w_down,
            grad_gains,
        )
    )
    return (result.astype(jnp.bfloat16)[None], input_grad) + own


XY = 4
LINE = 4


def mm(a, b):
    return lax.dot_general(a, b, (((1,), (0,)), ((), ())), preferred_element_type=F32)


def mm_nt(a, b):
    return lax.dot_general(a, b, (((1,), (1,)), ((), ())), preferred_element_type=F32)


def mm_tn(a, b):
    return lax.dot_general(a, b, (((0,), (0,)), ((), ())), preferred_element_type=F32)


def inverse_rms(x):
    return lax.rsqrt(jnp.mean(x * x, axis=-1, keepdims=True) + EPS)


def norm_back(hat, inv, gain, grad):
    scaled = grad * gain
    return inv * (scaled - hat * jnp.mean(hat * scaled, axis=-1, keepdims=True))


def turn_fwd(x, cosine, sine):
    half = x.shape[1] // 2
    a, b = x[:, :half], x[:, half:]
    return jnp.concatenate([a * cosine - b * sine, b * cosine + a * sine], axis=1)


def turn_bwd(x, cosine, sine):
    half = x.shape[1] // 2
    a, b = x[:, :half], x[:, half:]
    return jnp.concatenate([a * cosine + b * sine, b * cosine - a * sine], axis=1)


def all_gains(core, mine, theirs):
    a = mine[...].astype(F32)
    b = theirs[...].astype(F32)[: a.shape[0]]
    low, high = jnp.where(core == 0, a, b), jnp.where(core == 0, b, a)
    rows = [half[r : r + 1, :] for half in (low, high) for r in range(a.shape[0])]
    return jnp.concatenate(rows, axis=1)


def row_order(table, width, place, core):
    owner = table[:, :1] ^ (place * 2 + core)
    source = owner * (width // (2 * XY * LINE)) + table[:, 1:2]
    ranks = lax.broadcasted_iota(jnp.int32, (table.shape[0], width), 1)
    return jnp.where(ranks == source, 1.0, 0.0).astype(BF16)


class Traffic:
    def __init__(self, sems):
        self.sems = sems
        self.used = 0
        self.pending = []

    def start(self, source, target):
        copy = pltpu.make_async_copy(source, target, self.sems.at[self.used])
        self.used += 1
        copy.start()
        return copy

    def fetch(self, pairs):
        return [self.start(source, target) for source, target in pairs]

    def halves(self, core, mine, pack, pieces, full):
        rows = mine.shape[0]
        begin = pl.multiple_of(core * rows, 16)
        copies = [self.start(mine, full.at[pl.ds(begin, rows)])]
        for row, number, pack_row, column, cols in pieces:
            begin = pl.multiple_of((1 - core) * rows + row, 16)
            source = pack.at[pack_row : pack_row + number, column : column + cols]
            copies.append(self.start(source, full.at[pl.ds(begin, number)]))
        return copies

    def emit(self, source, target):
        self.pending.append(self.start(source, target))

    def finish(self):
        for copy in self.pending:
            copy.wait()


def pack_layout(rows, widths, talls):
    layout, column = [], 0
    for width in widths:
        layout.append([(0, rows, 0, column, width)])
        column += width
    at = 0
    for height, width in talls:
        pieces, done = [], 0
        while done < height:
            take = min(height - done, rows - at % rows)
            pieces.append((done, take, at % rows, column + at // rows * talls[0][1], width))
            done, at = done + take, at + take
        layout.append(pieces)
    return layout, column + -(-at // rows) * talls[0][1]


def prepare_kernel(layout, *refs):
    count = len(layout)
    tok_h, seg_h, *weights_h = refs[: count + 2]
    ext_h, pack_h = refs[count + 2 : count + 4]
    tok, seg, *weights = refs[count + 4 : 2 * count + 6]
    ext, gain_s, sems = refs[2 * count + 6 :]
    traffic = Traffic(sems)
    first = traffic.fetch([(tok_h, tok), (seg_h, seg)])
    rest = traffic.fetch(list(zip(weights_h, weights)))
    wait(first)
    rows, width = tok.shape
    ext[:rows, :] = tok[...]
    ext[rows:, :] = jnp.zeros((SEG_ROWS, width), BF16)
    ids = seg[...].astype(F32)
    ext[rows:, :rows] = jnp.broadcast_to(ids, (SEG_ROWS, rows)).astype(BF16)
    traffic.emit(ext, ext_h)
    for copy, source, pieces in zip(rest, weights, layout):
        copy.wait()
        if source is weights[-1]:
            missing = gain_s.shape[0] - source.shape[0]
            filled = [source[...].astype(F32), jnp.zeros((missing, LANES), F32)]
            gain_s[...] = jnp.concatenate(filled, axis=0).astype(BF16)
            source = gain_s
        for row, number, pack_row, column, cols in pieces:
            traffic.emit(
                source.at[row : row + number, :],
                pack_h.at[pack_row : pack_row + number, column : column + cols],
            )
    traffic.finish()


def wait(copies):
    for copy in copies:
        copy.wait()


def attention(reach, place, halo, gains, cos_ref, sin_ref, wq, wk, wv, outs, ready):
    n1_out, qraw_out, q_out, kraw_out, k_out, v_out, p_out, ao_out = outs
    width = n1_out.shape[1]
    rows = halo[0].shape[0] - SEG_ROWS
    size = k_out.shape[1]
    heads = q_out.shape[1] // size
    scale = size ** (-0.5)
    ready("halo")
    gains = gains()
    g_in = gains[:, :width]
    g_q = gains[:, width : width + size]
    g_k = gains[:, width + size : width + 2 * size]
    for block in range(reach + 1):
        x = halo[block][:rows, :].astype(F32)
        n1_out[block * rows : (block + 1) * rows, :] = (x * inverse_rms(x) * g_in).astype(BF16)
    ready("kv")
    n1 = n1_out[...]
    kraw = mm(n1, wk[...])
    kraw_out[...] = kraw
    k = turn_fwd(kraw * inverse_rms(kraw) * g_k, cos_ref[...], sin_ref[...]).astype(BF16)
    k_out[...] = k
    v = mm(n1, wv[...]).astype(BF16)
    v_out[...] = v
    keys = (reach + 1) * rows
    seg_rows = [halo[b][rows:, :rows].astype(F32)[:1] for b in range(reach + 1)]
    seg_keys = jnp.concatenate(seg_rows, axis=1)
    square = lax.broadcasted_iota(jnp.int32, (rows, rows), 0) == lax.broadcasted_iota(
        jnp.int32, (rows, rows), 1
    )
    seg_own = jnp.sum(jnp.where(square, seg_rows[reach], 0.0), axis=1, keepdims=True)
    at_query = reach * rows + lax.broadcasted_iota(jnp.int32, (rows, keys), 0)
    at_key = lax.broadcasted_iota(jnp.int32, (rows, keys), 1)
    gap = at_query - at_key
    allowed = (
        (seg_keys == seg_own)
        & (gap >= 0)
        & (gap < WINDOW)
        & (at_key >= (reach - place) * rows)
    )
    cos_own, sin_own = cos_ref[reach * rows :, :], sin_ref[reach * rows :, :]
    ready("query")
    for h in range(heads):
        cols = slice(h * size, (h + 1) * size)
        qraw = mm(n1_out[reach * rows :, :], wq[:, cols])
        qraw_out[:, cols] = qraw
        q = turn_fwd(qraw * inverse_rms(qraw) * g_q, cos_own, sin_own) * scale
        q = q.astype(BF16)
        q_out[:, cols] = q
        s = jnp.where(allowed, mm_nt(q, k), -1e30)
        e = jnp.exp(s - jnp.max(s, axis=-1, keepdims=True))
        p = e * (1.0 / jnp.sum(e, axis=-1, keepdims=True))
        p_out[h] = p
        ao_out[:, cols] = mm(p.astype(BF16), v).astype(BF16)


def pick_halves(core, unit):
    row = lax.broadcasted_iota(jnp.int32, (2 * LANES, 2 * LANES), 0)
    col = lax.broadcasted_iota(jnp.int32, (2 * LANES, 2 * LANES), 1)
    side = jnp.where(col < LANES, core, 1 - core)
    at = col & (LANES - 1)
    want = (lax.div(at, unit) * 2 + side) * unit + lax.rem(at, unit)
    return jnp.where(row == want, 1.0, 0.0).astype(BF16)


def store_halves(keep, send, base, source, unit, core):
    pick = pick_halves(core, unit)
    for b in range(source.shape[1] // (2 * LANES)):
        block = mm(source[:, 2 * b * LANES : 2 * (b + 1) * LANES], pick).astype(BF16)
        keep[:, base + b * LANES : base + (b + 1) * LANES] = block[:, :LANES]
        send[:, base + b * LANES : base + (b + 1) * LANES] = block[:, LANES:]


def pair_columns(width, ff, attn):
    sizes = (ff, ff, width, width, ff // 2, attn // 2, padded(width // 2))
    starts = [sum(sizes[:n]) for n in range(len(sizes) + 1)]
    return starts[:-1], starts[-1]


def padded(columns):
    return -(-columns // LANES) * LANES


def forward_kernel(reach, layout, *refs):
    halo_h, refs = refs[: reach + 1], refs[reach + 1 :]
    ct_h, gains_h, order_h, cos_h, sin_h = refs[:5]
    wq_a, wk_a, wv_a, wg_a, wu_a, wo_a, wd_a, pack_h = refs[5:13]
    outs_h, refs = refs[13:28], refs[28:]
    halo, refs = refs[: reach + 1], refs[reach + 1 :]
    ct, gain_a, order, cos_ref, sin_ref = refs[:5]
    outs, refs = refs[5:20], refs[20:]
    wq, wk, wv, wo, wg, wu, wd, act_s, slope_s, hid_s, ao_ref, gain_b, sems = refs
    place, core = lax.axis_index("seq"), lax.axis_index("fsdp")
    traffic = Traffic(sems)
    waits = {}
    _, _, pack_row, column, cols = layout[7][0]
    gain_far = pack_h.at[pack_row : pack_row + 16, column : column + cols]
    waits["halo"] = traffic.fetch(list(zip(halo_h, halo)))
    waits["halo"] += traffic.fetch([(gains_h, gain_a), (gain_far, gain_b)])
    waits["kv"] = traffic.halves(core, wk_a, pack_h, layout[1], wk)
    waits["kv"] += traffic.halves(core, wv_a, pack_h, layout[2], wv)
    waits["kv"] += traffic.fetch([(cos_h, cos_ref), (sin_h, sin_ref)])
    waits["query"] = traffic.halves(core, wq_a, pack_h, layout[0], wq)
    waits["out"] = traffic.halves(core, wo_a, pack_h, layout[5], wo)
    waits["gate"] = traffic.halves(core, wg_a, pack_h, layout[3], wg)
    waits["gate"] += traffic.halves(core, wu_a, pack_h, layout[4], wu)
    waits["down"] = traffic.halves(core, wd_a, pack_h, layout[6], wd)
    waits["rest"] = traffic.fetch([(ct_h, ct), (order_h, order)])

    def ready(name):
        wait(waits[name])

    attention(
        reach,
        place,
        halo,
        lambda: all_gains(core, gain_a, gain_b),
        cos_ref,
        sin_ref,
        wq,
        wk,
        wv,
        (*outs[:7], ao_ref),
        ready,
    )
    for source, target in zip(outs[:7], outs_h[:7]):
        traffic.emit(source, target)
    mixed_out, dx_out, dao_out, dg_out, keep, send, gains_out, _ = outs[7:]
    for block in range(reach):
        traffic.emit(halo[block], outs_h[14].at[block])
    rows, width = ct.shape
    gains = all_gains(core, gain_a, gain_b)
    gains_out[...] = gains
    size2 = gains.shape[1] - 4 * width
    ff = wg.shape[1]
    base = width + size2
    g_pa = gains[:, base : base + width]
    g_pf = gains[:, base + width : base + 2 * width]
    g_pff = gains[:, base + 2 * width :]
    x = halo[reach][:rows, :].astype(F32)
    ready("out")
    ya = mm(ao_ref[...], wo[...])
    inv_a = inverse_rms(ya)
    hat_a = ya * inv_a
    x2 = x + hat_a * g_pa
    inv_f = inverse_rms(x2)
    hat_f = x2 * inv_f
    n2 = (hat_f * g_pf).astype(BF16)
    ready("gate")
    ready("down")
    ready("rest")
    c = ct[...].astype(F32)
    part = 512
    (at_gate, at_up, at_df, at_dya, at_hid, at_ao, at_n2), end = pair_columns(
        width, ff, ao_ref.shape[1]
    )
    keep_h, send_h = outs_h[11:13]

    def sent(begin, stop):
        for ref, target in ((send, send_h), (keep, keep_h)):
            traffic.emit(ref.at[:, begin:stop], target.at[:, begin:stop])

    n2_owned = mm_nt(n2, row_order(order, width, place, core)).astype(BF16)
    half = n2_owned.shape[1] // 2
    keep[:, at_n2:end] = n2_owned[:, :half]
    send[:, at_n2:end] = n2_owned[:, half:]
    store_halves(keep, send, at_ao, ao_ref, ao_ref.shape[1] // 32, core)
    sent(at_ao, end)
    root = math.sqrt(2.0 / math.pi)
    f = jnp.zeros((rows, width), F32)
    for at in range(0, ff, part):
        cols = slice(at, at + part)
        gate = mm(n2, wg[:, cols])
        up = mm(n2, wu[:, cols])
        t = jnp.tanh(root * (gate + 0.044715 * (gate * gate * gate)))
        act = 0.5 * gate * (1.0 + t)
        slope = 0.5 * (1.0 + t) + 0.5 * gate * (1.0 - t * t) * (
            root * (1.0 + 3.0 * 0.044715 * (gate * gate))
        )
        act_s[:, cols] = act
        slope_s[:, cols] = up * slope
        hid = (act * up).astype(BF16)
        hid_s[:, cols] = hid
        f = f + mm(hid, wd[cols, :])
    store_halves(keep, send, at_hid, hid_s, ff // 32, core)
    sent(at_hid, at_ao)
    inv_d = inverse_rms(f)
    hat_d = f * inv_d
    mixed_out[...] = (x2 + hat_d * g_pff).astype(BF16)
    traffic.emit(mixed_out, outs_h[7])
    df = norm_back(hat_d, inv_d, g_pff, c).astype(BF16)
    for ref in (send, keep):
        ref[:, at_df : at_df + width] = df
    sent(at_df, at_df + width)
    dn2 = jnp.zeros((rows, width), F32)
    for at in range(0, ff, part):
        cols = slice(at, at + part)
        dhid = mm_nt(df, wd[cols, :])
        dgate = (dhid * slope_s[:, cols]).astype(BF16)
        dup = (dhid * act_s[:, cols]).astype(BF16)
        for ref in (send, keep):
            ref[:, at_gate + at : at_gate + at + part] = dgate
            ref[:, at_up + at : at_up + at + part] = dup
        sent(at_gate + at, at_gate + at + part)
        sent(at_up + at, at_up + at + part)
        dn2 = dn2 + mm_nt(dgate, wg[:, cols]) + mm_nt(dup, wu[:, cols])
    dx2 = c + norm_back(hat_f, inv_f, g_pf, dn2)
    dya = norm_back(hat_a, inv_a, g_pa, dx2).astype(BF16)
    for ref in (send, keep):
        ref[:, at_dya : at_dya + width] = dya
    sent(at_dya, at_dya + width)
    dao_out[...] = mm_nt(dya, wo[...]).astype(BF16)
    traffic.emit(dao_out, outs_h[9])
    dx_out[...] = dx2
    traffic.emit(dx_out, outs_h[8])
    dg_out[:, :width] = jnp.sum(dx2 * hat_a, axis=0, keepdims=True)
    dg_out[:, width : 2 * width] = jnp.sum(dn2 * hat_f, axis=0, keepdims=True)
    dg_out[:, 2 * width :] = jnp.sum(c * hat_d, axis=0, keepdims=True)
    traffic.emit(dg_out, outs_h[10])
    traffic.emit(gains_out, outs_h[13])
    traffic.finish()


def put(xk, xs, first, plane, at, value):
    x_bit, y_bit = plane & 1, plane >> 1
    lead, other = (x_bit, y_bit) if first == "x" else (y_bit, x_bit)
    ref = xs if lead else xk
    ref[other, at : at + value.shape[0], :] = value


def grads_kernel(width, ff, attn, *refs):
    sources, outs_h, outs = refs[:2], refs[3:9], refs[9:15]
    gk, gs, uk, us, dk, ds = outs
    both, prod_s, sems = refs[15:]
    traffic = Traffic(sems)
    place = lax.axis_index("seq")
    (at_gate, at_up, at_df, at_dya, at_hid, at_ao, at_n2), end = pair_columns(width, ff, attn)

    def sent(ref):
        traffic.emit(ref, outs_h[[r is ref for r in outs].index(True)])

    def fetch(begin, stop):
        return traffic.fetch(
            (source.at[:, begin:stop], both.at[side * LANES : (side + 1) * LANES, begin:stop])
            for side, source in enumerate(sources)
        )

    gate_w = fetch(at_n2, end) + fetch(at_gate, at_up)
    up_w = fetch(at_up, at_df)
    rest_w = fetch(at_df, at_n2)
    per = width // 2 // XY
    for copies, base, (keep, send), first in (
        (gate_w, at_gate, (gk, gs), "x"),
        (up_w, at_up, (uk, us), "y"),
    ):
        wait(copies)
        for col in range(0, ff, 512):
            right = both[:, base + col : base + col + 512]
            out = mm_tn(both[:, at_n2:end], right).astype(BF16)
            for plane in range(XY):
                for b in range(4):
                    put(
                        keep,
                        send,
                        first,
                        plane,
                        (col // LANES + b) * per,
                        out[plane * per : (plane + 1) * per, b * LANES : (b + 1) * LANES],
                    )
        sent(send)
        sent(keep)
    wait(rest_w)
    row = 0
    for at_left, at_right, count in ((at_hid, at_df, ff // 2), (at_ao, at_dya, attn // 2)):
        left, right = both[:, at_left : at_left + count], both[:, at_right : at_right + width]
        prod_s[:count, :] = mm_tn(left, right)
        unit = count // (XY * LINE)
        for plane in range(XY):
            for line in range(LINE):
                whose = (place ^ (line * XY + plane)) * unit
                block = prod_s[pl.ds(pl.multiple_of(whose, unit), unit), :].astype(BF16)
                ref = ds if line & 1 else dk
                chunk = (plane >> 1) * 4 + (plane & 1) * 2 + (line >> 1)
                for b in range(width // LANES):
                    ref[chunk, row + b * unit : row + (b + 1) * unit, :] = block[
                        :, b * LANES : (b + 1) * LANES
                    ]
        row += width // LANES * unit
    sent(ds)
    sent(dk)
    traffic.finish()


def heads_kernel(*refs):
    count = 9
    ins_h, outs_h, refs = refs[:count], refs[count : count + 4], refs[count + 4 :]
    ins, outs, sems = refs[:count], refs[count : count + 4], refs[-1]
    gains, cos_ref, sin_ref, qraw_ref, q_ref, k_ref, v_ref, dao_ref, p_ref = ins
    dqr, dkr, dv_out, dgq_out = outs
    traffic = Traffic(sems)
    heads = p_ref.shape[0]
    first = traffic.fetch([(ins_h[n], ins[n]) for n in (7, 6, 5)])
    p_w = [traffic.start(ins_h[8].at[0], p_ref.at[0])]
    second = traffic.fetch([(ins_h[n], ins[n]) for n in range(5)])
    p_w += [traffic.start(ins_h[8].at[h], p_ref.at[h]) for h in range(1, heads)]
    wait(first)
    rows, size = q_ref.shape[0], k_ref.shape[1]
    keys = k_ref.shape[0]
    width = gains.shape[1] // 4 - size // 2
    scale = size ** (-0.5)
    k, v = k_ref[...], v_ref[...]
    dk = jnp.zeros((keys, size), F32)
    dv = jnp.zeros((keys, size), F32)
    dgq = jnp.zeros((1, size), F32)
    for h in range(heads):
        cols = slice(h * size, (h + 1) * size)
        p_w[h].wait()
        p = p_ref[h]
        dao = dao_ref[:, cols]
        dp = mm_nt(dao, v)
        ds = (p * (dp - jnp.sum(p * dp, axis=-1, keepdims=True))).astype(BF16)
        dv = dv + mm_tn(p.astype(BF16), dao)
        if h == 0:
            wait(second)
            g_q = gains[:, width : width + size]
            cos_own, sin_own = cos_ref[keys - rows :, :], sin_ref[keys - rows :, :]
        dk = dk + mm_tn(ds, q_ref[:, cols])
        dq = turn_bwd(mm(ds, k) * scale, cos_own, sin_own)
        qraw = qraw_ref[:, cols]
        inv = inverse_rms(qraw)
        hat = qraw * inv
        dgq = dgq + jnp.sum(dq * hat, axis=0, keepdims=True)
        dqr[:, cols] = norm_back(hat, inv, g_q, dq).astype(BF16)
    dkr[...] = turn_bwd(dk, cos_ref[...], sin_ref[...])
    dv_out[...] = dv.astype(BF16)
    dgq_out[...] = dgq
    for source, target in zip(outs, outs_h):
        traffic.emit(source, target)
    traffic.finish()


def back_kernel(reach, layout, *refs):
    count = 12
    ins_h, refs = refs[:count], refs[count:]
    _, wq_a, wk_a, wv_a, pack_h = refs[:5]
    outs_h, refs = refs[5:9], refs[9:]
    ins, refs = refs[:count], refs[count:]
    toks, tok, gains, order, scale_order, dg_post, dgq, n1_ref, kraw_ref, dkr, dqr, dv_ref = ins
    halo = [toks.at[n] for n in range(reach)] + [tok]
    outs = keep, send, dn1_own, dn1_far = refs[:4]
    wq, wk, wv, dkv_s, sems = refs[4:]
    place, core = lax.axis_index("seq"), lax.axis_index("fsdp")
    traffic = Traffic(sems)
    first = traffic.fetch([(ins_h[n], ins[n]) for n in (3, 7)])
    second = traffic.fetch([(ins_h[n], ins[n]) for n in (8, 9, 10, 11, 2)])
    copies = traffic.fetch([(ins_h[n], ins[n]) for n in (4, 5, 6, 0, 1)])
    for n, (mine, full) in enumerate(((wq_a, wq), (wk_a, wk), (wv_a, wv))):
        copies += traffic.halves(core, mine, pack_h, layout[n], full)
    rows = tok.shape[0] - SEG_ROWS
    width = n1_ref.shape[1]
    size = kraw_ref.shape[1]
    wait(first)
    perm = row_order(order, width, place, core)
    n1_t = mm_nt(perm, n1_ref[...]).astype(BF16)
    wait(second)
    g_k = gains[:, width + size : width + 2 * size]
    kraw = kraw_ref[...]
    inv = inverse_rms(kraw)
    hat = kraw * inv
    dk = dkr[...]
    dgk = jnp.sum(dk * hat, axis=0, keepdims=True)
    dkv_s[:, :size] = norm_back(hat, inv, g_k, dk).astype(BF16)
    dkv_s[:, size:] = dv_ref[...]
    half = width // 2
    per = half // XY
    attn = dqr.shape[1]
    wait(copies)
    dgi = jnp.zeros((1, width), F32)
    for block in range(reach + 1):
        span = slice(block * rows, (block + 1) * rows)
        dn1 = mm_nt(dkv_s[span, :size], wk[...]) + mm_nt(dkv_s[span, size:], wv[...])
        if block == reach:
            dn1 = dn1 + mm_nt(dqr[...], wq[...])
        x = halo[block][:rows, :].astype(F32)
        dgi = dgi + jnp.sum(dn1 * (x * inverse_rms(x)), axis=0, keepdims=True)
        if block == reach:
            dn1_own[...] = dn1
        else:
            bits = (place ^ (place - (reach - block))) & (XY - 1)
            low = dn1.astype(BF16)
            for b in range(width // LANES):
                dn1_far[bits, b * rows : (b + 1) * rows, :] = low[:, b * LANES : (b + 1) * LANES]
    scales = owners_rows(jnp.concatenate([dgi, dgq[...], dgk, dg_post[...]], axis=1))
    owner = scale_order[:, :1] ^ (place * 2 + core)
    mine = scale_order[:, 1:2] * 1024 + (owner & 3) * 8 + (owner >> 2)
    columns = lax.broadcasted_iota(jnp.int32, (mine.shape[0], 2 * XY * LINE), 1)
    scales = mm(jnp.where(columns == mine, 1.0, 0.0).astype(BF16), scales).astype(BF16)
    rows_each = scales.shape[0] // (2 * XY)
    for ref, begin, group in ((send, half, XY), (keep, 0, 0)):
        left = n1_t[begin : begin + half]
        own = left[:, reach * rows :]
        at = 0
        for value, left_part, total in (
            (dqr, own, attn),
            (dkv_s, left, 2 * size),
        ):
            for col in range(0, total, 512):
                out = mm(left_part, value[:, col : col + 512]).astype(BF16)
                for plane in range(XY):
                    for b in range(4):
                        ref[
                            plane,
                            at + (col // LANES + b) * per : at + (col // LANES + b + 1) * per,
                            :,
                        ] = out[plane * per : (plane + 1) * per, b * LANES : (b + 1) * LANES]
            at += total // LANES * per
        for plane in range(XY):
            row = (group + plane) * rows_each
            ref[plane, at : at + rows_each, :] = scales[row : row + rows_each]
        traffic.emit(ref, outs_h[0 if ref is keep else 1])
    for n in (3, 2):
        traffic.emit(outs[n], outs_h[n])
    traffic.finish()


def owners_rows(line):
    pieces = [line[:, r * LANES : (r + 1) * LANES] for r in range(line.shape[1] // LANES)]
    first, second, third = (jnp.concatenate(pieces[n::3], axis=0) for n in range(3))
    lane = lax.broadcasted_iota(jnp.int32, first.shape, 1)
    quarter = LANES // 4
    groups = [
        first,
        jnp.where(
            lane < quarter, pltpu.roll(first, quarter, 1), pltpu.roll(second, quarter, 1)
        ),
        jnp.where(
            lane < 2 * quarter,
            pltpu.roll(second, 2 * quarter, 1),
            pltpu.roll(third, 2 * quarter, 1),
        ),
        pltpu.roll(third, 3 * quarter, 1),
    ]
    return jnp.concatenate(groups, axis=0).astype(BF16)


def collect_kernel(skip, *refs):
    own_h, far_h, *near = refs[: XY + 1]
    total_out, below_out, own, far, sems = refs[XY + 3 :]
    traffic = Traffic(sems)
    wait(traffic.fetch([(own_h, own), (far_h.at[0], far)]))
    place = lax.axis_index("seq") & (XY - 1)
    rows = own.shape[0]
    total = own[...]
    below = far[...].astype(F32)
    for bits, ref in enumerate(near, 1):
        part = ref[skip:, :].astype(F32)
        mine = (place ^ bits) > place
        below = below + jnp.where(mine, 0.0, part)
        lanes = [part[b * rows : (b + 1) * rows] for b in range(part.shape[0] // rows)]
        total = total + jnp.where(mine, jnp.concatenate(lanes, axis=1), 0.0)
    total_out[...] = total
    below_out[...] = below.astype(BF16)


def finish_kernel(*refs):
    ins_h, (dn1, above), out_h, ins = refs[:3], refs[3:5], refs[5], refs[6:9]
    out, sems = refs[9:]
    traffic = Traffic(sems)
    wait(traffic.fetch(list(zip(ins_h, ins))))
    tok, gains, dx = ins
    rows, width = dx.shape
    lanes = [above[b * rows : (b + 1) * rows, :] for b in range(width // LANES)]
    total = dn1[...] + jnp.concatenate(lanes, axis=1).astype(F32)
    x = tok[:rows, :].astype(F32)
    inv = inverse_rms(x)
    out[...] = dx[...] + norm_back(x * inv, inv, gains[:, :width], total)
    traffic.emit(out, out_h)
    traffic.finish()


def line_split_kernel(groups, entries, extra, direct, after, *refs):
    count = sum(groups)
    ins, (keep, send, split, *sums) = refs[:count], refs[count + after :]
    at = 0
    for number, total in zip(groups, sums):
        value = ins[at][...].astype(F32)
        for other in ins[at + 1 : at + number]:
            value = value + other[: value.shape[0], :].astype(F32)
        total[...] = value
        at += number
    at = 0
    for group, row, blocks, unit in entries:
        for b in range(blocks):
            for position in range(LINE):
                begin = row + (b * LINE + position) * unit
                split[position, at : at + unit, :] = sums[group][begin : begin + unit, :]
            at += unit
    if extra:
        group, row = extra
        for position in range(LINE):
            one = sums[group][row + position : row + position + 1, :]
            split[position, at : at + 16, :] = jnp.broadcast_to(one, (16, LANES))
    order = ((keep, (0,)), (send, (1, 2, 3))) if direct else ((keep, (0, 2)), (send, (1, 3)))
    for ref, positions in order:
        for n, position in enumerate(positions):
            ref[n] = split[position].astype(ref.dtype)


def join_kernel(parts, entries, extra, *refs):
    count = len(entries) + extra
    ins, outs_h, refs = refs[:parts], refs[parts : parts + count], refs[parts + count :]
    flag, outs, (sum_s, sems) = refs[0], refs[1 : count + 1], refs[count + 1 :]
    flag[...] = jnp.zeros_like(flag)
    traffic = Traffic(sems)
    total = ins[0][...].astype(F32)
    for part in ins[1:]:
        total = total + part[...].astype(F32)
    sum_s[...] = total
    at = 0
    for (blocks, unit), out in zip(entries, outs):
        for b in range(blocks):
            out[pl.ds(b, unit, stride=blocks), :] = sum_s[at : at + unit, :]
            at += unit
    if extra:
        outs[-1][...] = sum_s[at : at + 8, :][:1, : outs[-1].shape[1]]
    for out, out_h in zip(outs, outs_h):
        traffic.emit(out, out_h)
    traffic.finish()


def call(kernel, fetched, others, outs, scratch, copies, limit=61):
    hbm = pl.BlockSpec(memory_space=pl.ANY)
    return pl.pallas_call(
        kernel,
        out_shape=outs,
        in_specs=[hbm] * (len(fetched) + len(others)),
        out_specs=[hbm] * len(outs),
        scratch_shapes=[pltpu.VMEM(a.shape, a.dtype) for a in (*fetched, *outs)]
        + scratch
        + [pltpu.SemaphoreType.DMA((copies,))],
        compiler_params=pltpu.CompilerParams(vmem_limit_bytes=limit * MIB),
        cost_estimate=pl.CostEstimate(flops=0, bytes_accessed=0, transcendentals=0),
    )(*fetched, *others)


def shape(dims, dtype):
    return jax.ShapeDtypeStruct(dims, dtype)


vmem = pl.BlockSpec(memory_space=pltpu.VMEM)
hbm = pl.BlockSpec(memory_space=pl.ANY)


def fast(
    tokens,
    segments,
    positions,
    w_query,
    w_key,
    w_value,
    w_out,
    w_gate,
    w_up,
    w_down,
    norm_gains,
    cotangent,
):
    rows, width = tokens.shape[1:]
    size = w_key.shape[1]
    attn = w_query.shape[1]
    heads = attn // size
    ff = w_gate.shape[1]
    count = norm_gains.shape[0] * 2
    reach = (WINDOW - 1 + rows - 1) // rows
    keys = (reach + 1) * rows
    place = lax.axis_index("seq")
    core = lax.axis_index("fsdp")

    def partner(value):
        return lax.ppermute(value, "fsdp", [(0, 1), (1, 0)])

    def across(value, bits):
        return lax.ppermute(value, "seq", [(i, i ^ bits) for i in range(XY * LINE)])

    gains_own = norm_gains.reshape(-1, LANES)
    weights = (w_query, w_key, w_value, w_gate, w_up, w_out, w_down)
    layout, columns = pack_layout(
        width // 2,
        [w.shape[1] for w in weights[:5]],
        [w.shape for w in weights[5:]] + [(16, LANES)],
    )
    tok, pack = pl.pallas_call(
        functools.partial(prepare_kernel, layout),
        out_shape=[
            shape((rows + SEG_ROWS, width), BF16),
            shape((width // 2, columns), BF16),
        ],
        in_specs=[pl.BlockSpec(memory_space=pl.ANY)] * 10,
        out_specs=[pl.BlockSpec(memory_space=pl.ANY)] * 2,
        scratch_shapes=[pltpu.VMEM((rows, width), BF16), pltpu.VMEM((1, rows), jnp.int32)]
        + [pltpu.VMEM(w.shape, BF16) for w in (*weights, gains_own)]
        + [
            pltpu.VMEM((rows + SEG_ROWS, width), BF16),
            pltpu.VMEM((16, LANES), BF16),
            pltpu.SemaphoreType.DMA((40,)),
        ],
        compiler_params=pltpu.CompilerParams(vmem_limit_bytes=61 * MIB),
    )(tokens[0], segments, *weights, gains_own)
    pack_far = partner(pack)
    halo = [shifted(tok, "seq", distance) for distance in range(reach, 0, -1)] + [tok]

    unit = width // (2 * XY * LINE)
    new = np.arange(width) // unit
    core_bit, plane, line = new // (XY * LINE), new // LINE % XY, new % LINE
    owner = (line * XY + plane) * 2 + core_bit
    order = jnp.asarray(np.stack([owner, np.arange(width) % unit], axis=1).astype(np.int32))
    apart = np.full((2, padded(width // 2), 2), [0, 1 << 20])
    apart[:, : width // 2] = np.stack([owner, np.arange(width) % unit], axis=1).reshape(2, -1, 2)
    order_pair = jnp.asarray(apart.reshape(-1, 2).astype(np.int32))
    freq = np.exp(np.arange(size // 2, dtype=np.float64) * (-2.0 * math.log(10000.0) / size))
    turn = np.arange(keys, dtype=np.float64)[:, None] * freq
    cosine = jnp.asarray(np.cos(turn).astype(np.float32))
    sine = jnp.asarray(np.sin(turn).astype(np.float32))

    pair_end = pair_columns(width, ff, attn)[1]
    n1, qraw, q, kraw, k, v, p, mixed, dx, dao, dg_post, mlp_keep, mlp_send, gains, toks = call(
        functools.partial(forward_kernel, reach, layout),
        (*halo, cotangent[0], gains_own, order_pair, cosine, sine),
        (*weights, pack_far),
        [
            shape((keys, width), BF16),
            shape((rows, attn), F32),
            shape((rows, attn), BF16),
            shape((keys, size), F32),
            shape((keys, size), BF16),
            shape((keys, size), BF16),
            shape((heads, rows, keys), F32),
            shape((rows, width), BF16),
            shape((rows, width), F32),
            shape((rows, attn), BF16),
            shape((1, 3 * width), F32),
            shape((rows, pair_end), BF16),
            shape((rows, pair_end), BF16),
            shape((1, count), F32),
            shape((reach, rows + SEG_ROWS, width), BF16),
        ],
        [
            pltpu.VMEM((width, attn), BF16),
            pltpu.VMEM((width, size), BF16),
            pltpu.VMEM((width, size), BF16),
            pltpu.VMEM((attn, width), BF16),
            pltpu.VMEM((width, ff), BF16),
            pltpu.VMEM((width, ff), BF16),
            pltpu.VMEM((ff, width), BF16),
            pltpu.VMEM((rows, ff), F32),
            pltpu.VMEM((rows, ff), F32),
            pltpu.VMEM((rows, ff), BF16),
            pltpu.VMEM((rows, attn), BF16),
            pltpu.VMEM((16, LANES), BF16),
        ],
        128,
    )
    mlp_recv = partner(mlp_send)

    dqr, dkr, dv, dgq = call(
        heads_kernel,
        (gains, cosine, sine, qraw, q, k, v, dao, p),
        (),
        [
            shape((rows, attn), BF16),
            shape((keys, size), F32),
            shape((keys, size), BF16),
            shape((1, size), F32),
        ],
        [],
        24,
        63,
    )

    per_ff = width // 2 // XY * ff // LANES
    per_down = ff // 2 // XY * width // LANES
    per_out = attn // 2 // XY * width // LANES
    gk, gs, uk, us, dk, ds = call(
        functools.partial(grads_kernel, width, ff, attn),
        (),
        (mlp_keep, mlp_recv, dgq),
        [shape((2, per_ff, LANES), BF16)] * 4
        + [shape((8, (per_down + per_out) // LINE, LANES), BF16)] * 2,
        [
            pltpu.VMEM((2 * rows, pair_end), BF16),
            pltpu.VMEM((ff // 2, width), F32),
        ],
        16,
    )

    per_q = width // 2 // XY * attn // LANES
    per_k = width // 2 // XY * size // LANES
    per_back = per_q + 2 * per_k
    share = count // (2 * XY * LINE)
    new = np.arange(2 * XY * 16)
    core_bit, plane, line = new // (XY * 16), new // 16 % XY, new % 16
    owner = (line % LINE * XY + plane) * 2 + core_bit
    scale_order = jnp.asarray(np.stack([owner, line // LINE], axis=1).astype(np.int32))
    back_keep, back_send, dn1_own, dn1_far = call(
        functools.partial(back_kernel, reach, layout),
        (toks, tok, gains, order, scale_order, dg_post, dgq, n1, kraw, dkr, dqr, dv),
        (gk, *weights[:3], pack_far),
        [
            shape((XY, per_back + 16, LANES), BF16),
            shape((XY, per_back + 16, LANES), BF16),
            shape((rows, width), F32),
            shape((XY, rows * width // LANES, LANES), BF16),
        ],
        [
            pltpu.VMEM((width, attn), BF16),
            pltpu.VMEM((width, size), BF16),
            pltpu.VMEM((width, size), BF16),
            pltpu.VMEM((keys, 2 * size), BF16),
        ],
        64,
    )
    back_recv = partner(back_send)

    def add(a, b):
        return (a.astype(F32) + b.astype(F32)).astype(BF16)

    def halves(keep, near):
        half = keep.shape[0] // 2
        return add(keep[:half], near[:half]), add(keep[half:], near[half:])

    def step(keep, send, bits):
        return halves(keep, across(send, bits))

    def line_split(groups, entries, extra, direct, after=()):
        part = sum(blocks * unit for _, _, blocks, unit in entries) + (16 if extra else 0)
        stay = 1 if direct else 2
        arrays = [array for g in groups for array in g]
        return pl.pallas_call(
            functools.partial(
                line_split_kernel, [len(g) for g in groups], entries, extra, direct, len(after)
            ),
            out_shape=[shape((n, part, LANES), BF16) for n in (stay, LINE - stay)],
            in_specs=[vmem] * (len(arrays) + len(after)),
            out_specs=[vmem] * 2,
            scratch_shapes=[pltpu.VMEM((LINE, part, LANES), F32)]
            + [pltpu.VMEM(g[0].shape, F32) for g in groups],
            compiler_params=pltpu.CompilerParams(vmem_limit_bytes=12 * MIB),
            cost_estimate=pl.CostEstimate(flops=0, bytes_accessed=0, transcendentals=0),
        )(*arrays, *after)

    def join(parts, entries, extra=False):
        outs = [shape((blocks * unit, LANES), F32) for blocks, unit in entries]
        if extra:
            outs.append(shape((1, share), F32))
        *arrays, flag = pl.pallas_call(
            functools.partial(join_kernel, len(parts), entries, int(extra)),
            out_shape=outs + [shape((8, LANES), F32)],
            in_specs=[vmem] * len(parts),
            out_specs=[hbm] * len(outs) + [vmem],
            scratch_shapes=[pltpu.VMEM(a.shape, a.dtype) for a in outs]
            + [pltpu.VMEM(parts[0].shape, F32), pltpu.SemaphoreType.DMA((len(outs),))],
            compiler_params=pltpu.CompilerParams(vmem_limit_bytes=12 * MIB),
            cost_estimate=pl.CostEstimate(flops=0, bytes_accessed=0, transcendentals=0),
        )(*parts)
        return arrays, flag

    wide, narrow = ff // LANES, width // LANES
    unit_out, unit_down = attn // 32, ff // 32

    planes = [add(back_keep[n], back_recv[n]) for n in range(XY)]
    planes = [planes[0]] + [
        across(jnp.concatenate([planes[n], dn1_far[n]]), n) for n in range(1, XY)
    ]

    gate_0, gate_1 = step(gk, gs, 1)
    up_0, up_1 = step(uk, us, 2)
    gate_2, up_2 = across(gate_1, 2), across(up_1, 1)
    flat = lambda value: value.reshape(value.shape[1:])
    keep, send = line_split(
        ((flat(gate_0), flat(gate_2)), (flat(up_0), flat(up_2))),
        ((0, 0, wide, unit), (1, 0, wide, unit)),
        None,
        False,
    )
    mlp_0, mlp_1 = step(keep, send, XY)
    (own_gate, own_up), mlp_done = join(
        (flat(mlp_0), flat(across(mlp_1, 2 * XY))), ((wide, unit), (wide, unit))
    )
    down_0, down_1 = step(dk, ds, XY)
    down_0, down_1 = step(down_0, down_1, 2)
    down_2, down_3 = step(down_0, down_1, 1)
    (own_down, own_out), down_done = join(
        (flat(down_2), flat(across(down_3, 2 * XY))), ((narrow, unit_down), (narrow, unit_out))
    )

    far_shape = (rows * width // LANES, LANES)
    dn1, below = pl.pallas_call(
        functools.partial(collect_kernel, per_back + 16),
        out_shape=[shape((rows, width), F32), shape(far_shape, BF16)],
        in_specs=[hbm] * 2 + [vmem] * (XY + 1),
        out_specs=[vmem] * 2,
        scratch_shapes=[
            pltpu.VMEM((rows, width), F32),
            pltpu.VMEM(far_shape, BF16),
            pltpu.SemaphoreType.DMA((2,)),
        ],
        compiler_params=pltpu.CompilerParams(vmem_limit_bytes=12 * MIB),
        cost_estimate=pl.CostEstimate(flops=0, bytes_accessed=0, transcendentals=0),
    )(dn1_own, dn1_far, *planes[1:], mlp_done, down_done)
    keep, send = line_split(
        (planes,),
        (
            (0, 0, attn // LANES, unit),
            (0, per_q, size // LANES, unit),
            (0, per_q + per_k, size // LANES, unit),
        ),
        (0, per_back),
        True,
        (below,),
    )
    (own_query, own_key, own_value, own_gains), _ = join(
        (flat(keep), *[across(send[n], (n + 1) * XY) for n in range(LINE - 1)]),
        ((attn // LANES, unit), (size // LANES, unit), (size // LANES, unit)),
        True,
    )

    input_grad = pl.pallas_call(
        finish_kernel,
        out_shape=shape((rows, width), F32),
        in_specs=[hbm] * 3 + [vmem] * 2,
        out_specs=hbm,
        scratch_shapes=[pltpu.VMEM(a.shape, a.dtype) for a in (tok, gains, dx, dx)]
        + [pltpu.SemaphoreType.DMA((4,))],
        compiler_params=pltpu.CompilerParams(vmem_limit_bytes=12 * MIB),
        cost_estimate=pl.CostEstimate(flops=0, bytes_accessed=0, transcendentals=0),
    )(tok, gains, dx, dn1, shifted(below, "seq", -XY))
    return (
        mixed[None],
        input_grad[None],
        own_query.reshape(-1),
        own_key.reshape(-1),
        own_value.reshape(-1),
        own_out.reshape(-1),
        own_gate.reshape(-1),
        own_up.reshape(-1),
        own_down.reshape(-1),
        own_gains.reshape(-1),
    )


def solution(mesh):
    placed = (
        P("fsdp", "seq", None),
        P("fsdp", "seq"),
        P("fsdp", "seq"),
        P("fsdp", None),
        P("fsdp", None),
        P("fsdp", None),
        P("fsdp", None),
        P("fsdp", None),
        P("fsdp", None),
        P("fsdp", None),
        P("fsdp"),
        P("fsdp", "seq", None),
    )
    small = mesh.shape["seq"] == XY * LINE and mesh.shape["fsdp"] == 2
    return jax.shard_map(
        fast if small else general,
        mesh=mesh,
        in_specs=placed,
        out_specs=(
            P("fsdp", "seq", None),
            P("fsdp", "seq", None),
            P(("seq", "fsdp")),
            P(("seq", "fsdp")),
            P(("seq", "fsdp")),
            P(("seq", "fsdp")),
            P(("seq", "fsdp")),
            P(("seq", "fsdp")),
            P(("seq", "fsdp")),
            P(("seq", "fsdp")),
        ),
        check_vma=False,
    )
```

```python
import functools
import math

import jax
import jax.numpy as jnp
import numpy as np
from jax import lax
from jax.experimental import pallas as pl
from jax.experimental.pallas import tpu as pltpu
from jax.sharding import PartitionSpec as P

WINDOW = 512
EPS = 1e-06
LANES = 128
SEG_ROWS = 16
F32 = jnp.float32
BF16 = jnp.bfloat16
MIB = 1 << 20


def shifted(x, axis, by):
    peers = lax.axis_size(axis)
    pairs = [(i, i + by) for i in range(peers) if 0 <= i + by < peers]
    return lax.ppermute(x, axis, pairs)


def norm_rows(value, gain):
    return value * lax.rsqrt(jnp.mean(value * value, axis=-1, keepdims=True) + EPS) * gain


def rotate(value, cosine, sine):
    half = value.shape[-1] // 2
    first = value[..., :half]
    second = value[..., half:]
    return jnp.concatenate(
        [first * cosine - second * sine, second * cosine + first * sine], axis=-1
    )


def angles(positions, size):
    freq = jnp.exp(jnp.arange(size // 2, dtype=jnp.float32) * (-2.0 * math.log(10000.0) / size))
    turn = positions.astype(jnp.float32)[..., None] * freq
    return (jnp.cos(turn), jnp.sin(turn))


def product(form, left, right):
    return jnp.einsum(form, left, right, preferred_element_type=jnp.float32)


def general(
    tokens,
    segments,
    positions,
    w_query,
    w_key,
    w_value,
    w_out,
    w_gate,
    w_up,
    w_down,
    norm_gains,
    cotangent,
):
    tok_rows = tokens.shape[1]
    width = tokens.shape[2]
    head_size = w_key.shape[1]
    head_count = w_query.shape[1] // head_size
    reach = (WINDOW - 1 + tok_rows - 1) // tok_rows
    scale = head_size ** (-0.5)
    gathered = tuple(
        lax.all_gather(w, "fsdp", axis=0, tiled=True)
        for w in (w_query, w_key, w_value, w_out, w_gate, w_up, w_down, norm_gains)
    )
    query_full, key_full, value_full, out_full, gate_full, up_full, down_full, gains_full = gathered
    gains = gains_full.astype(jnp.float32)
    gain_in = gains[:width]
    gain_q = gains[width : width + head_size]
    gain_k = gains[width + head_size : width + 2 * head_size]
    gain_pa = gains[width + 2 * head_size : 2 * width + 2 * head_size]
    gain_pf = gains[2 * width + 2 * head_size : 3 * width + 2 * head_size]
    gain_pff = gains[3 * width + 2 * head_size :]
    hidden_in = tokens[0].astype(jnp.float32)
    segment = segments[0]
    cosine, sine = angles(positions[0], head_size)
    normed, first_back = jax.vjp(norm_rows, hidden_in, gain_in)
    normed_low = normed.astype(jnp.bfloat16)
    query_raw = jnp.dot(normed_low, query_full, preferred_element_type=jnp.float32)
    key_raw = jnp.dot(normed_low, key_full, preferred_element_type=jnp.float32)
    value_low = jnp.dot(normed_low, value_full, preferred_element_type=jnp.float32).astype(
        jnp.bfloat16
    )

    def turn(query, key, gain_query, gain_key):
        query = norm_rows(query.reshape(tok_rows, head_count, head_size), gain_query)
        query = rotate(query, cosine[:, None, :], sine[:, None, :]) * scale
        key = rotate(norm_rows(key, gain_key), cosine, sine)
        return (query, key)

    (query_rot, key_rot), turn_back = jax.vjp(turn, query_raw, key_raw, gain_q, gain_k)
    query_low = query_rot.astype(jnp.bfloat16)
    packed = jnp.concatenate([key_rot.astype(jnp.bfloat16), value_low], axis=1)
    pieces = [packed]
    seg_pieces = [segment]
    for distance in range(1, reach + 1):
        far_pack, far_seg = shifted((packed, segment), "seq", distance)
        pieces.insert(0, far_pack)
        seg_pieces.insert(0, far_seg)
    keys_all = jnp.concatenate(pieces, axis=0)
    seg_all = jnp.concatenate(seg_pieces, axis=0)
    key_part = keys_all[:, :head_size]
    value_part = keys_all[:, head_size:]
    place = lax.axis_index("seq")
    query_index = place * tok_rows + jnp.arange(tok_rows, dtype=jnp.int32)
    key_index = (place - reach) * tok_rows + jnp.arange((reach + 1) * tok_rows, dtype=jnp.int32)
    spacing = query_index[:, None] - key_index[None, :]
    allowed = (
        (segment[:, None] == seg_all[None, :])
        & (spacing >= 0)
        & (spacing < WINDOW)
        & (key_index[None, :] >= 0)
    )
    scores = product("qhd,kd->hqk", query_low, key_part)
    masked = jnp.where(allowed[None], scores, -1e30)
    top = jnp.max(masked, axis=-1, keepdims=True)
    expd = jnp.exp(masked - top)
    total = jnp.sum(expd, axis=-1, keepdims=True)
    probs_low = (expd / total).astype(jnp.bfloat16)
    log_total = top + jnp.log(total)
    mixed_heads = (
        product("hqk,kd->qhd", probs_low, value_part)
        .reshape(tok_rows, head_count * head_size)
        .astype(jnp.bfloat16)
    )
    attn_out = jnp.dot(mixed_heads, out_full, preferred_element_type=jnp.float32)

    def middle(resid, branch, gain_a, gain_b):
        after = resid + norm_rows(branch, gain_a)
        return (after, norm_rows(after, gain_b))

    (after, normed_ff), middle_back = jax.vjp(middle, hidden_in, attn_out, gain_pa, gain_pf)
    ff_low = normed_ff.astype(jnp.bfloat16)
    gate = jnp.dot(ff_low, gate_full, preferred_element_type=jnp.float32)
    up_value = jnp.dot(ff_low, up_full, preferred_element_type=jnp.float32)

    def mixer(gate_in, up_in):
        return jax.nn.gelu(gate_in, approximate=True) * up_in

    inner, mixer_back = jax.vjp(mixer, gate, up_value)
    inner_low = inner.astype(jnp.bfloat16)
    down = jnp.dot(inner_low, down_full, preferred_element_type=jnp.float32)

    def finish(resid, branch, gain):
        return resid + norm_rows(branch, gain)

    result, finish_back = jax.vjp(finish, after, down, gain_pff)
    grad_result = cotangent[0].astype(jnp.float32)
    grad_after, grad_down, grad_gpff = finish_back(grad_result)
    down_grad_low = grad_down.astype(jnp.bfloat16)
    grad_w_down = product("tf,td->fd", inner_low, down_grad_low)
    grad_inner = product("td,fd->tf", down_grad_low, down_full)
    grad_gate, grad_upv = mixer_back(grad_inner)
    gate_grad_low = grad_gate.astype(jnp.bfloat16)
    up_grad_low = grad_upv.astype(jnp.bfloat16)
    grad_w_gate = product("td,tf->df", ff_low, gate_grad_low)
    grad_w_up = product("td,tf->df", ff_low, up_grad_low)
    grad_normed_ff = product("tf,df->td", gate_grad_low, gate_full) + product(
        "tf,df->td", up_grad_low, up_full
    )
    grad_resid, grad_branch, grad_gpa, grad_gpf = middle_back((grad_after, grad_normed_ff))
    branch_grad_low = grad_branch.astype(jnp.bfloat16)
    grad_w_out = product("ta,td->ad", mixed_heads, branch_grad_low)
    grad_heads = (
        product("td,ad->ta", branch_grad_low, out_full)
        .astype(jnp.bfloat16)
        .reshape(tok_rows, head_count, head_size)
    )
    scores_again = product("qhd,kd->hqk", query_low, key_part)
    probs = jnp.exp(jnp.where(allowed[None], scores_again, -1e30) - log_total)
    probs_again = probs.astype(jnp.bfloat16)
    grad_probs = product("qhd,kd->hqk", grad_heads, value_part)
    grad_scores = (
        probs * (grad_probs - jnp.sum(probs * grad_probs, axis=-1, keepdims=True))
    ).astype(jnp.bfloat16)
    grad_query_rot = product("hqk,kd->qhd", grad_scores, key_part)
    grad_keys = product("hqk,qhd->kd", grad_scores, query_low)
    grad_values = product("hqk,qhd->kd", probs_again, grad_heads)
    grad_packed = jnp.concatenate([grad_keys, grad_values], axis=1)
    collected = grad_packed[reach * tok_rows :]
    for distance in range(1, reach + 1):
        begin = (reach - distance) * tok_rows
        collected = collected + shifted(
            grad_packed[begin : begin + tok_rows].astype(jnp.bfloat16), "seq", -distance
        ).astype(jnp.float32)
    grad_key_rot = collected[:, :head_size]
    value_grad_low = collected[:, head_size:].astype(jnp.bfloat16)
    grad_q_raw, grad_k_raw, grad_gq, grad_gk = turn_back((grad_query_rot, grad_key_rot))
    query_grad_low = grad_q_raw.astype(jnp.bfloat16)
    key_grad_low = grad_k_raw.astype(jnp.bfloat16)
    grad_w_query = product("td,te->de", normed_low, query_grad_low)
    grad_w_key = product("td,te->de", normed_low, key_grad_low)
    grad_w_value = product("td,te->de", normed_low, value_grad_low)
    grad_normed = (
        product("te,de->td", query_grad_low, query_full)
        + product("te,de->td", key_grad_low, key_full)
        + product("te,de->td", value_grad_low, value_full)
    )
    grad_in, grad_gin = first_back(grad_normed)
    input_grad = (grad_resid + grad_in)[None]
    grad_gains = jnp.concatenate([grad_gin, grad_gq, grad_gk, grad_gpa, grad_gpf, grad_gpff])
    own = tuple(
        lax.psum_scatter(g.reshape(-1), ("seq", "fsdp"), scatter_dimension=0, tiled=True)
        for g in (
            grad_w_query,
            grad_w_key,
            grad_w_value,
            grad_w_out,
            grad_w_gate,
            grad_w_up,
            grad_w_down,
            grad_gains,
        )
    )
    return (result.astype(jnp.bfloat16)[None], input_grad) + own


XY = 4
LINE = 4


def mm(a, b):
    return lax.dot_general(a, b, (((1,), (0,)), ((), ())), preferred_element_type=F32)


def mm_nt(a, b):
    return lax.dot_general(a, b, (((1,), (1,)), ((), ())), preferred_element_type=F32)


def mm_tn(a, b):
    return lax.dot_general(a, b, (((0,), (0,)), ((), ())), preferred_element_type=F32)


def inverse_rms(x):
    return lax.rsqrt(jnp.mean(x * x, axis=-1, keepdims=True) + EPS)


def norm_back(hat, inv, gain, grad):
    scaled = grad * gain
    return inv * (scaled - hat * jnp.mean(hat * scaled, axis=-1, keepdims=True))


def turn_fwd(x, cosine, sine):
    half = x.shape[1] // 2
    a, b = x[:, :half], x[:, half:]
    return jnp.concatenate([a * cosine - b * sine, b * cosine + a * sine], axis=1)


def turn_bwd(x, cosine, sine):
    half = x.shape[1] // 2
    a, b = x[:, :half], x[:, half:]
    return jnp.concatenate([a * cosine + b * sine, b * cosine - a * sine], axis=1)


def all_gains(core, mine, theirs):
    a = mine[...].astype(F32)
    b = theirs[...].astype(F32)[: a.shape[0]]
    low, high = jnp.where(core == 0, a, b), jnp.where(core == 0, b, a)
    rows = [half[r : r + 1, :] for half in (low, high) for r in range(a.shape[0])]
    return jnp.concatenate(rows, axis=1)


def row_order(table, width, place, core):
    owner = table[:, :1] ^ (place * 2 + core)
    source = owner * (width // (2 * XY * LINE)) + table[:, 1:2]
    ranks = lax.broadcasted_iota(jnp.int32, (table.shape[0], width), 1)
    return jnp.where(ranks == source, 1.0, 0.0).astype(BF16)


class Traffic:
    def __init__(self, sems):
        self.sems = sems
        self.used = 0
        self.pending = []

    def start(self, source, target):
        copy = pltpu.make_async_copy(source, target, self.sems.at[self.used])
        self.used += 1
        copy.start()
        return copy

    def fetch(self, pairs):
        return [self.start(source, target) for source, target in pairs]

    def halves(self, core, mine, pack, pieces, full):
        rows = mine.shape[0]
        begin = pl.multiple_of(core * rows, 16)
        copies = [self.start(mine, full.at[pl.ds(begin, rows)])]
        for row, number, pack_row, column, cols in pieces:
            begin = pl.multiple_of((1 - core) * rows + row, 16)
            source = pack.at[pack_row : pack_row + number, column : column + cols]
            copies.append(self.start(source, full.at[pl.ds(begin, number)]))
        return copies

    def emit(self, source, target):
        self.pending.append(self.start(source, target))

    def finish(self):
        for copy in self.pending:
            copy.wait()


def pack_layout(rows, widths, talls):
    layout, column = [], 0
    for width in widths:
        layout.append([(0, rows, 0, column, width)])
        column += width
    at = 0
    for height, width in talls:
        pieces, done = [], 0
        while done < height:
            take = min(height - done, rows - at % rows)
            pieces.append((done, take, at % rows, column + at // rows * talls[0][1], width))
            done, at = done + take, at + take
        layout.append(pieces)
    return layout, column + -(-at // rows) * talls[0][1]


def prepare_kernel(layout, *refs):
    count = len(layout)
    tok_h, seg_h, *weights_h = refs[: count + 2]
    ext_h, pack_h = refs[count + 2 : count + 4]
    tok, seg, *weights = refs[count + 4 : 2 * count + 6]
    ext, gain_s, sems = refs[2 * count + 6 :]
    traffic = Traffic(sems)
    first = traffic.fetch([(tok_h, tok), (seg_h, seg)])
    rest = traffic.fetch(list(zip(weights_h, weights)))
    wait(first)
    rows, width = tok.shape
    ext[:rows, :] = tok[...]
    ext[rows:, :] = jnp.zeros((SEG_ROWS, width), BF16)
    ids = seg[...].astype(F32)
    ext[rows:, :rows] = jnp.broadcast_to(ids, (SEG_ROWS, rows)).astype(BF16)
    traffic.emit(ext, ext_h)
    for copy, source, pieces in zip(rest, weights, layout):
        copy.wait()
        if source is weights[-1]:
            missing = gain_s.shape[0] - source.shape[0]
            filled = [source[...].astype(F32), jnp.zeros((missing, LANES), F32)]
            gain_s[...] = jnp.concatenate(filled, axis=0).astype(BF16)
            source = gain_s
        for row, number, pack_row, column, cols in pieces:
            traffic.emit(
                source.at[row : row + number, :],
                pack_h.at[pack_row : pack_row + number, column : column + cols],
            )
    traffic.finish()


def wait(copies):
    for copy in copies:
        copy.wait()


def attention(reach, place, halo, gains, cos_ref, sin_ref, wq, wk, wv, outs, ready):
    n1_out, qraw_out, q_out, kraw_out, k_out, v_out, p_out, ao_out = outs
    width = n1_out.shape[1]
    rows = halo[0].shape[0] - SEG_ROWS
    size = k_out.shape[1]
    heads = q_out.shape[1] // size
    scale = size ** (-0.5)
    ready("halo")
    gains = gains()
    g_in = gains[:, :width]
    g_q = gains[:, width : width + size]
    g_k = gains[:, width + size : width + 2 * size]
    for block in range(reach + 1):
        x = halo[block][:rows, :].astype(F32)
        n1_out[block * rows : (block + 1) * rows, :] = (x * inverse_rms(x) * g_in).astype(BF16)
    ready("kv")
    n1 = n1_out[...]
    kraw = mm(n1, wk[...])
    kraw_out[...] = kraw
    k = turn_fwd(kraw * inverse_rms(kraw) * g_k, cos_ref[...], sin_ref[...]).astype(BF16)
    k_out[...] = k
    v = mm(n1, wv[...]).astype(BF16)
    v_out[...] = v
    keys = (reach + 1) * rows
    seg_rows = [halo[b][rows:, :rows].astype(F32)[:1] for b in range(reach + 1)]
    seg_keys = jnp.concatenate(seg_rows, axis=1)
    square = lax.broadcasted_iota(jnp.int32, (rows, rows), 0) == lax.broadcasted_iota(
        jnp.int32, (rows, rows), 1
    )
    seg_own = jnp.sum(jnp.where(square, seg_rows[reach], 0.0), axis=1, keepdims=True)
    at_query = reach * rows + lax.broadcasted_iota(jnp.int32, (rows, keys), 0)
    at_key = lax.broadcasted_iota(jnp.int32, (rows, keys), 1)
    gap = at_query - at_key
    allowed = (
        (seg_keys == seg_own)
        & (gap >= 0)
        & (gap < WINDOW)
        & (at_key >= (reach - place) * rows)
    )
    cos_own, sin_own = cos_ref[reach * rows :, :], sin_ref[reach * rows :, :]
    ready("query")
    for h in range(heads):
        cols = slice(h * size, (h + 1) * size)
        qraw = mm(n1_out[reach * rows :, :], wq[:, cols])
        qraw_out[:, cols] = qraw
        q = turn_fwd(qraw * inverse_rms(qraw) * g_q, cos_own, sin_own) * scale
        q = q.astype(BF16)
        q_out[:, cols] = q
        s = jnp.where(allowed, mm_nt(q, k), -1e30)
        e = jnp.exp(s - jnp.max(s, axis=-1, keepdims=True))
        p = e * (1.0 / jnp.sum(e, axis=-1, keepdims=True))
        p_out[h] = p
        ao_out[:, cols] = mm(p.astype(BF16), v).astype(BF16)


def pick_halves(core, unit):
    row = lax.broadcasted_iota(jnp.int32, (2 * LANES, 2 * LANES), 0)
    col = lax.broadcasted_iota(jnp.int32, (2 * LANES, 2 * LANES), 1)
    side = jnp.where(col < LANES, core, 1 - core)
    at = col & (LANES - 1)
    want = (lax.div(at, unit) * 2 + side) * unit + lax.rem(at, unit)
    return jnp.where(row == want, 1.0, 0.0).astype(BF16)


def store_halves(keep, send, base, source, unit, core):
    pick = pick_halves(core, unit)
    for b in range(source.shape[1] // (2 * LANES)):
        block = mm(source[:, 2 * b * LANES : 2 * (b + 1) * LANES], pick).astype(BF16)
        keep[:, base + b * LANES : base + (b + 1) * LANES] = block[:, :LANES]
        send[:, base + b * LANES : base + (b + 1) * LANES] = block[:, LANES:]


def pair_columns(width, ff, attn):
    sizes = (ff, ff, width, width, ff // 2, attn // 2, padded(width // 2))
    starts = [sum(sizes[:n]) for n in range(len(sizes) + 1)]
    return starts[:-1], starts[-1]


def padded(columns):
    return -(-columns // LANES) * LANES


def forward_kernel(reach, layout, *refs):
    halo_h, refs = refs[: reach + 1], refs[reach + 1 :]
    ct_h, gains_h, order_h, cos_h, sin_h = refs[:5]
    wq_a, wk_a, wv_a, wg_a, wu_a, wo_a, wd_a, pack_h = refs[5:13]
    outs_h, refs = refs[13:28], refs[28:]
    halo, refs = refs[: reach + 1], refs[reach + 1 :]
    ct, gain_a, order, cos_ref, sin_ref = refs[:5]
    outs, refs = refs[5:20], refs[20:]
    wq, wk, wv, wo, wg, wu, wd, act_s, slope_s, hid_s, ao_ref, gain_b, sems = refs
    place, core = lax.axis_index("seq"), lax.axis_index("fsdp")
    traffic = Traffic(sems)
    waits = {}
    _, _, pack_row, column, cols = layout[7][0]
    gain_far = pack_h.at[pack_row : pack_row + 16, column : column + cols]
    waits["halo"] = traffic.fetch(list(zip(halo_h, halo)))
    waits["halo"] += traffic.fetch([(gains_h, gain_a), (gain_far, gain_b)])
    waits["kv"] = traffic.halves(core, wk_a, pack_h, layout[1], wk)
    waits["kv"] += traffic.halves(core, wv_a, pack_h, layout[2], wv)
    waits["kv"] += traffic.fetch([(cos_h, cos_ref), (sin_h, sin_ref)])
    waits["query"] = traffic.halves(core, wq_a, pack_h, layout[0], wq)
    waits["out"] = traffic.halves(core, wo_a, pack_h, layout[5], wo)
    waits["gate"] = traffic.halves(core, wg_a, pack_h, layout[3], wg)
    waits["gate"] += traffic.halves(core, wu_a, pack_h, layout[4], wu)
    waits["down"] = traffic.halves(core, wd_a, pack_h, layout[6], wd)
    waits["rest"] = traffic.fetch([(ct_h, ct), (order_h, order)])

    def ready(name):
        wait(waits[name])

    attention(
        reach,
        place,
        halo,
        lambda: all_gains(core, gain_a, gain_b),
        cos_ref,
        sin_ref,
        wq,
        wk,
        wv,
        (*outs[:7], ao_ref),
        ready,
    )
    for source, target in zip(outs[:7], outs_h[:7]):
        traffic.emit(source, target)
    mixed_out, dx_out, dao_out, dg_out, keep, send, gains_out, _ = outs[7:]
    for block in range(reach):
        traffic.emit(halo[block], outs_h[14].at[block])
    rows, width = ct.shape
    gains = all_gains(core, gain_a, gain_b)
    gains_out[...] = gains
    size2 = gains.shape[1] - 4 * width
    ff = wg.shape[1]
    base = width + size2
    g_pa = gains[:, base : base + width]
    g_pf = gains[:, base + width : base + 2 * width]
    g_pff = gains[:, base + 2 * width :]
    x = halo[reach][:rows, :].astype(F32)
    ready("out")
    ya = mm(ao_ref[...], wo[...])
    inv_a = inverse_rms(ya)
    hat_a = ya * inv_a
    x2 = x + hat_a * g_pa
    inv_f = inverse_rms(x2)
    hat_f = x2 * inv_f
    n2 = (hat_f * g_pf).astype(BF16)
    ready("gate")
    ready("down")
    ready("rest")
    c = ct[...].astype(F32)
    part = 512
    (at_gate, at_up, at_df, at_dya, at_hid, at_ao, at_n2), end = pair_columns(
        width, ff, ao_ref.shape[1]
    )
    keep_h, send_h = outs_h[11:13]

    def sent(begin, stop):
        both = ((send, send_h), (keep, keep_h)) if begin >= at_hid else ((send, send_h),)
        for ref, target in both:
            traffic.emit(ref.at[:, begin:stop], target.at[:, begin:stop])

    n2_owned = mm_nt(n2, row_order(order, width, place, core)).astype(BF16)
    half = n2_owned.shape[1] // 2
    keep[:, at_n2:end] = n2_owned[:, :half]
    send[:, at_n2:end] = n2_owned[:, half:]
    store_halves(keep, send, at_ao, ao_ref, ao_ref.shape[1] // 32, core)
    sent(at_ao, end)
    root = math.sqrt(2.0 / math.pi)
    f = jnp.zeros((rows, width), F32)
    for at in range(0, ff, part):
        cols = slice(at, at + part)
        gate = mm(n2, wg[:, cols])
        up = mm(n2, wu[:, cols])
        t = jnp.tanh(root * (gate + 0.044715 * (gate * gate * gate)))
        act = 0.5 * gate * (1.0 + t)
        slope = 0.5 * (1.0 + t) + 0.5 * gate * (1.0 - t * t) * (
            root * (1.0 + 3.0 * 0.044715 * (gate * gate))
        )
        act_s[:, cols] = act
        slope_s[:, cols] = up * slope
        hid = (act * up).astype(BF16)
        hid_s[:, cols] = hid
        f = f + mm(hid, wd[cols, :])
    store_halves(keep, send, at_hid, hid_s, ff // 32, core)
    sent(at_hid, at_ao)
    inv_d = inverse_rms(f)
    hat_d = f * inv_d
    mixed_out[...] = (x2 + hat_d * g_pff).astype(BF16)
    traffic.emit(mixed_out, outs_h[7])
    df = norm_back(hat_d, inv_d, g_pff, c).astype(BF16)
    send[:, at_df : at_df + width] = df
    sent(at_df, at_df + width)
    dn2 = jnp.zeros((rows, width), F32)
    for at in range(0, ff, part):
        cols = slice(at, at + part)
        dhid = mm_nt(df, wd[cols, :])
        dgate = (dhid * slope_s[:, cols]).astype(BF16)
        dup = (dhid * act_s[:, cols]).astype(BF16)
        send[:, at_gate + at : at_gate + at + part] = dgate
        send[:, at_up + at : at_up + at + part] = dup
        sent(at_gate + at, at_gate + at + part)
        sent(at_up + at, at_up + at + part)
        dn2 = dn2 + mm_nt(dgate, wg[:, cols]) + mm_nt(dup, wu[:, cols])
    dx2 = c + norm_back(hat_f, inv_f, g_pf, dn2)
    dya = norm_back(hat_a, inv_a, g_pa, dx2).astype(BF16)
    send[:, at_dya : at_dya + width] = dya
    sent(at_dya, at_dya + width)
    dao_out[...] = mm_nt(dya, wo[...]).astype(BF16)
    traffic.emit(dao_out, outs_h[9])
    dx_out[...] = dx2
    traffic.emit(dx_out, outs_h[8])
    dg_out[:, :width] = jnp.sum(dx2 * hat_a, axis=0, keepdims=True)
    dg_out[:, width : 2 * width] = jnp.sum(dn2 * hat_f, axis=0, keepdims=True)
    dg_out[:, 2 * width :] = jnp.sum(c * hat_d, axis=0, keepdims=True)
    traffic.emit(dg_out, outs_h[10])
    traffic.emit(gains_out, outs_h[13])
    traffic.finish()


def put(xk, xs, first, plane, at, value):
    x_bit, y_bit = plane & 1, plane >> 1
    lead, other = (x_bit, y_bit) if first == "x" else (y_bit, x_bit)
    ref = xs if lead else xk
    ref[other, at : at + value.shape[0], :] = value


def grads_kernel(width, ff, attn, *refs):
    keep_h, send_h, recv_h = refs[:3]
    outs_h, outs = refs[4:10], refs[10:16]
    gk, gs, uk, us, dk, ds = outs
    both, prod_s, sems = refs[16:]
    traffic = Traffic(sems)
    place = lax.axis_index("seq")
    (at_gate, at_up, at_df, at_dya, at_hid, at_ao, at_n2), end = pair_columns(width, ff, attn)

    def sent(ref):
        traffic.emit(ref, outs_h[[r is ref for r in outs].index(True)])

    def fetch(begin, stop):
        own_h = keep_h if begin >= at_hid else send_h
        return traffic.fetch(
            (source.at[:, begin:stop], both.at[side * LANES : (side + 1) * LANES, begin:stop])
            for side, source in enumerate((own_h, recv_h))
        )

    gate_w = fetch(at_n2, end) + fetch(at_gate, at_up)
    up_w = fetch(at_up, at_df)
    rest_w = fetch(at_df, at_hid) + fetch(at_hid, at_n2)
    per = width // 2 // XY
    for copies, base, (keep, send), first in (
        (gate_w, at_gate, (gk, gs), "x"),
        (up_w, at_up, (uk, us), "y"),
    ):
        wait(copies)
        for col in range(0, ff, 512):
            right = both[:, base + col : base + col + 512]
            out = mm_tn(both[:, at_n2:end], right).astype(BF16)
            for plane in range(XY):
                for b in range(4):
                    put(
                        keep,
                        send,
                        first,
                        plane,
                        (col // LANES + b) * per,
                        out[plane * per : (plane + 1) * per, b * LANES : (b + 1) * LANES],
                    )
        sent(send)
        sent(keep)
    wait(rest_w)
    row = 0
    for at_left, at_right, count in ((at_hid, at_df, ff // 2), (at_ao, at_dya, attn // 2)):
        left, right = both[:, at_left : at_left + count], both[:, at_right : at_right + width]
        prod_s[:count, :] = mm_tn(left, right)
        unit = count // (XY * LINE)
        for plane in range(XY):
            for line in range(LINE):
                whose = (place ^ (line * XY + plane)) * unit
                block = prod_s[pl.ds(pl.multiple_of(whose, unit), unit), :].astype(BF16)
                ref = ds if line & 1 else dk
                chunk = (plane >> 1) * 4 + (plane & 1) * 2 + (line >> 1)
                for b in range(width // LANES):
                    ref[chunk, row + b * unit : row + (b + 1) * unit, :] = block[
                        :, b * LANES : (b + 1) * LANES
                    ]
        row += width // LANES * unit
    sent(ds)
    sent(dk)
    traffic.finish()


def heads_kernel(*refs):
    count = 5
    ins_h, outs_h, refs = refs[:count], refs[count : count + 3], refs[count + 3 :]
    ins, outs, sems = refs[:count], refs[count : count + 3], refs[-1]
    q_ref, k_ref, v_ref, dao_ref, p_ref = ins
    dq_out, dk_out, done = outs
    traffic = Traffic(sems)
    heads = p_ref.shape[0]
    first = traffic.fetch([(ins_h[n], ins[n]) for n in (3, 2)])
    p_w = [traffic.start(ins_h[4].at[0], p_ref.at[0])]
    second = traffic.fetch([(ins_h[n], ins[n]) for n in (1, 0)])
    p_w += [traffic.start(ins_h[4].at[h], p_ref.at[h]) for h in range(1, heads)]
    keys, size = k_ref.shape
    wait(first)
    v = v_ref[...]
    dk = jnp.zeros((keys, size), F32)
    for h in range(heads):
        cols = slice(h * size, (h + 1) * size)
        dp = mm_nt(dao_ref[:, cols], v)
        p_w[h].wait()
        p = p_ref[h]
        ds = (p * (dp - jnp.sum(p * dp, axis=-1, keepdims=True))).astype(BF16)
        if h == 0:
            wait(second)
            k = k_ref[...]
        dk = dk + mm_tn(ds, q_ref[:, cols])
        dq_out[:, cols] = mm(ds, k)
    dk_out[...] = dk
    done[...] = jnp.zeros_like(done)
    for source, target in zip(outs, outs_h):
        traffic.emit(source, target)
    traffic.finish()


def back_kernel(reach, layout, *refs):
    count = 15
    ins_h, refs = refs[:count], refs[count:]
    _, wq_a, wk_a, wv_a, pack_h = refs[:5]
    outs_h, refs = refs[5:9], refs[9:]
    ins, refs = refs[:count], refs[count:]
    toks, tok, gains, order, scale_order, dg_post, cos_ref, sin_ref, *more = ins
    n1_ref, dao_ref, p_ref, qraw_ref, kraw_ref, dq_ref, dk_ref = more
    halo = [toks.at[n] for n in range(reach)] + [tok]
    outs = keep, send, dn1_own, dn1_far = refs[:4]
    wq, wk, wv, dkv_s, dqr, sems = refs[4:]
    place, core = lax.axis_index("seq"), lax.axis_index("fsdp")
    traffic = Traffic(sems)
    first = traffic.fetch([(ins_h[n], ins[n]) for n in (3, 8)])
    second = traffic.fetch([(ins_h[n], ins[n]) for n in (9, 10)])
    third = traffic.fetch([(ins_h[n], ins[n]) for n in (2, 6, 7, 11, 12, 13, 14)])
    copies = traffic.fetch([(ins_h[n], ins[n]) for n in (4, 5, 0, 1)])
    for n, (mine, full) in enumerate(((wq_a, wq), (wk_a, wk), (wv_a, wv))):
        copies += traffic.halves(core, mine, pack_h, layout[n], full)
    rows = tok.shape[0] - SEG_ROWS
    width = n1_ref.shape[1]
    size = kraw_ref.shape[1]
    wait(first)
    perm = row_order(order, width, place, core)
    n1_t = mm_nt(perm, n1_ref[...]).astype(BF16)
    wait(second)
    heads = p_ref.shape[0]
    dv = jnp.zeros((n1_ref.shape[0], size), F32)
    for h in range(heads):
        dv = dv + mm_tn(p_ref[h].astype(BF16), dao_ref[:, h * size : (h + 1) * size])
    dkv_s[:, size:] = dv.astype(BF16)
    wait(third)
    g_q = gains[:, width : width + size]
    cos_own, sin_own = cos_ref[reach * rows :, :], sin_ref[reach * rows :, :]
    dgq = jnp.zeros((1, size), F32)
    for h in range(heads):
        cols = slice(h * size, (h + 1) * size)
        dq = turn_bwd(dq_ref[:, cols] * size ** (-0.5), cos_own, sin_own)
        qraw = qraw_ref[:, cols]
        inv = inverse_rms(qraw)
        hat = qraw * inv
        dgq = dgq + jnp.sum(dq * hat, axis=0, keepdims=True)
        dqr[:, cols] = norm_back(hat, inv, g_q, dq).astype(BF16)
    g_k = gains[:, width + size : width + 2 * size]
    kraw = kraw_ref[...]
    inv = inverse_rms(kraw)
    hat = kraw * inv
    dk = turn_bwd(dk_ref[...], cos_ref[...], sin_ref[...])
    dgk = jnp.sum(dk * hat, axis=0, keepdims=True)
    dkv_s[:, :size] = norm_back(hat, inv, g_k, dk).astype(BF16)
    half = width // 2
    per = half // XY
    attn = dqr.shape[1]
    wait(copies)
    dgi = jnp.zeros((1, width), F32)
    for block in range(reach + 1):
        span = slice(block * rows, (block + 1) * rows)
        dn1 = mm_nt(dkv_s[span, :size], wk[...]) + mm_nt(dkv_s[span, size:], wv[...])
        if block == reach:
            dn1 = dn1 + mm_nt(dqr[...], wq[...])
        x = halo[block][:rows, :].astype(F32)
        dgi = dgi + jnp.sum(dn1 * (x * inverse_rms(x)), axis=0, keepdims=True)
        if block == reach:
            dn1_own[...] = dn1
        else:
            bits = (place ^ (place - (reach - block))) & (XY - 1)
            low = dn1.astype(BF16)
            for b in range(width // LANES):
                dn1_far[bits, b * rows : (b + 1) * rows, :] = low[:, b * LANES : (b + 1) * LANES]
    scales = owners_rows(jnp.concatenate([dgi, dgq, dgk, dg_post[...]], axis=1))
    owner = scale_order[:, :1] ^ (place * 2 + core)
    mine = scale_order[:, 1:2] * 1024 + (owner & 3) * 8 + (owner >> 2)
    columns = lax.broadcasted_iota(jnp.int32, (mine.shape[0], 2 * XY * LINE), 1)
    scales = mm(jnp.where(columns == mine, 1.0, 0.0).astype(BF16), scales).astype(BF16)
    rows_each = scales.shape[0] // (2 * XY)
    for ref, begin, group in ((send, half, XY), (keep, 0, 0)):
        left = n1_t[begin : begin + half]
        own = left[:, reach * rows :]
        at = 0
        for value, left_part, total in (
            (dqr, own, attn),
            (dkv_s, left, 2 * size),
        ):
            for col in range(0, total, 512):
                out = mm(left_part, value[:, col : col + 512]).astype(BF16)
                for plane in range(XY):
                    for b in range(4):
                        ref[
                            plane,
                            at + (col // LANES + b) * per : at + (col // LANES + b + 1) * per,
                            :,
                        ] = out[plane * per : (plane + 1) * per, b * LANES : (b + 1) * LANES]
            at += total // LANES * per
        for plane in range(XY):
            row = (group + plane) * rows_each
            ref[plane, at : at + rows_each, :] = scales[row : row + rows_each]
        traffic.emit(ref, outs_h[0 if ref is keep else 1])
    for n in (3, 2):
        traffic.emit(outs[n], outs_h[n])
    traffic.finish()


def owners_rows(line):
    pieces = [line[:, r * LANES : (r + 1) * LANES] for r in range(line.shape[1] // LANES)]
    first, second, third = (jnp.concatenate(pieces[n::3], axis=0) for n in range(3))
    lane = lax.broadcasted_iota(jnp.int32, first.shape, 1)
    quarter = LANES // 4
    groups = [
        first,
        jnp.where(
            lane < quarter, pltpu.roll(first, quarter, 1), pltpu.roll(second, quarter, 1)
        ),
        jnp.where(
            lane < 2 * quarter,
            pltpu.roll(second, 2 * quarter, 1),
            pltpu.roll(third, 2 * quarter, 1),
        ),
        pltpu.roll(third, 3 * quarter, 1),
    ]
    return jnp.concatenate(groups, axis=0).astype(BF16)


def collect_kernel(skip, *refs):
    own_h, far_h, *near = refs[: XY + 1]
    total_out, below_out, own, far, sems = refs[XY + 3 :]
    traffic = Traffic(sems)
    wait(traffic.fetch([(own_h, own), (far_h.at[0], far)]))
    place = lax.axis_index("seq") & (XY - 1)
    rows = own.shape[0]
    total = own[...]
    below = far[...].astype(F32)
    for bits, ref in enumerate(near, 1):
        part = ref[skip:, :].astype(F32)
        mine = (place ^ bits) > place
        below = below + jnp.where(mine, 0.0, part)
        lanes = [part[b * rows : (b + 1) * rows] for b in range(part.shape[0] // rows)]
        total = total + jnp.where(mine, jnp.concatenate(lanes, axis=1), 0.0)
    total_out[...] = total
    below_out[...] = below.astype(BF16)


def finish_kernel(*refs):
    ins_h, (dn1, above), out_h, ins = refs[:3], refs[3:5], refs[5], refs[6:9]
    out, sems = refs[9:]
    traffic = Traffic(sems)
    wait(traffic.fetch(list(zip(ins_h, ins))))
    tok, gains, dx = ins
    rows, width = dx.shape
    lanes = [above[b * rows : (b + 1) * rows, :] for b in range(width // LANES)]
    total = dn1[...] + jnp.concatenate(lanes, axis=1).astype(F32)
    x = tok[:rows, :].astype(F32)
    inv = inverse_rms(x)
    out[...] = dx[...] + norm_back(x * inv, inv, gains[:, :width], total)
    traffic.emit(out, out_h)
    traffic.finish()


def line_split_kernel(groups, entries, extra, direct, after, *refs):
    count = sum(groups)
    ins, (keep, send, split, *sums) = refs[:count], refs[count + after :]
    at = 0
    for number, total in zip(groups, sums):
        value = ins[at][...].astype(F32)
        for other in ins[at + 1 : at + number]:
            value = value + other[: value.shape[0], :].astype(F32)
        total[...] = value
        at += number
    at = 0
    for group, row, blocks, unit in entries:
        for b in range(blocks):
            for position in range(LINE):
                begin = row + (b * LINE + position) * unit
                split[position, at : at + unit, :] = sums[group][begin : begin + unit, :]
            at += unit
    if extra:
        group, row = extra
        for position in range(LINE):
            one = sums[group][row + position : row + position + 1, :]
            split[position, at : at + 16, :] = jnp.broadcast_to(one, (16, LANES))
    order = ((keep, (0,)), (send, (1, 2, 3))) if direct else ((keep, (0, 2)), (send, (1, 3)))
    for ref, positions in order:
        for n, position in enumerate(positions):
            ref[n] = split[position].astype(ref.dtype)


def join_kernel(parts, entries, extra, *refs):
    count = len(entries) + extra
    ins, outs_h, refs = refs[:parts], refs[parts : parts + count], refs[parts + count :]
    flag, outs, (sum_s, sems) = refs[0], refs[1 : count + 1], refs[count + 1 :]
    flag[...] = jnp.zeros_like(flag)
    traffic = Traffic(sems)
    total = ins[0][...].astype(F32)
    for part in ins[1:]:
        total = total + part[...].astype(F32)
    sum_s[...] = total
    at = 0
    for (blocks, unit), out in zip(entries, outs):
        for b in range(blocks):
            out[pl.ds(b, unit, stride=blocks), :] = sum_s[at : at + unit, :]
            at += unit
    if extra:
        outs[-1][...] = sum_s[at : at + 8, :][:1, : outs[-1].shape[1]]
    for out, out_h in zip(outs, outs_h):
        traffic.emit(out, out_h)
    traffic.finish()


def call(kernel, fetched, others, outs, scratch, copies, limit=61):
    hbm = pl.BlockSpec(memory_space=pl.ANY)
    return pl.pallas_call(
        kernel,
        out_shape=outs,
        in_specs=[hbm] * (len(fetched) + len(others)),
        out_specs=[hbm] * len(outs),
        scratch_shapes=[pltpu.VMEM(a.shape, a.dtype) for a in (*fetched, *outs)]
        + scratch
        + [pltpu.SemaphoreType.DMA((copies,))],
        compiler_params=pltpu.CompilerParams(vmem_limit_bytes=limit * MIB),
        cost_estimate=pl.CostEstimate(flops=0, bytes_accessed=0, transcendentals=0),
    )(*fetched, *others)


def shape(dims, dtype):
    return jax.ShapeDtypeStruct(dims, dtype)


vmem = pl.BlockSpec(memory_space=pltpu.VMEM)
hbm = pl.BlockSpec(memory_space=pl.ANY)


def fast(
    tokens,
    segments,
    positions,
    w_query,
    w_key,
    w_value,
    w_out,
    w_gate,
    w_up,
    w_down,
    norm_gains,
    cotangent,
):
    rows, width = tokens.shape[1:]
    size = w_key.shape[1]
    attn = w_query.shape[1]
    heads = attn // size
    ff = w_gate.shape[1]
    count = norm_gains.shape[0] * 2
    reach = (WINDOW - 1 + rows - 1) // rows
    keys = (reach + 1) * rows
    place = lax.axis_index("seq")
    core = lax.axis_index("fsdp")

    def partner(value):
        return lax.ppermute(value, "fsdp", [(0, 1), (1, 0)])

    def across(value, bits):
        return lax.ppermute(value, "seq", [(i, i ^ bits) for i in range(XY * LINE)])

    gains_own = norm_gains.reshape(-1, LANES)
    weights = (w_query, w_key, w_value, w_gate, w_up, w_out, w_down)
    layout, columns = pack_layout(
        width // 2,
        [w.shape[1] for w in weights[:5]],
        [w.shape for w in weights[5:]] + [(16, LANES)],
    )
    tok, pack = pl.pallas_call(
        functools.partial(prepare_kernel, layout),
        out_shape=[
            shape((rows + SEG_ROWS, width), BF16),
            shape((width // 2, columns), BF16),
        ],
        in_specs=[pl.BlockSpec(memory_space=pl.ANY)] * 10,
        out_specs=[pl.BlockSpec(memory_space=pl.ANY)] * 2,
        scratch_shapes=[pltpu.VMEM((rows, width), BF16), pltpu.VMEM((1, rows), jnp.int32)]
        + [pltpu.VMEM(w.shape, BF16) for w in (*weights, gains_own)]
        + [
            pltpu.VMEM((rows + SEG_ROWS, width), BF16),
            pltpu.VMEM((16, LANES), BF16),
            pltpu.SemaphoreType.DMA((40,)),
        ],
        compiler_params=pltpu.CompilerParams(vmem_limit_bytes=61 * MIB),
    )(tokens[0], segments, *weights, gains_own)
    pack_far = partner(pack)
    halo = [shifted(tok, "seq", distance) for distance in range(reach, 0, -1)] + [tok]

    unit = width // (2 * XY * LINE)
    new = np.arange(width) // unit
    core_bit, plane, line = new // (XY * LINE), new // LINE % XY, new % LINE
    owner = (line * XY + plane) * 2 + core_bit
    order = jnp.asarray(np.stack([owner, np.arange(width) % unit], axis=1).astype(np.int32))
    apart = np.full((2, padded(width // 2), 2), [0, 1 << 20])
    apart[:, : width // 2] = np.stack([owner, np.arange(width) % unit], axis=1).reshape(2, -1, 2)
    order_pair = jnp.asarray(apart.reshape(-1, 2).astype(np.int32))
    freq = np.exp(np.arange(size // 2, dtype=np.float64) * (-2.0 * math.log(10000.0) / size))
    turn = np.arange(keys, dtype=np.float64)[:, None] * freq
    cosine = jnp.asarray(np.cos(turn).astype(np.float32))
    sine = jnp.asarray(np.sin(turn).astype(np.float32))

    pair_end = pair_columns(width, ff, attn)[1]
    n1, qraw, q, kraw, k, v, p, mixed, dx, dao, dg_post, mlp_keep, mlp_send, gains, toks = call(
        functools.partial(forward_kernel, reach, layout),
        (*halo, cotangent[0], gains_own, order_pair, cosine, sine),
        (*weights, pack_far),
        [
            shape((keys, width), BF16),
            shape((rows, attn), F32),
            shape((rows, attn), BF16),
            shape((keys, size), F32),
            shape((keys, size), BF16),
            shape((keys, size), BF16),
            shape((heads, rows, keys), F32),
            shape((rows, width), BF16),
            shape((rows, width), F32),
            shape((rows, attn), BF16),
            shape((1, 3 * width), F32),
            shape((rows, pair_end), BF16),
            shape((rows, pair_end), BF16),
            shape((1, count), F32),
            shape((reach, rows + SEG_ROWS, width), BF16),
        ],
        [
            pltpu.VMEM((width, attn), BF16),
            pltpu.VMEM((width, size), BF16),
            pltpu.VMEM((width, size), BF16),
            pltpu.VMEM((attn, width), BF16),
            pltpu.VMEM((width, ff), BF16),
            pltpu.VMEM((width, ff), BF16),
            pltpu.VMEM((ff, width), BF16),
            pltpu.VMEM((rows, ff), F32),
            pltpu.VMEM((rows, ff), F32),
            pltpu.VMEM((rows, ff), BF16),
            pltpu.VMEM((rows, attn), BF16),
            pltpu.VMEM((16, LANES), BF16),
        ],
        128,
    )
    mlp_recv = partner(mlp_send)

    dq, dk, heads_done = call(
        heads_kernel,
        (q, k, v, dao, p),
        (),
        [shape((rows, attn), F32), shape((keys, size), F32), shape((8, LANES), F32)],
        [],
        16,
        63,
    )

    per_ff = width // 2 // XY * ff // LANES
    per_down = ff // 2 // XY * width // LANES
    per_out = attn // 2 // XY * width // LANES
    gk, gs, uk, us, tk, ts = call(
        functools.partial(grads_kernel, width, ff, attn),
        (),
        (mlp_keep, mlp_send, mlp_recv, heads_done),
        [shape((2, per_ff, LANES), BF16)] * 4
        + [shape((8, (per_down + per_out) // LINE, LANES), BF16)] * 2,
        [
            pltpu.VMEM((2 * rows, pair_end), BF16),
            pltpu.VMEM((ff // 2, width), F32),
        ],
        16,
    )

    per_q = width // 2 // XY * attn // LANES
    per_k = width // 2 // XY * size // LANES
    per_back = per_q + 2 * per_k
    share = count // (2 * XY * LINE)
    new = np.arange(2 * XY * 16)
    core_bit, plane, line = new // (XY * 16), new // 16 % XY, new % 16
    owner = (line % LINE * XY + plane) * 2 + core_bit
    scale_order = jnp.asarray(np.stack([owner, line // LINE], axis=1).astype(np.int32))
    back_keep, back_send, dn1_own, dn1_far = call(
        functools.partial(back_kernel, reach, layout),
        (
            toks,
            tok,
            gains,
            order,
            scale_order,
            dg_post,
            cosine,
            sine,
            n1,
            dao,
            p,
            qraw,
            kraw,
            dq,
            dk,
        ),
        (gk, *weights[:3], pack_far),
        [
            shape((XY, per_back + 16, LANES), BF16),
            shape((XY, per_back + 16, LANES), BF16),
            shape((rows, width), F32),
            shape((XY, rows * width // LANES, LANES), BF16),
        ],
        [
            pltpu.VMEM((width, attn), BF16),
            pltpu.VMEM((width, size), BF16),
            pltpu.VMEM((width, size), BF16),
            pltpu.VMEM((keys, 2 * size), BF16),
            pltpu.VMEM((rows, attn), BF16),
        ],
        64,
    )
    back_recv = partner(back_send)

    def add(a, b):
        return (a.astype(F32) + b.astype(F32)).astype(BF16)

    def halves(keep, near):
        half = keep.shape[0] // 2
        return add(keep[:half], near[:half]), add(keep[half:], near[half:])

    def step(keep, send, bits):
        return halves(keep, across(send, bits))

    def line_split(groups, entries, extra, direct, after=()):
        part = sum(blocks * unit for _, _, blocks, unit in entries) + (16 if extra else 0)
        stay = 1 if direct else 2
        arrays = [array for g in groups for array in g]
        return pl.pallas_call(
            functools.partial(
                line_split_kernel, [len(g) for g in groups], entries, extra, direct, len(after)
            ),
            out_shape=[shape((n, part, LANES), BF16) for n in (stay, LINE - stay)],
            in_specs=[vmem] * (len(arrays) + len(after)),
            out_specs=[vmem] * 2,
            scratch_shapes=[pltpu.VMEM((LINE, part, LANES), F32)]
            + [pltpu.VMEM(g[0].shape, F32) for g in groups],
            compiler_params=pltpu.CompilerParams(vmem_limit_bytes=12 * MIB),
            cost_estimate=pl.CostEstimate(flops=0, bytes_accessed=0, transcendentals=0),
        )(*arrays, *after)

    def join(parts, entries, extra=False):
        outs = [shape((blocks * unit, LANES), F32) for blocks, unit in entries]
        if extra:
            outs.append(shape((1, share), F32))
        *arrays, flag = pl.pallas_call(
            functools.partial(join_kernel, len(parts), entries, int(extra)),
            out_shape=outs + [shape((8, LANES), F32)],
            in_specs=[vmem] * len(parts),
            out_specs=[hbm] * len(outs) + [vmem],
            scratch_shapes=[pltpu.VMEM(a.shape, a.dtype) for a in outs]
            + [pltpu.VMEM(parts[0].shape, F32), pltpu.SemaphoreType.DMA((len(outs),))],
            compiler_params=pltpu.CompilerParams(vmem_limit_bytes=12 * MIB),
            cost_estimate=pl.CostEstimate(flops=0, bytes_accessed=0, transcendentals=0),
        )(*parts)
        return arrays, flag

    wide, narrow = ff // LANES, width // LANES
    unit_out, unit_down = attn // 32, ff // 32

    planes = [add(back_keep[n], back_recv[n]) for n in range(XY)]
    planes = [planes[0]] + [
        across(jnp.concatenate([planes[n], dn1_far[n]]), n) for n in range(1, XY)
    ]

    gate_0, gate_1 = step(gk, gs, 1)
    up_0, up_1 = step(uk, us, 2)
    gate_2, up_2 = across(gate_1, 2), across(up_1, 1)
    flat = lambda value: value.reshape(value.shape[1:])
    keep, send = line_split(
        ((flat(gate_0), flat(gate_2)), (flat(up_0), flat(up_2))),
        ((0, 0, wide, unit), (1, 0, wide, unit)),
        None,
        False,
    )
    mlp_0, mlp_1 = step(keep, send, XY)
    (own_gate, own_up), mlp_done = join(
        (flat(mlp_0), flat(across(mlp_1, 2 * XY))), ((wide, unit), (wide, unit))
    )
    down_0, down_1 = step(tk, ts, XY)
    down_0, down_1 = step(down_0, down_1, 2)
    down_2, down_3 = step(down_0, down_1, 1)
    (own_down, own_out), down_done = join(
        (flat(down_2), flat(across(down_3, 2 * XY))), ((narrow, unit_down), (narrow, unit_out))
    )

    far_shape = (rows * width // LANES, LANES)
    dn1, below = pl.pallas_call(
        functools.partial(collect_kernel, per_back + 16),
        out_shape=[shape((rows, width), F32), shape(far_shape, BF16)],
        in_specs=[hbm] * 2 + [vmem] * (XY + 1),
        out_specs=[vmem] * 2,
        scratch_shapes=[
            pltpu.VMEM((rows, width), F32),
            pltpu.VMEM(far_shape, BF16),
            pltpu.SemaphoreType.DMA((2,)),
        ],
        compiler_params=pltpu.CompilerParams(vmem_limit_bytes=12 * MIB),
        cost_estimate=pl.CostEstimate(flops=0, bytes_accessed=0, transcendentals=0),
    )(dn1_own, dn1_far, *planes[1:], mlp_done, down_done)
    keep, send = line_split(
        (planes,),
        (
            (0, 0, attn // LANES, unit),
            (0, per_q, size // LANES, unit),
            (0, per_q + per_k, size // LANES, unit),
        ),
        (0, per_back),
        True,
        (below,),
    )
    (own_query, own_key, own_value, own_gains), _ = join(
        (flat(keep), *[across(send[n], (n + 1) * XY) for n in range(LINE - 1)]),
        ((attn // LANES, unit), (size // LANES, unit), (size // LANES, unit)),
        True,
    )

    input_grad = pl.pallas_call(
        finish_kernel,
        out_shape=shape((rows, width), F32),
        in_specs=[hbm] * 3 + [vmem] * 2,
        out_specs=hbm,
        scratch_shapes=[pltpu.VMEM(a.shape, a.dtype) for a in (tok, gains, dx, dx)]
        + [pltpu.SemaphoreType.DMA((4,))],
        compiler_params=pltpu.CompilerParams(vmem_limit_bytes=12 * MIB),
        cost_estimate=pl.CostEstimate(flops=0, bytes_accessed=0, transcendentals=0),
    )(tok, gains, dx, dn1, shifted(below, "seq", -XY))
    return (
        mixed[None],
        input_grad[None],
        own_query.reshape(-1),
        own_key.reshape(-1),
        own_value.reshape(-1),
        own_out.reshape(-1),
        own_gate.reshape(-1),
        own_up.reshape(-1),
        own_down.reshape(-1),
        own_gains.reshape(-1),
    )


def solution(mesh):
    placed = (
        P("fsdp", "seq", None),
        P("fsdp", "seq"),
        P("fsdp", "seq"),
        P("fsdp", None),
        P("fsdp", None),
        P("fsdp", None),
        P("fsdp", None),
        P("fsdp", None),
        P("fsdp", None),
        P("fsdp", None),
        P("fsdp"),
        P("fsdp", "seq", None),
    )
    small = mesh.shape["seq"] == XY * LINE and mesh.shape["fsdp"] == 2
    return jax.shard_map(
        fast if small else general,
        mesh=mesh,
        in_specs=placed,
        out_specs=(
            P("fsdp", "seq", None),
            P("fsdp", "seq", None),
            P(("seq", "fsdp")),
            P(("seq", "fsdp")),
            P(("seq", "fsdp")),
            P(("seq", "fsdp")),
            P(("seq", "fsdp")),
            P(("seq", "fsdp")),
            P(("seq", "fsdp")),
            P(("seq", "fsdp")),
        ),
        check_vma=False,
    )
```

```python
import functools
import math

import jax
import jax.numpy as jnp
import numpy as np
from jax import lax
from jax.experimental import pallas as pl
from jax.experimental.pallas import tpu as pltpu
from jax.sharding import PartitionSpec as P

WINDOW = 512
EPS = 1e-06
LANES = 128
SEG_ROWS = 16
F32 = jnp.float32
BF16 = jnp.bfloat16
MIB = 1 << 20


def shifted(x, axis, by):
    peers = lax.axis_size(axis)
    pairs = [(i, i + by) for i in range(peers) if 0 <= i + by < peers]
    return lax.ppermute(x, axis, pairs)


def norm_rows(value, gain):
    return value * lax.rsqrt(jnp.mean(value * value, axis=-1, keepdims=True) + EPS) * gain


def rotate(value, cosine, sine):
    half = value.shape[-1] // 2
    first = value[..., :half]
    second = value[..., half:]
    return jnp.concatenate(
        [first * cosine - second * sine, second * cosine + first * sine], axis=-1
    )


def angles(positions, size):
    freq = jnp.exp(jnp.arange(size // 2, dtype=jnp.float32) * (-2.0 * math.log(10000.0) / size))
    turn = positions.astype(jnp.float32)[..., None] * freq
    return (jnp.cos(turn), jnp.sin(turn))


def product(form, left, right):
    return jnp.einsum(form, left, right, preferred_element_type=jnp.float32)


def general(
    tokens,
    segments,
    positions,
    w_query,
    w_key,
    w_value,
    w_out,
    w_gate,
    w_up,
    w_down,
    norm_gains,
    cotangent,
):
    tok_rows = tokens.shape[1]
    width = tokens.shape[2]
    head_size = w_key.shape[1]
    head_count = w_query.shape[1] // head_size
    reach = (WINDOW - 1 + tok_rows - 1) // tok_rows
    scale = head_size ** (-0.5)
    gathered = tuple(
        lax.all_gather(w, "fsdp", axis=0, tiled=True)
        for w in (w_query, w_key, w_value, w_out, w_gate, w_up, w_down, norm_gains)
    )
    query_full, key_full, value_full, out_full, gate_full, up_full, down_full, gains_full = gathered
    gains = gains_full.astype(jnp.float32)
    gain_in = gains[:width]
    gain_q = gains[width : width + head_size]
    gain_k = gains[width + head_size : width + 2 * head_size]
    gain_pa = gains[width + 2 * head_size : 2 * width + 2 * head_size]
    gain_pf = gains[2 * width + 2 * head_size : 3 * width + 2 * head_size]
    gain_pff = gains[3 * width + 2 * head_size :]
    hidden_in = tokens[0].astype(jnp.float32)
    segment = segments[0]
    cosine, sine = angles(positions[0], head_size)
    normed, first_back = jax.vjp(norm_rows, hidden_in, gain_in)
    normed_low = normed.astype(jnp.bfloat16)
    query_raw = jnp.dot(normed_low, query_full, preferred_element_type=jnp.float32)
    key_raw = jnp.dot(normed_low, key_full, preferred_element_type=jnp.float32)
    value_low = jnp.dot(normed_low, value_full, preferred_element_type=jnp.float32).astype(
        jnp.bfloat16
    )

    def turn(query, key, gain_query, gain_key):
        query = norm_rows(query.reshape(tok_rows, head_count, head_size), gain_query)
        query = rotate(query, cosine[:, None, :], sine[:, None, :]) * scale
        key = rotate(norm_rows(key, gain_key), cosine, sine)
        return (query, key)

    (query_rot, key_rot), turn_back = jax.vjp(turn, query_raw, key_raw, gain_q, gain_k)
    query_low = query_rot.astype(jnp.bfloat16)
    packed = jnp.concatenate([key_rot.astype(jnp.bfloat16), value_low], axis=1)
    pieces = [packed]
    seg_pieces = [segment]
    for distance in range(1, reach + 1):
        far_pack, far_seg = shifted((packed, segment), "seq", distance)
        pieces.insert(0, far_pack)
        seg_pieces.insert(0, far_seg)
    keys_all = jnp.concatenate(pieces, axis=0)
    seg_all = jnp.concatenate(seg_pieces, axis=0)
    key_part = keys_all[:, :head_size]
    value_part = keys_all[:, head_size:]
    place = lax.axis_index("seq")
    query_index = place * tok_rows + jnp.arange(tok_rows, dtype=jnp.int32)
    key_index = (place - reach) * tok_rows + jnp.arange((reach + 1) * tok_rows, dtype=jnp.int32)
    spacing = query_index[:, None] - key_index[None, :]
    allowed = (
        (segment[:, None] == seg_all[None, :])
        & (spacing >= 0)
        & (spacing < WINDOW)
        & (key_index[None, :] >= 0)
    )
    scores = product("qhd,kd->hqk", query_low, key_part)
    masked = jnp.where(allowed[None], scores, -1e30)
    top = jnp.max(masked, axis=-1, keepdims=True)
    expd = jnp.exp(masked - top)
    total = jnp.sum(expd, axis=-1, keepdims=True)
    probs_low = (expd / total).astype(jnp.bfloat16)
    log_total = top + jnp.log(total)
    mixed_heads = (
        product("hqk,kd->qhd", probs_low, value_part)
        .reshape(tok_rows, head_count * head_size)
        .astype(jnp.bfloat16)
    )
    attn_out = jnp.dot(mixed_heads, out_full, preferred_element_type=jnp.float32)

    def middle(resid, branch, gain_a, gain_b):
        after = resid + norm_rows(branch, gain_a)
        return (after, norm_rows(after, gain_b))

    (after, normed_ff), middle_back = jax.vjp(middle, hidden_in, attn_out, gain_pa, gain_pf)
    ff_low = normed_ff.astype(jnp.bfloat16)
    gate = jnp.dot(ff_low, gate_full, preferred_element_type=jnp.float32)
    up_value = jnp.dot(ff_low, up_full, preferred_element_type=jnp.float32)

    def mixer(gate_in, up_in):
        return jax.nn.gelu(gate_in, approximate=True) * up_in

    inner, mixer_back = jax.vjp(mixer, gate, up_value)
    inner_low = inner.astype(jnp.bfloat16)
    down = jnp.dot(inner_low, down_full, preferred_element_type=jnp.float32)

    def finish(resid, branch, gain):
        return resid + norm_rows(branch, gain)

    result, finish_back = jax.vjp(finish, after, down, gain_pff)
    grad_result = cotangent[0].astype(jnp.float32)
    grad_after, grad_down, grad_gpff = finish_back(grad_result)
    down_grad_low = grad_down.astype(jnp.bfloat16)
    grad_w_down = product("tf,td->fd", inner_low, down_grad_low)
    grad_inner = product("td,fd->tf", down_grad_low, down_full)
    grad_gate, grad_upv = mixer_back(grad_inner)
    gate_grad_low = grad_gate.astype(jnp.bfloat16)
    up_grad_low = grad_upv.astype(jnp.bfloat16)
    grad_w_gate = product("td,tf->df", ff_low, gate_grad_low)
    grad_w_up = product("td,tf->df", ff_low, up_grad_low)
    grad_normed_ff = product("tf,df->td", gate_grad_low, gate_full) + product(
        "tf,df->td", up_grad_low, up_full
    )
    grad_resid, grad_branch, grad_gpa, grad_gpf = middle_back((grad_after, grad_normed_ff))
    branch_grad_low = grad_branch.astype(jnp.bfloat16)
    grad_w_out = product("ta,td->ad", mixed_heads, branch_grad_low)
    grad_heads = (
        product("td,ad->ta", branch_grad_low, out_full)
        .astype(jnp.bfloat16)
        .reshape(tok_rows, head_count, head_size)
    )
    scores_again = product("qhd,kd->hqk", query_low, key_part)
    probs = jnp.exp(jnp.where(allowed[None], scores_again, -1e30) - log_total)
    probs_again = probs.astype(jnp.bfloat16)
    grad_probs = product("qhd,kd->hqk", grad_heads, value_part)
    grad_scores = (
        probs * (grad_probs - jnp.sum(probs * grad_probs, axis=-1, keepdims=True))
    ).astype(jnp.bfloat16)
    grad_query_rot = product("hqk,kd->qhd", grad_scores, key_part)
    grad_keys = product("hqk,qhd->kd", grad_scores, query_low)
    grad_values = product("hqk,qhd->kd", probs_again, grad_heads)
    grad_packed = jnp.concatenate([grad_keys, grad_values], axis=1)
    collected = grad_packed[reach * tok_rows :]
    for distance in range(1, reach + 1):
        begin = (reach - distance) * tok_rows
        collected = collected + shifted(
            grad_packed[begin : begin + tok_rows].astype(jnp.bfloat16), "seq", -distance
        ).astype(jnp.float32)
    grad_key_rot = collected[:, :head_size]
    value_grad_low = collected[:, head_size:].astype(jnp.bfloat16)
    grad_q_raw, grad_k_raw, grad_gq, grad_gk = turn_back((grad_query_rot, grad_key_rot))
    query_grad_low = grad_q_raw.astype(jnp.bfloat16)
    key_grad_low = grad_k_raw.astype(jnp.bfloat16)
    grad_w_query = product("td,te->de", normed_low, query_grad_low)
    grad_w_key = product("td,te->de", normed_low, key_grad_low)
    grad_w_value = product("td,te->de", normed_low, value_grad_low)
    grad_normed = (
        product("te,de->td", query_grad_low, query_full)
        + product("te,de->td", key_grad_low, key_full)
        + product("te,de->td", value_grad_low, value_full)
    )
    grad_in, grad_gin = first_back(grad_normed)
    input_grad = (grad_resid + grad_in)[None]
    grad_gains = jnp.concatenate([grad_gin, grad_gq, grad_gk, grad_gpa, grad_gpf, grad_gpff])
    own = tuple(
        lax.psum_scatter(g.reshape(-1), ("seq", "fsdp"), scatter_dimension=0, tiled=True)
        for g in (
            grad_w_query,
            grad_w_key,
            grad_w_value,
            grad_w_out,
            grad_w_gate,
            grad_w_up,
            grad_w_down,
            grad_gains,
        )
    )
    return (result.astype(jnp.bfloat16)[None], input_grad) + own


XY = 4
LINE = 4


def mm(a, b):
    return lax.dot_general(a, b, (((1,), (0,)), ((), ())), preferred_element_type=F32)


def mm_nt(a, b):
    return lax.dot_general(a, b, (((1,), (1,)), ((), ())), preferred_element_type=F32)


def mm_tn(a, b):
    return lax.dot_general(a, b, (((0,), (0,)), ((), ())), preferred_element_type=F32)


def inverse_rms(x):
    return lax.rsqrt(jnp.mean(x * x, axis=-1, keepdims=True) + EPS)


def norm_back(hat, inv, gain, grad):
    scaled = grad * gain
    return inv * (scaled - hat * jnp.mean(hat * scaled, axis=-1, keepdims=True))


def turn_fwd(x, cosine, sine):
    half = x.shape[1] // 2
    a, b = x[:, :half], x[:, half:]
    return jnp.concatenate([a * cosine - b * sine, b * cosine + a * sine], axis=1)


def turn_bwd(x, cosine, sine):
    half = x.shape[1] // 2
    a, b = x[:, :half], x[:, half:]
    return jnp.concatenate([a * cosine + b * sine, b * cosine - a * sine], axis=1)


def all_gains(core, mine, theirs):
    a = mine[...].astype(F32)
    b = theirs[...].astype(F32)[: a.shape[0]]
    low, high = jnp.where(core == 0, a, b), jnp.where(core == 0, b, a)
    rows = [half[r : r + 1, :] for half in (low, high) for r in range(a.shape[0])]
    return jnp.concatenate(rows, axis=1)


def row_order(table, width, place, core):
    owner = table[:, :1] ^ (place * 2 + core)
    source = owner * (width // (2 * XY * LINE)) + table[:, 1:2]
    ranks = lax.broadcasted_iota(jnp.int32, (table.shape[0], width), 1)
    return jnp.where(ranks == source, 1.0, 0.0).astype(BF16)


class Traffic:
    def __init__(self, sems):
        self.sems = sems
        self.used = 0
        self.pending = []

    def start(self, source, target):
        copy = pltpu.make_async_copy(source, target, self.sems.at[self.used])
        self.used += 1
        copy.start()
        return copy

    def fetch(self, pairs):
        return [self.start(source, target) for source, target in pairs]

    def halves(self, core, mine, pack, pieces, full):
        rows = mine.shape[0]
        begin = pl.multiple_of(core * rows, 16)
        copies = [self.start(mine, full.at[pl.ds(begin, rows)])]
        for row, number, pack_row, column, cols in pieces:
            begin = pl.multiple_of((1 - core) * rows + row, 16)
            source = pack.at[pack_row : pack_row + number, column : column + cols]
            copies.append(self.start(source, full.at[pl.ds(begin, number)]))
        return copies

    def emit(self, source, target):
        self.pending.append(self.start(source, target))

    def finish(self):
        for copy in self.pending:
            copy.wait()


def pack_layout(rows, widths, talls):
    layout, column = [], 0
    for width in widths:
        layout.append([(0, rows, 0, column, width)])
        column += width
    at = 0
    for height, width in talls:
        pieces, done = [], 0
        while done < height:
            take = min(height - done, rows - at % rows)
            pieces.append((done, take, at % rows, column + at // rows * talls[0][1], width))
            done, at = done + take, at + take
        layout.append(pieces)
    return layout, column + -(-at // rows) * talls[0][1]


def prepare_kernel(layout, *refs):
    count = len(layout)
    tok_h, seg_h, *weights_h = refs[: count + 2]
    ext_h, pack_h = refs[count + 2 : count + 4]
    tok, seg, *weights = refs[count + 4 : 2 * count + 6]
    ext, gain_s, sems = refs[2 * count + 6 :]
    traffic = Traffic(sems)
    first = traffic.fetch([(tok_h, tok), (seg_h, seg)])
    rest = traffic.fetch(list(zip(weights_h, weights)))
    wait(first)
    rows, width = tok.shape
    ext[:rows, :] = tok[...]
    ext[rows:, :] = jnp.zeros((SEG_ROWS, width), BF16)
    ids = seg[...].astype(F32)
    ext[rows:, :rows] = jnp.broadcast_to(ids, (SEG_ROWS, rows)).astype(BF16)
    traffic.emit(ext, ext_h)
    for copy, source, pieces in zip(rest, weights, layout):
        copy.wait()
        if source is weights[-1]:
            missing = gain_s.shape[0] - source.shape[0]
            filled = [source[...].astype(F32), jnp.zeros((missing, LANES), F32)]
            gain_s[...] = jnp.concatenate(filled, axis=0).astype(BF16)
            source = gain_s
        for row, number, pack_row, column, cols in pieces:
            traffic.emit(
                source.at[row : row + number, :],
                pack_h.at[pack_row : pack_row + number, column : column + cols],
            )
    traffic.finish()


def wait(copies):
    for copy in copies:
        copy.wait()


def attention(reach, place, halo, gains, cos_ref, sin_ref, wq, wk, wv, outs, ready):
    n1_out, qraw_out, q_out, kraw_out, k_out, v_out, p_out, ao_out = outs
    width = n1_out.shape[1]
    rows = halo[0].shape[0] - SEG_ROWS
    size = k_out.shape[1]
    heads = q_out.shape[1] // size
    scale = size ** (-0.5)
    ready("halo")
    gains = gains()
    g_in = gains[:, :width]
    g_q = gains[:, width : width + size]
    g_k = gains[:, width + size : width + 2 * size]
    for block in range(reach + 1):
        x = halo[block][:rows, :].astype(F32)
        n1_out[block * rows : (block + 1) * rows, :] = (x * inverse_rms(x) * g_in).astype(BF16)
    ready("kv")
    n1 = n1_out[...]
    kraw = mm(n1, wk[...])
    kraw_out[...] = kraw
    k = turn_fwd(kraw * inverse_rms(kraw) * g_k, cos_ref[...], sin_ref[...]).astype(BF16)
    k_out[...] = k
    v = mm(n1, wv[...]).astype(BF16)
    v_out[...] = v
    keys = (reach + 1) * rows
    seg_rows = [halo[b][rows:, :rows].astype(F32)[:1] for b in range(reach + 1)]
    seg_keys = jnp.concatenate(seg_rows, axis=1)
    square = lax.broadcasted_iota(jnp.int32, (rows, rows), 0) == lax.broadcasted_iota(
        jnp.int32, (rows, rows), 1
    )
    seg_own = jnp.sum(jnp.where(square, seg_rows[reach], 0.0), axis=1, keepdims=True)
    at_query = reach * rows + lax.broadcasted_iota(jnp.int32, (rows, keys), 0)
    at_key = lax.broadcasted_iota(jnp.int32, (rows, keys), 1)
    gap = at_query - at_key
    allowed = (
        (seg_keys == seg_own)
        & (gap >= 0)
        & (gap < WINDOW)
        & (at_key >= (reach - place) * rows)
    )
    cos_own, sin_own = cos_ref[reach * rows :, :], sin_ref[reach * rows :, :]
    ready("query")
    for h in range(heads):
        cols = slice(h * size, (h + 1) * size)
        qraw = mm(n1_out[reach * rows :, :], wq[:, cols])
        qraw_out[:, cols] = qraw
        q = turn_fwd(qraw * inverse_rms(qraw) * g_q, cos_own, sin_own) * scale
        q = q.astype(BF16)
        q_out[:, cols] = q
        s = jnp.where(allowed, mm_nt(q, k), -1e30)
        e = jnp.exp(s - jnp.max(s, axis=-1, keepdims=True))
        p = e * (1.0 / jnp.sum(e, axis=-1, keepdims=True))
        p_out[h] = p
        ao_out[:, cols] = mm(p.astype(BF16), v).astype(BF16)


def pick_halves(core, unit):
    row = lax.broadcasted_iota(jnp.int32, (2 * LANES, 2 * LANES), 0)
    col = lax.broadcasted_iota(jnp.int32, (2 * LANES, 2 * LANES), 1)
    side = jnp.where(col < LANES, core, 1 - core)
    at = col & (LANES - 1)
    want = (lax.div(at, unit) * 2 + side) * unit + lax.rem(at, unit)
    return jnp.where(row == want, 1.0, 0.0).astype(BF16)


def store_halves(keep, send, base, source, unit, core):
    pick = pick_halves(core, unit)
    for b in range(source.shape[1] // (2 * LANES)):
        block = mm(source[:, 2 * b * LANES : 2 * (b + 1) * LANES], pick).astype(BF16)
        keep[:, base + b * LANES : base + (b + 1) * LANES] = block[:, :LANES]
        send[:, base + b * LANES : base + (b + 1) * LANES] = block[:, LANES:]


def pair_columns(width, ff, attn):
    sizes = (ff, ff, width, width, ff // 2, attn // 2, padded(width // 2))
    starts = [sum(sizes[:n]) for n in range(len(sizes) + 1)]
    return starts[:-1], starts[-1]


def padded(columns):
    return -(-columns // LANES) * LANES


def forward_kernel(reach, layout, *refs):
    halo_h, refs = refs[: reach + 1], refs[reach + 1 :]
    ct_h, gains_h, order_h, cos_h, sin_h = refs[:5]
    wq_a, wk_a, wv_a, wg_a, wu_a, wo_a, wd_a, pack_h = refs[5:13]
    outs_h, refs = refs[13:28], refs[28:]
    halo, refs = refs[: reach + 1], refs[reach + 1 :]
    ct, gain_a, order, cos_ref, sin_ref = refs[:5]
    outs, refs = refs[5:20], refs[20:]
    wq, wk, wv, wo, wg, wu, wd, act_s, slope_s, hid_s, ao_ref, gain_b, sems = refs
    place, core = lax.axis_index("seq"), lax.axis_index("fsdp")
    traffic = Traffic(sems)
    waits = {}
    _, _, pack_row, column, cols = layout[7][0]
    gain_far = pack_h.at[pack_row : pack_row + 16, column : column + cols]
    waits["halo"] = traffic.fetch(list(zip(halo_h, halo)))
    waits["halo"] += traffic.fetch([(gains_h, gain_a), (gain_far, gain_b)])
    waits["kv"] = traffic.halves(core, wk_a, pack_h, layout[1], wk)
    waits["kv"] += traffic.halves(core, wv_a, pack_h, layout[2], wv)
    waits["kv"] += traffic.fetch([(cos_h, cos_ref), (sin_h, sin_ref)])
    waits["query"] = traffic.halves(core, wq_a, pack_h, layout[0], wq)
    waits["out"] = traffic.halves(core, wo_a, pack_h, layout[5], wo)
    waits["gate"] = traffic.halves(core, wg_a, pack_h, layout[3], wg)
    waits["gate"] += traffic.halves(core, wu_a, pack_h, layout[4], wu)
    waits["down"] = traffic.halves(core, wd_a, pack_h, layout[6], wd)
    waits["rest"] = traffic.fetch([(ct_h, ct), (order_h, order)])

    def ready(name):
        wait(waits[name])

    attention(
        reach,
        place,
        halo,
        lambda: all_gains(core, gain_a, gain_b),
        cos_ref,
        sin_ref,
        wq,
        wk,
        wv,
        (*outs[:7], ao_ref),
        ready,
    )
    for source, target in zip(outs[:7], outs_h[:7]):
        traffic.emit(source, target)
    mixed_out, dx_out, dao_out, dg_out, keep, send, gains_out, _ = outs[7:]
    for block in range(reach):
        traffic.emit(halo[block], outs_h[14].at[block])
    rows, width = ct.shape
    gains = all_gains(core, gain_a, gain_b)
    gains_out[...] = gains
    size2 = gains.shape[1] - 4 * width
    ff = wg.shape[1]
    base = width + size2
    g_pa = gains[:, base : base + width]
    g_pf = gains[:, base + width : base + 2 * width]
    g_pff = gains[:, base + 2 * width :]
    x = halo[reach][:rows, :].astype(F32)
    ready("out")
    ya = mm(ao_ref[...], wo[...])
    inv_a = inverse_rms(ya)
    hat_a = ya * inv_a
    x2 = x + hat_a * g_pa
    inv_f = inverse_rms(x2)
    hat_f = x2 * inv_f
    n2 = (hat_f * g_pf).astype(BF16)
    ready("gate")
    ready("down")
    ready("rest")
    c = ct[...].astype(F32)
    part = 1024
    (at_gate, at_up, at_df, at_dya, at_hid, at_ao, at_n2), end = pair_columns(
        width, ff, ao_ref.shape[1]
    )
    keep_h, send_h = outs_h[11:13]

    def sent(begin, stop):
        both = ((send, send_h), (keep, keep_h)) if begin >= at_hid else ((send, send_h),)
        for ref, target in both:
            traffic.emit(ref.at[:, begin:stop], target.at[:, begin:stop])

    n2_owned = mm_nt(n2, row_order(order, width, place, core)).astype(BF16)
    half = n2_owned.shape[1] // 2
    keep[:, at_n2:end] = n2_owned[:, :half]
    send[:, at_n2:end] = n2_owned[:, half:]
    store_halves(keep, send, at_ao, ao_ref, ao_ref.shape[1] // 32, core)
    sent(at_ao, end)
    root = math.sqrt(2.0 / math.pi)
    f = jnp.zeros((rows, width), F32)
    for at in range(0, ff, part):
        cols = slice(at, at + part)
        gate = mm(n2, wg[:, cols])
        up = mm(n2, wu[:, cols])
        t = jnp.tanh(root * (gate + 0.044715 * (gate * gate * gate)))
        act = 0.5 * gate * (1.0 + t)
        slope = 0.5 * (1.0 + t) + 0.5 * gate * (1.0 - t * t) * (
            root * (1.0 + 3.0 * 0.044715 * (gate * gate))
        )
        act_s[:, cols] = act
        slope_s[:, cols] = up * slope
        hid = (act * up).astype(BF16)
        hid_s[:, cols] = hid
        f = f + mm(hid, wd[cols, :])
    store_halves(keep, send, at_hid, hid_s, ff // 32, core)
    sent(at_hid, at_ao)
    inv_d = inverse_rms(f)
    hat_d = f * inv_d
    mixed_out[...] = (x2 + hat_d * g_pff).astype(BF16)
    traffic.emit(mixed_out, outs_h[7])
    df = norm_back(hat_d, inv_d, g_pff, c).astype(BF16)
    send[:, at_df : at_df + width] = df
    sent(at_df, at_df + width)
    dn2 = jnp.zeros((rows, width), F32)
    for at in range(0, ff, part):
        cols = slice(at, at + part)
        dhid = mm_nt(df, wd[cols, :])
        dgate = (dhid * slope_s[:, cols]).astype(BF16)
        dup = (dhid * act_s[:, cols]).astype(BF16)
        send[:, at_gate + at : at_gate + at + part] = dgate
        send[:, at_up + at : at_up + at + part] = dup
        sent(at_gate + at, at_gate + at + part)
        sent(at_up + at, at_up + at + part)
        dn2 = dn2 + mm_nt(dgate, wg[:, cols]) + mm_nt(dup, wu[:, cols])
    dx2 = c + norm_back(hat_f, inv_f, g_pf, dn2)
    dya = norm_back(hat_a, inv_a, g_pa, dx2).astype(BF16)
    send[:, at_dya : at_dya + width] = dya
    sent(at_dya, at_dya + width)
    dao_out[...] = mm_nt(dya, wo[...]).astype(BF16)
    traffic.emit(dao_out, outs_h[9])
    dx_out[...] = dx2
    traffic.emit(dx_out, outs_h[8])
    dg_out[:, :width] = jnp.sum(dx2 * hat_a, axis=0, keepdims=True)
    dg_out[:, width : 2 * width] = jnp.sum(dn2 * hat_f, axis=0, keepdims=True)
    dg_out[:, 2 * width :] = jnp.sum(c * hat_d, axis=0, keepdims=True)
    traffic.emit(dg_out, outs_h[10])
    traffic.emit(gains_out, outs_h[13])
    traffic.finish()


def put(xk, xs, first, plane, at, value):
    x_bit, y_bit = plane & 1, plane >> 1
    lead, other = (x_bit, y_bit) if first == "x" else (y_bit, x_bit)
    ref = xs if lead else xk
    ref[other, at : at + value.shape[0], :] = value


def grads_kernel(width, ff, attn, *refs):
    keep_h, send_h, recv_h = refs[:3]
    outs_h, outs = refs[4:10], refs[10:16]
    gk, gs, uk, us, dk, ds = outs
    both, prod_s, sems = refs[16:]
    traffic = Traffic(sems)
    place = lax.axis_index("seq")
    (at_gate, at_up, at_df, at_dya, at_hid, at_ao, at_n2), end = pair_columns(width, ff, attn)

    def sent(ref):
        traffic.emit(ref, outs_h[[r is ref for r in outs].index(True)])

    def fetch(begin, stop):
        own_h = keep_h if begin >= at_hid else send_h
        return traffic.fetch(
            (source.at[:, begin:stop], both.at[side * LANES : (side + 1) * LANES, begin:stop])
            for side, source in enumerate((own_h, recv_h))
        )

    gate_w = fetch(at_n2, end) + fetch(at_gate, at_up)
    up_w = fetch(at_up, at_df)
    rest_w = fetch(at_df, at_hid) + fetch(at_hid, at_n2)
    per = width // 2 // XY
    for copies, base, (keep, send), first in (
        (gate_w, at_gate, (gk, gs), "x"),
        (up_w, at_up, (uk, us), "y"),
    ):
        wait(copies)
        for col in range(0, ff, 512):
            right = both[:, base + col : base + col + 512]
            out = mm_tn(both[:, at_n2:end], right).astype(BF16)
            for plane in range(XY):
                for b in range(4):
                    put(
                        keep,
                        send,
                        first,
                        plane,
                        (col // LANES + b) * per,
                        out[plane * per : (plane + 1) * per, b * LANES : (b + 1) * LANES],
                    )
        sent(send)
        sent(keep)
    wait(rest_w)
    row = 0
    for at_left, at_right, count in ((at_hid, at_df, ff // 2), (at_ao, at_dya, attn // 2)):
        left, right = both[:, at_left : at_left + count], both[:, at_right : at_right + width]
        prod_s[:count, :] = mm_tn(left, right)
        unit = count // (XY * LINE)
        for plane in range(XY):
            for line in range(LINE):
                whose = (place ^ (line * XY + plane)) * unit
                block = prod_s[pl.ds(pl.multiple_of(whose, unit), unit), :].astype(BF16)
                ref = ds if line & 1 else dk
                chunk = (plane >> 1) * 4 + (plane & 1) * 2 + (line >> 1)
                for b in range(width // LANES):
                    ref[chunk, row + b * unit : row + (b + 1) * unit, :] = block[
                        :, b * LANES : (b + 1) * LANES
                    ]
        row += width // LANES * unit
    sent(ds)
    sent(dk)
    traffic.finish()


def heads_kernel(*refs):
    count = 5
    ins_h, outs_h, refs = refs[:count], refs[count : count + 3], refs[count + 3 :]
    ins, outs, sems = refs[:count], refs[count : count + 3], refs[-1]
    q_ref, k_ref, v_ref, dao_ref, p_ref = ins
    dq_out, dk_out, done = outs
    traffic = Traffic(sems)
    heads = p_ref.shape[0]
    first = traffic.fetch([(ins_h[n], ins[n]) for n in (3, 2)])
    p_w = [traffic.start(ins_h[4].at[0], p_ref.at[0])]
    second = traffic.fetch([(ins_h[n], ins[n]) for n in (1, 0)])
    p_w += [traffic.start(ins_h[4].at[h], p_ref.at[h]) for h in range(1, heads)]
    keys, size = k_ref.shape
    wait(first)
    v = v_ref[...]
    dk = jnp.zeros((keys, size), F32)
    for h in range(heads):
        cols = slice(h * size, (h + 1) * size)
        dp = mm_nt(dao_ref[:, cols], v)
        p_w[h].wait()
        p = p_ref[h]
        ds = (p * (dp - jnp.sum(p * dp, axis=-1, keepdims=True))).astype(BF16)
        if h == 0:
            wait(second)
            k = k_ref[...]
        dk = dk + mm_tn(ds, q_ref[:, cols])
        dq_out[:, cols] = mm(ds, k)
    dk_out[...] = dk
    done[...] = jnp.zeros_like(done)
    for source, target in zip(outs, outs_h):
        traffic.emit(source, target)
    traffic.finish()


def back_kernel(reach, layout, *refs):
    count = 15
    ins_h, refs = refs[:count], refs[count:]
    _, wq_a, wk_a, wv_a, pack_h = refs[:5]
    outs_h, refs = refs[5:9], refs[9:]
    ins, refs = refs[:count], refs[count:]
    toks, tok, gains, order, scale_order, dg_post, cos_ref, sin_ref, *more = ins
    n1_ref, dao_ref, p_ref, qraw_ref, kraw_ref, dq_ref, dk_ref = more
    halo = [toks.at[n] for n in range(reach)] + [tok]
    outs = keep, send, dn1_own, dn1_far = refs[:4]
    wq, wk, wv, dkv_s, dqr, sems = refs[4:]
    place, core = lax.axis_index("seq"), lax.axis_index("fsdp")
    traffic = Traffic(sems)
    first = traffic.fetch([(ins_h[n], ins[n]) for n in (3, 8)])
    second = traffic.fetch([(ins_h[n], ins[n]) for n in (9, 10)])
    third = traffic.fetch([(ins_h[n], ins[n]) for n in (2, 6, 7, 11, 12, 13, 14)])
    copies = traffic.fetch([(ins_h[n], ins[n]) for n in (4, 5, 0, 1)])
    for n, (mine, full) in enumerate(((wq_a, wq), (wk_a, wk), (wv_a, wv))):
        copies += traffic.halves(core, mine, pack_h, layout[n], full)
    rows = tok.shape[0] - SEG_ROWS
    width = n1_ref.shape[1]
    size = kraw_ref.shape[1]
    wait(first)
    perm = row_order(order, width, place, core)
    n1_t = mm_nt(perm, n1_ref[...]).astype(BF16)
    wait(second)
    heads = p_ref.shape[0]
    dv = jnp.zeros((n1_ref.shape[0], size), F32)
    for h in range(heads):
        dv = dv + mm_tn(p_ref[h].astype(BF16), dao_ref[:, h * size : (h + 1) * size])
    dkv_s[:, size:] = dv.astype(BF16)
    wait(third)
    g_q = gains[:, width : width + size]
    cos_own, sin_own = cos_ref[reach * rows :, :], sin_ref[reach * rows :, :]
    dgq = jnp.zeros((1, size), F32)
    for h in range(heads):
        cols = slice(h * size, (h + 1) * size)
        dq = turn_bwd(dq_ref[:, cols] * size ** (-0.5), cos_own, sin_own)
        qraw = qraw_ref[:, cols]
        inv = inverse_rms(qraw)
        hat = qraw * inv
        dgq = dgq + jnp.sum(dq * hat, axis=0, keepdims=True)
        dqr[:, cols] = norm_back(hat, inv, g_q, dq).astype(BF16)
    g_k = gains[:, width + size : width + 2 * size]
    kraw = kraw_ref[...]
    inv = inverse_rms(kraw)
    hat = kraw * inv
    dk = turn_bwd(dk_ref[...], cos_ref[...], sin_ref[...])
    dgk = jnp.sum(dk * hat, axis=0, keepdims=True)
    dkv_s[:, :size] = norm_back(hat, inv, g_k, dk).astype(BF16)
    half = width // 2
    per = half // XY
    attn = dqr.shape[1]
    wait(copies)
    dgi = jnp.zeros((1, width), F32)
    for block in range(reach + 1):
        span = slice(block * rows, (block + 1) * rows)
        dn1 = mm_nt(dkv_s[span, :size], wk[...]) + mm_nt(dkv_s[span, size:], wv[...])
        if block == reach:
            dn1 = dn1 + mm_nt(dqr[...], wq[...])
        x = halo[block][:rows, :].astype(F32)
        dgi = dgi + jnp.sum(dn1 * (x * inverse_rms(x)), axis=0, keepdims=True)
        if block == reach:
            dn1_own[...] = dn1
        else:
            bits = (place ^ (place - (reach - block))) & (XY - 1)
            low = dn1.astype(BF16)
            for b in range(width // LANES):
                dn1_far[bits, b * rows : (b + 1) * rows, :] = low[:, b * LANES : (b + 1) * LANES]
    scales = owners_rows(jnp.concatenate([dgi, dgq, dgk, dg_post[...]], axis=1))
    owner = scale_order[:, :1] ^ (place * 2 + core)
    mine = scale_order[:, 1:2] * 1024 + (owner & 3) * 8 + (owner >> 2)
    columns = lax.broadcasted_iota(jnp.int32, (mine.shape[0], 2 * XY * LINE), 1)
    scales = mm(jnp.where(columns == mine, 1.0, 0.0).astype(BF16), scales).astype(BF16)
    rows_each = scales.shape[0] // (2 * XY)
    for ref, begin, group in ((send, half, XY), (keep, 0, 0)):
        left = n1_t[begin : begin + half]
        own = left[:, reach * rows :]
        at = 0
        for value, left_part, total in (
            (dqr, own, attn),
            (dkv_s, left, 2 * size),
        ):
            for col in range(0, total, 512):
                out = mm(left_part, value[:, col : col + 512]).astype(BF16)
                for plane in range(XY):
                    for b in range(4):
                        ref[
                            plane,
                            at + (col // LANES + b) * per : at + (col // LANES + b + 1) * per,
                            :,
                        ] = out[plane * per : (plane + 1) * per, b * LANES : (b + 1) * LANES]
            at += total // LANES * per
        for plane in range(XY):
            row = (group + plane) * rows_each
            ref[plane, at : at + rows_each, :] = scales[row : row + rows_each]
        traffic.emit(ref, outs_h[0 if ref is keep else 1])
    for n in (3, 2):
        traffic.emit(outs[n], outs_h[n])
    traffic.finish()


def owners_rows(line):
    pieces = [line[:, r * LANES : (r + 1) * LANES] for r in range(line.shape[1] // LANES)]
    first, second, third = (jnp.concatenate(pieces[n::3], axis=0) for n in range(3))
    lane = lax.broadcasted_iota(jnp.int32, first.shape, 1)
    quarter = LANES // 4
    groups = [
        first,
        jnp.where(
            lane < quarter, pltpu.roll(first, quarter, 1), pltpu.roll(second, quarter, 1)
        ),
        jnp.where(
            lane < 2 * quarter,
            pltpu.roll(second, 2 * quarter, 1),
            pltpu.roll(third, 2 * quarter, 1),
        ),
        pltpu.roll(third, 3 * quarter, 1),
    ]
    return jnp.concatenate(groups, axis=0).astype(BF16)


def collect_kernel(skip, *refs):
    own_h, far_h, *near = refs[: XY + 1]
    total_out, below_out, own, far, sems = refs[XY + 3 :]
    traffic = Traffic(sems)
    wait(traffic.fetch([(own_h, own), (far_h.at[0], far)]))
    place = lax.axis_index("seq") & (XY - 1)
    rows = own.shape[0]
    total = own[...]
    below = far[...].astype(F32)
    for bits, ref in enumerate(near, 1):
        part = ref[skip:, :].astype(F32)
        mine = (place ^ bits) > place
        below = below + jnp.where(mine, 0.0, part)
        lanes = [part[b * rows : (b + 1) * rows] for b in range(part.shape[0] // rows)]
        total = total + jnp.where(mine, jnp.concatenate(lanes, axis=1), 0.0)
    total_out[...] = total
    below_out[...] = below.astype(BF16)


def finish_kernel(*refs):
    ins_h, (dn1, above), out_h, ins = refs[:3], refs[3:5], refs[5], refs[6:9]
    out, sems = refs[9:]
    traffic = Traffic(sems)
    wait(traffic.fetch(list(zip(ins_h, ins))))
    tok, gains, dx = ins
    rows, width = dx.shape
    lanes = [above[b * rows : (b + 1) * rows, :] for b in range(width // LANES)]
    total = dn1[...] + jnp.concatenate(lanes, axis=1).astype(F32)
    x = tok[:rows, :].astype(F32)
    inv = inverse_rms(x)
    out[...] = dx[...] + norm_back(x * inv, inv, gains[:, :width], total)
    traffic.emit(out, out_h)
    traffic.finish()


def line_split_kernel(groups, entries, extra, direct, after, *refs):
    count = sum(groups)
    ins, (keep, send, split, *sums) = refs[:count], refs[count + after :]
    at = 0
    for number, total in zip(groups, sums):
        value = ins[at][...].astype(F32)
        for other in ins[at + 1 : at + number]:
            value = value + other[: value.shape[0], :].astype(F32)
        total[...] = value
        at += number
    at = 0
    for group, row, blocks, unit in entries:
        for b in range(blocks):
            for position in range(LINE):
                begin = row + (b * LINE + position) * unit
                split[position, at : at + unit, :] = sums[group][begin : begin + unit, :]
            at += unit
    if extra:
        group, row = extra
        for position in range(LINE):
            one = sums[group][row + position : row + position + 1, :]
            split[position, at : at + 16, :] = jnp.broadcast_to(one, (16, LANES))
    order = ((keep, (0,)), (send, (1, 2, 3))) if direct else ((keep, (0, 2)), (send, (1, 3)))
    for ref, positions in order:
        for n, position in enumerate(positions):
            ref[n] = split[position].astype(ref.dtype)


def join_kernel(parts, entries, extra, *refs):
    count = len(entries) + extra
    ins, outs_h, refs = refs[:parts], refs[parts : parts + count], refs[parts + count :]
    flag, outs, (sum_s, sems) = refs[0], refs[1 : count + 1], refs[count + 1 :]
    flag[...] = jnp.zeros_like(flag)
    traffic = Traffic(sems)
    total = ins[0][...].astype(F32)
    for part in ins[1:]:
        total = total + part[...].astype(F32)
    sum_s[...] = total
    at = 0
    for (blocks, unit), out in zip(entries, outs):
        for b in range(blocks):
            out[pl.ds(b, unit, stride=blocks), :] = sum_s[at : at + unit, :]
            at += unit
    if extra:
        outs[-1][...] = sum_s[at : at + 8, :][:1, : outs[-1].shape[1]]
    for out, out_h in zip(outs, outs_h):
        traffic.emit(out, out_h)
    traffic.finish()


def call(kernel, fetched, others, outs, scratch, copies, limit=61):
    hbm = pl.BlockSpec(memory_space=pl.ANY)
    return pl.pallas_call(
        kernel,
        out_shape=outs,
        in_specs=[hbm] * (len(fetched) + len(others)),
        out_specs=[hbm] * len(outs),
        scratch_shapes=[pltpu.VMEM(a.shape, a.dtype) for a in (*fetched, *outs)]
        + scratch
        + [pltpu.SemaphoreType.DMA((copies,))],
        compiler_params=pltpu.CompilerParams(vmem_limit_bytes=limit * MIB),
        cost_estimate=pl.CostEstimate(flops=0, bytes_accessed=0, transcendentals=0),
    )(*fetched, *others)


def shape(dims, dtype):
    return jax.ShapeDtypeStruct(dims, dtype)


vmem = pl.BlockSpec(memory_space=pltpu.VMEM)
hbm = pl.BlockSpec(memory_space=pl.ANY)


def fast(
    tokens,
    segments,
    positions,
    w_query,
    w_key,
    w_value,
    w_out,
    w_gate,
    w_up,
    w_down,
    norm_gains,
    cotangent,
):
    rows, width = tokens.shape[1:]
    size = w_key.shape[1]
    attn = w_query.shape[1]
    heads = attn // size
    ff = w_gate.shape[1]
    count = norm_gains.shape[0] * 2
    reach = (WINDOW - 1 + rows - 1) // rows
    keys = (reach + 1) * rows
    place = lax.axis_index("seq")
    core = lax.axis_index("fsdp")

    def partner(value):
        return lax.ppermute(value, "fsdp", [(0, 1), (1, 0)])

    def across(value, bits):
        return lax.ppermute(value, "seq", [(i, i ^ bits) for i in range(XY * LINE)])

    gains_own = norm_gains.reshape(-1, LANES)
    weights = (w_query, w_key, w_value, w_gate, w_up, w_out, w_down)
    layout, columns = pack_layout(
        width // 2,
        [w.shape[1] for w in weights[:5]],
        [w.shape for w in weights[5:]] + [(16, LANES)],
    )
    tok, pack = pl.pallas_call(
        functools.partial(prepare_kernel, layout),
        out_shape=[
            shape((rows + SEG_ROWS, width), BF16),
            shape((width // 2, columns), BF16),
        ],
        in_specs=[pl.BlockSpec(memory_space=pl.ANY)] * 10,
        out_specs=[pl.BlockSpec(memory_space=pl.ANY)] * 2,
        scratch_shapes=[pltpu.VMEM((rows, width), BF16), pltpu.VMEM((1, rows), jnp.int32)]
        + [pltpu.VMEM(w.shape, BF16) for w in (*weights, gains_own)]
        + [
            pltpu.VMEM((rows + SEG_ROWS, width), BF16),
            pltpu.VMEM((16, LANES), BF16),
            pltpu.SemaphoreType.DMA((40,)),
        ],
        compiler_params=pltpu.CompilerParams(vmem_limit_bytes=61 * MIB),
    )(tokens[0], segments, *weights, gains_own)
    pack_far = partner(pack)
    halo = [shifted(tok, "seq", distance) for distance in range(reach, 0, -1)] + [tok]

    unit = width // (2 * XY * LINE)
    new = np.arange(width) // unit
    core_bit, plane, line = new // (XY * LINE), new // LINE % XY, new % LINE
    owner = (line * XY + plane) * 2 + core_bit
    order = jnp.asarray(np.stack([owner, np.arange(width) % unit], axis=1).astype(np.int32))
    apart = np.full((2, padded(width // 2), 2), [0, 1 << 20])
    apart[:, : width // 2] = np.stack([owner, np.arange(width) % unit], axis=1).reshape(2, -1, 2)
    order_pair = jnp.asarray(apart.reshape(-1, 2).astype(np.int32))
    freq = np.exp(np.arange(size // 2, dtype=np.float64) * (-2.0 * math.log(10000.0) / size))
    turn = np.arange(keys, dtype=np.float64)[:, None] * freq
    cosine = jnp.asarray(np.cos(turn).astype(np.float32))
    sine = jnp.asarray(np.sin(turn).astype(np.float32))

    pair_end = pair_columns(width, ff, attn)[1]
    n1, qraw, q, kraw, k, v, p, mixed, dx, dao, dg_post, mlp_keep, mlp_send, gains, toks = call(
        functools.partial(forward_kernel, reach, layout),
        (*halo, cotangent[0], gains_own, order_pair, cosine, sine),
        (*weights, pack_far),
        [
            shape((keys, width), BF16),
            shape((rows, attn), F32),
            shape((rows, attn), BF16),
            shape((keys, size), F32),
            shape((keys, size), BF16),
            shape((keys, size), BF16),
            shape((heads, rows, keys), F32),
            shape((rows, width), BF16),
            shape((rows, width), F32),
            shape((rows, attn), BF16),
            shape((1, 3 * width), F32),
            shape((rows, pair_end), BF16),
            shape((rows, pair_end), BF16),
            shape((1, count), F32),
            shape((reach, rows + SEG_ROWS, width), BF16),
        ],
        [
            pltpu.VMEM((width, attn), BF16),
            pltpu.VMEM((width, size), BF16),
            pltpu.VMEM((width, size), BF16),
            pltpu.VMEM((attn, width), BF16),
            pltpu.VMEM((width, ff), BF16),
            pltpu.VMEM((width, ff), BF16),
            pltpu.VMEM((ff, width), BF16),
            pltpu.VMEM((rows, ff), F32),
            pltpu.VMEM((rows, ff), F32),
            pltpu.VMEM((rows, ff), BF16),
            pltpu.VMEM((rows, attn), BF16),
            pltpu.VMEM((16, LANES), BF16),
        ],
        128,
    )
    mlp_recv = partner(mlp_send)

    dq, dk, heads_done = call(
        heads_kernel,
        (q, k, v, dao, p),
        (),
        [shape((rows, attn), F32), shape((keys, size), F32), shape((8, LANES), F32)],
        [],
        16,
        63,
    )

    per_ff = width // 2 // XY * ff // LANES
    per_down = ff // 2 // XY * width // LANES
    per_out = attn // 2 // XY * width // LANES
    gk, gs, uk, us, tk, ts = call(
        functools.partial(grads_kernel, width, ff, attn),
        (),
        (mlp_keep, mlp_send, mlp_recv, heads_done),
        [shape((2, per_ff, LANES), BF16)] * 4
        + [shape((8, (per_down + per_out) // LINE, LANES), BF16)] * 2,
        [
            pltpu.VMEM((2 * rows, pair_end), BF16),
            pltpu.VMEM((ff // 2, width), F32),
        ],
        16,
    )

    per_q = width // 2 // XY * attn // LANES
    per_k = width // 2 // XY * size // LANES
    per_back = per_q + 2 * per_k
    share = count // (2 * XY * LINE)
    new = np.arange(2 * XY * 16)
    core_bit, plane, line = new // (XY * 16), new // 16 % XY, new % 16
    owner = (line % LINE * XY + plane) * 2 + core_bit
    scale_order = jnp.asarray(np.stack([owner, line // LINE], axis=1).astype(np.int32))
    back_keep, back_send, dn1_own, dn1_far = call(
        functools.partial(back_kernel, reach, layout),
        (
            toks,
            tok,
            gains,
            order,
            scale_order,
            dg_post,
            cosine,
            sine,
            n1,
            dao,
            p,
            qraw,
            kraw,
            dq,
            dk,
        ),
        (gk, *weights[:3], pack_far),
        [
            shape((XY, per_back + 16, LANES), BF16),
            shape((XY, per_back + 16, LANES), BF16),
            shape((rows, width), F32),
            shape((XY, rows * width // LANES, LANES), BF16),
        ],
        [
            pltpu.VMEM((width, attn), BF16),
            pltpu.VMEM((width, size), BF16),
            pltpu.VMEM((width, size), BF16),
            pltpu.VMEM((keys, 2 * size), BF16),
            pltpu.VMEM((rows, attn), BF16),
        ],
        64,
    )
    back_recv = partner(back_send)

    def add(a, b):
        return (a.astype(F32) + b.astype(F32)).astype(BF16)

    def halves(keep, near):
        half = keep.shape[0] // 2
        return add(keep[:half], near[:half]), add(keep[half:], near[half:])

    def step(keep, send, bits):
        return halves(keep, across(send, bits))

    def line_split(groups, entries, extra, direct, after=()):
        part = sum(blocks * unit for _, _, blocks, unit in entries) + (16 if extra else 0)
        stay = 1 if direct else 2
        arrays = [array for g in groups for array in g]
        return pl.pallas_call(
            functools.partial(
                line_split_kernel, [len(g) for g in groups], entries, extra, direct, len(after)
            ),
            out_shape=[shape((n, part, LANES), BF16) for n in (stay, LINE - stay)],
            in_specs=[vmem] * (len(arrays) + len(after)),
            out_specs=[vmem] * 2,
            scratch_shapes=[pltpu.VMEM((LINE, part, LANES), F32)]
            + [pltpu.VMEM(g[0].shape, F32) for g in groups],
            compiler_params=pltpu.CompilerParams(vmem_limit_bytes=12 * MIB),
            cost_estimate=pl.CostEstimate(flops=0, bytes_accessed=0, transcendentals=0),
        )(*arrays, *after)

    def join(parts, entries, extra=False):
        outs = [shape((blocks * unit, LANES), F32) for blocks, unit in entries]
        if extra:
            outs.append(shape((1, share), F32))
        *arrays, flag = pl.pallas_call(
            functools.partial(join_kernel, len(parts), entries, int(extra)),
            out_shape=outs + [shape((8, LANES), F32)],
            in_specs=[vmem] * len(parts),
            out_specs=[hbm] * len(outs) + [vmem],
            scratch_shapes=[pltpu.VMEM(a.shape, a.dtype) for a in outs]
            + [pltpu.VMEM(parts[0].shape, F32), pltpu.SemaphoreType.DMA((len(outs),))],
            compiler_params=pltpu.CompilerParams(vmem_limit_bytes=12 * MIB),
            cost_estimate=pl.CostEstimate(flops=0, bytes_accessed=0, transcendentals=0),
        )(*parts)
        return arrays, flag

    wide, narrow = ff // LANES, width // LANES
    unit_out, unit_down = attn // 32, ff // 32

    planes = [add(back_keep[n], back_recv[n]) for n in range(XY)]
    planes = [planes[0]] + [
        across(jnp.concatenate([planes[n], dn1_far[n]]), n) for n in range(1, XY)
    ]

    gate_0, gate_1 = step(gk, gs, 1)
    up_0, up_1 = step(uk, us, 2)
    gate_2, up_2 = across(gate_1, 2), across(up_1, 1)
    flat = lambda value: value.reshape(value.shape[1:])
    keep, send = line_split(
        ((flat(gate_0), flat(gate_2)), (flat(up_0), flat(up_2))),
        ((0, 0, wide, unit), (1, 0, wide, unit)),
        None,
        False,
    )
    mlp_0, mlp_1 = step(keep, send, XY)
    (own_gate, own_up), mlp_done = join(
        (flat(mlp_0), flat(across(mlp_1, 2 * XY))), ((wide, unit), (wide, unit))
    )
    down_0, down_1 = step(tk, ts, XY)
    down_0, down_1 = step(down_0, down_1, 2)
    down_2, down_3 = step(down_0, down_1, 1)
    (own_down, own_out), down_done = join(
        (flat(down_2), flat(across(down_3, 2 * XY))), ((narrow, unit_down), (narrow, unit_out))
    )

    far_shape = (rows * width // LANES, LANES)
    dn1, below = pl.pallas_call(
        functools.partial(collect_kernel, per_back + 16),
        out_shape=[shape((rows, width), F32), shape(far_shape, BF16)],
        in_specs=[hbm] * 2 + [vmem] * (XY + 1),
        out_specs=[vmem] * 2,
        scratch_shapes=[
            pltpu.VMEM((rows, width), F32),
            pltpu.VMEM(far_shape, BF16),
            pltpu.SemaphoreType.DMA((2,)),
        ],
        compiler_params=pltpu.CompilerParams(vmem_limit_bytes=12 * MIB),
        cost_estimate=pl.CostEstimate(flops=0, bytes_accessed=0, transcendentals=0),
    )(dn1_own, dn1_far, *planes[1:], mlp_done, down_done)
    keep, send = line_split(
        (planes,),
        (
            (0, 0, attn // LANES, unit),
            (0, per_q, size // LANES, unit),
            (0, per_q + per_k, size // LANES, unit),
        ),
        (0, per_back),
        True,
        (below,),
    )
    (own_query, own_key, own_value, own_gains), _ = join(
        (flat(keep), *[across(send[n], (n + 1) * XY) for n in range(LINE - 1)]),
        ((attn // LANES, unit), (size // LANES, unit), (size // LANES, unit)),
        True,
    )

    input_grad = pl.pallas_call(
        finish_kernel,
        out_shape=shape((rows, width), F32),
        in_specs=[hbm] * 3 + [vmem] * 2,
        out_specs=hbm,
        scratch_shapes=[pltpu.VMEM(a.shape, a.dtype) for a in (tok, gains, dx, dx)]
        + [pltpu.SemaphoreType.DMA((4,))],
        compiler_params=pltpu.CompilerParams(vmem_limit_bytes=12 * MIB),
        cost_estimate=pl.CostEstimate(flops=0, bytes_accessed=0, transcendentals=0),
    )(tok, gains, dx, dn1, shifted(below, "seq", -XY))
    return (
        mixed[None],
        input_grad[None],
        own_query.reshape(-1),
        own_key.reshape(-1),
        own_value.reshape(-1),
        own_out.reshape(-1),
        own_gate.reshape(-1),
        own_up.reshape(-1),
        own_down.reshape(-1),
        own_gains.reshape(-1),
    )


def solution(mesh):
    placed = (
        P("fsdp", "seq", None),
        P("fsdp", "seq"),
        P("fsdp", "seq"),
        P("fsdp", None),
        P("fsdp", None),
        P("fsdp", None),
        P("fsdp", None),
        P("fsdp", None),
        P("fsdp", None),
        P("fsdp", None),
        P("fsdp"),
        P("fsdp", "seq", None),
    )
    small = mesh.shape["seq"] == XY * LINE and mesh.shape["fsdp"] == 2
    return jax.shard_map(
        fast if small else general,
        mesh=mesh,
        in_specs=placed,
        out_specs=(
            P("fsdp", "seq", None),
            P("fsdp", "seq", None),
            P(("seq", "fsdp")),
            P(("seq", "fsdp")),
            P(("seq", "fsdp")),
            P(("seq", "fsdp")),
            P(("seq", "fsdp")),
            P(("seq", "fsdp")),
            P(("seq", "fsdp")),
            P(("seq", "fsdp")),
        ),
        check_vma=False,
    )
```
